32 devices in a mesh: section: 4 (over y, x), dp: 8 (over z, core).
Axes of the slice: x: 2, y: 2, z: 4, core: 2. Of those that a mesh axis runs over, the one named last changes fastest.
Arguments:
- boundary: bfloat16 [4, 8192, 768], P('section', 'dp'), may hold values from -6 to 6
- bucket_ids: int32 [2, 16, 4], P(None, 'dp'), may hold values from 0 to 3, as said below
- w_in: bfloat16 [2, 768, 3072], P(None, 'dp'), may hold values from -0.21875 to 0.21875
- b_in: float32 [2, 3072], replicated, may hold values from -3 to 3
- w_out: bfloat16 [2, 3072, 768], P(None, 'dp'), may hold values from -0.109375 to 0.109375
- b_out: float32 [2, 768], replicated, may hold values from -3 to 3
- gain_one: float32 [2, 768], replicated, may hold values from 0.5 to 1.5
- shift_one: float32 [2, 768], replicated, may hold values from -3 to 3
- gain_two: float32 [2, 768], replicated, may hold values from 0.5 to 1.5
- shift_two: float32 [2, 768], replicated, may hold values from -3 to 3
Outputs:
- result: float32 [4, 8192, 768], P('section', 'dp')
- grad_w_in: float32 [2, 768, 3072], P(None, 'dp')
- grad_b_in: float32 [2, 3072], P(None, 'dp')
- grad_w_out: float32 [2, 3072, 768], P(None, 'dp')
- grad_b_out: float32 [2, 768], P(None, 'dp')
- grad_gain_one: float32 [2, 768], P(None, 'dp')
- grad_shift_one: float32 [2, 768], P(None, 'dp')
- grad_gain_two: float32 [2, 768], P(None, 'dp')
- grad_shift_two: float32 [2, 768], P(None, 'dp')
The draws below stay inside these ranges and needn't reach their ends.
Inputs may be any that keep to these rules, and one draw needn't show every extreme that they name: `bucket_ids`: each row lists the buckets of the sequences packed into one block of 512 tokens in order; bucket k holds sequences of 128 * 2**k tokens, 3 marks an empty slot; the used slots come first and their lengths add up to 512 exactly.
All inputs are finite; a program needn't handle non-finite values.
Results may differ from the reference program's by a relative error of at most 0.014.
Values may be sent and summed in bfloat16 or wider, within the bound.
No kernel may reach another device: no remote copies, remote signals or barrier semaphores. Data moves between devices by JAX's collectives and lax.ppermute only.
A program may use at most 256 MiB of HBM per device.

```python
import math
import jax
import jax.numpy as jnp
from jax import lax

D = 768
FF = 3072
BASE = 128
MICRO = 2
LAYERS = 2
SLAB = 512
COPIES = 2
ROWS = 8192
N_SECTION = 4
N_DP = 8


def draw_bucket_ids(key, part):
    key = jax.random.fold_in(key, 3)
    patterns = jnp.array([[2, 3, 3, 3], [1, 1, 3, 3], [1, 0, 0, 3], [0, 1, 0, 3], [0, 0, 1, 3], [0, 0, 0, 0]], jnp.int32)
    chosen = jax.random.randint(key, (COPIES, N_DP * MICRO), 0, 6)
    return patterns[chosen]


def steps_of(own_key, dims, pieces, least, top_value):
    level = 1.0
    for dim, blocks in pieces:
        draws = jax.random.uniform(jax.random.fold_in(jax.random.fold_in(own_key, 6), dim), (blocks,), jnp.float32, least / len(pieces), top_value / len(pieces))
        level = level * jnp.repeat(jnp.exp(draws), dims[dim] // blocks).reshape((-1,) + (1,) * (len(dims) - 1 - dim))
    return level


def gaussian(key, dims, width, most, split=(), held_as=jnp.bfloat16):
    values = jax.random.normal(key, dims, jnp.float32) * width
    if len(split) > 0:
        values = steps_of(key, dims, split, -0.22, 0.18) * values
    return jnp.clip(values, min=-most, max=most).astype(held_as)


def setup_inputs(seed: int = 0) -> dict:
    seeds = jax.random.split(jax.random.key(seed), 11)
    boundary = gaussian(seeds[0], (N_SECTION, ROWS, D), 1.0, 6.0, ((0, 4), (1, 8)))
    bucket_ids = draw_bucket_ids(jax.random.fold_in(seeds[10], 71), 0)
    w_in = gaussian(seeds[2], (LAYERS, D, FF), D ** -0.5, 0.21875, ((1, 8),))
    b_in = gaussian(seeds[3], (LAYERS, FF), 0.5, 3.0, (), jnp.float32)
    w_out = gaussian(seeds[4], (LAYERS, FF, D), FF ** -0.5, 0.109375, ((1, 8),))
    b_out = gaussian(seeds[5], (LAYERS, D), 0.5, 3.0, (), jnp.float32)
    gain_one = jnp.clip(1.0 + 0.1 * jax.random.normal(seeds[6], (LAYERS, D), jnp.float32), 0.5, 1.5)
    shift_one = gaussian(seeds[7], (LAYERS, D), 0.5, 3.0, (), jnp.float32)
    gain_two = jnp.clip(1.0 + 0.1 * jax.random.normal(seeds[8], (LAYERS, D), jnp.float32), 0.5, 1.5)
    shift_two = gaussian(seeds[9], (LAYERS, D), 0.5, 3.0, (), jnp.float32)
    return {"boundary": boundary, "bucket_ids": bucket_ids, "w_in": w_in, "b_in": b_in, "w_out": w_out, "b_out": b_out, "gain_one": gain_one, "shift_one": shift_one, "gain_two": gain_two, "shift_two": shift_two}


@jax.custom_vjp
def low(v):
    return lax.optimization_barrier(v.astype(jnp.bfloat16)).astype(jnp.float32)

@jax.custom_vjp
def low_back(v):
    return v

def low_keep(v):
    return (low(v), None)

def low_pass(kept, grad):
    return (grad,)

def back_keep(v):
    return (v, None)

def back_low(kept, grad):
    return (low(grad),)
low.defvjp(low_keep, low_pass)
low_back.defvjp(back_keep, back_low)

def matmul_f32(left, right):
    return jnp.dot(left, right, precision=lax.Precision.HIGHEST, preferred_element_type=jnp.float32)

def layer_norm(values, gain, shift):
    center = lax.optimization_barrier(jnp.mean(values, axis=-1, keepdims=True))
    offsets = values - center
    spread = lax.optimization_barrier(jnp.mean(offsets * offsets, axis=-1, keepdims=True))
    return offsets * lax.rsqrt(spread + 1e-05) * gain + shift

def hidden_tables(feat_width):
    positions = jnp.arange(feat_width, dtype=jnp.int32)
    phase_mod = positions[:, None] * positions[None, :] % feat_width
    angles = phase_mod.astype(jnp.float32) * (2.0 * math.pi) / feat_width
    scaling = 1.0 / math.sqrt(feat_width)
    return (jnp.cos(angles) * scaling, jnp.sin(angles) * scaling)

def block_tables(bucket_row, slab_len, base_len):
    lengths = base_len * (bucket_row == 0).astype(jnp.int32) + 2 * base_len * (bucket_row == 1).astype(jnp.int32) + 4 * base_len * (bucket_row == 2).astype(jnp.int32)
    ends_at = jnp.cumsum(lengths).astype(jnp.int32)
    starts_at = ends_at - lengths
    positions = jnp.arange(slab_len, dtype=jnp.int32)
    segment = lax.optimization_barrier(jnp.sum((positions[:, None] >= ends_at[None, :]).astype(jnp.int32), axis=1))
    one_hot = (segment[:, None] == jnp.arange(bucket_row.shape[0], dtype=jnp.int32)[None, :]).astype(jnp.int32)
    row_start = lax.optimization_barrier(jnp.sum(one_hot * starts_at[None, :], axis=1))
    row_length = lax.optimization_barrier(jnp.sum(one_hot * lengths[None, :], axis=1))
    local_pos = positions - row_start
    same_seq = segment[:, None] == segment[None, :]
    phase_mod = local_pos[:, None] * local_pos[None, :] % row_length[:, None]
    angles = phase_mod.astype(jnp.float32) * (2.0 * math.pi) / row_length[:, None].astype(jnp.float32)
    scaling = lax.rsqrt(row_length.astype(jnp.float32))[:, None]
    cos_table = jnp.where(same_seq, jnp.cos(angles) * scaling, 0.0)
    sin_table = jnp.where(same_seq, jnp.sin(angles) * scaling, 0.0)
    return (cos_table, sin_table)

def fnet_layer(layer_rows, hid_cos, hid_sin, seq_cos, seq_sin, weights):
    w_first, b_first, w_second, b_second, gain_first, shift_first, gain_second, shift_second = weights
    real_part = low_back(low(matmul_f32(layer_rows, hid_cos)))
    imag_part = low_back(low(matmul_f32(layer_rows, hid_sin)))
    mixed = low_back(matmul_f32(seq_cos, real_part) - matmul_f32(seq_sin, imag_part))
    normed = layer_norm(layer_rows + mixed, gain_first, shift_first)
    pre_act = low_back(matmul_f32(low(normed), w_first) + b_first)
    hidden = low(jax.nn.gelu(pre_act, approximate=True))
    branch = low_back(matmul_f32(hidden, w_second) + b_second)
    return layer_norm(normed + branch, gain_second, shift_second)

def reference(boundary, bucket_ids, w_in, b_in, w_out, b_out, gain_one, shift_one, gain_two, shift_two):
    feat_width = boundary.shape[2]
    rows_in = boundary[0::2].astype(jnp.float32).reshape(-1, SLAB, feat_width)
    cot_rows = boundary[1::2].astype(jnp.float32).reshape(-1, SLAB, feat_width)
    bucket_rows = bucket_ids.reshape(-1, bucket_ids.shape[2])
    params = tuple((param_array.astype(jnp.float32) for param_array in (w_in, b_in, w_out, b_out, gain_one, shift_one, gain_two, shift_two)))
    hid_cos, hid_sin = hidden_tables(feat_width)
    hid_cos, hid_sin = (low(hid_cos), low(hid_sin))

    def block_step(grad_sums, block_data):
        block_rows, block_cot, bucket_row = block_data
        seq_cos, seq_sin = block_tables(bucket_row, SLAB, BASE)
        seq_cos, seq_sin = (low(seq_cos), low(seq_sin))

        def two_layers(layer_rows, layer_params):
            first_out = fnet_layer(layer_rows, hid_cos, hid_sin, seq_cos, seq_sin, tuple((param_array[0] for param_array in layer_params)))
            mid_rows = low_back(low(first_out))
            return fnet_layer(mid_rows, hid_cos, hid_sin, seq_cos, seq_sin, tuple((param_array[1] for param_array in layer_params)))
        out_rows, back_fn = jax.vjp(two_layers, block_rows, params)
        row_grad, param_grads = back_fn(block_cot)
        return (jax.tree.map(jnp.add, grad_sums, param_grads), (out_rows, row_grad))
    init_sums = tuple((jnp.zeros(param_array.shape, jnp.float32) for param_array in params))
    grad_sums, (out_all, grad_all) = lax.scan(block_step, init_sums, (rows_in, cot_rows, bucket_rows))
    stacked = jnp.stack([grad_all.reshape(COPIES, -1, feat_width), out_all.reshape(COPIES, -1, feat_width)], axis=1)
    result = stacked.reshape(N_SECTION, -1, feat_width)
    return (result, grad_sums[0], grad_sums[1], grad_sums[2], grad_sums[3], grad_sums[4], grad_sums[5], grad_sums[6], grad_sums[7])
```

```python
from functools import partial
import math

import jax
import jax.numpy as jnp
import numpy as np
from jax import lax
from jax.experimental import pallas as pl
from jax.experimental.pallas import tpu as pltpu
from jax.sharding import PartitionSpec as P

AXES = ("section", "dp")
F32 = jnp.float32
BF16 = jnp.bfloat16


class Place:
    def __init__(self):
        self.n_section = lax.axis_size("section")
        self.n_dp = lax.axis_size("dp")
        self.chips = self.n_dp // 2
        self.section = lax.axis_index("section")
        self.dp = lax.axis_index("dp")
        self.chip = self.dp // 2
        self.core = self.dp % 2

    def permute(self, value, target):
        pairs = []
        for section in range(self.n_section):
            for chip in range(self.chips):
                for core in range(2):
                    place = target(section, chip, core)
                    if place is not None:
                        to_section, to_chip, to_core = place
                        pairs.append(
                            (
                                section * self.n_dp + chip * 2 + core,
                                to_section * self.n_dp + to_chip * 2 + to_core,
                            )
                        )
        return lax.ppermute(value, AXES, pairs)

    def swap_core(self, value):
        return self.permute(value, lambda s, z, c: (s, z, 1 - c))

    def plane_one(self, value):
        return self.permute(value, lambda s, z, c: (s ^ (1 + c), z, c))

    def plane_two(self, value):
        return self.permute(value, lambda s, z, c: (s ^ (2 - c), z, c))

    def shift_chip(self, value, apart):
        return self.permute(value, lambda s, z, c: (s, (z + apart) % self.chips, c))


def dft_tables(length):
    positions = np.arange(length)
    angles = (positions[:, None] * positions[None, :] % length) * (2.0 * math.pi) / length
    scaling = 1.0 / math.sqrt(length)
    return (np.cos(angles) * scaling, np.sin(angles) * scaling)


def sequence_tiles(base_len):
    cos_tiles, sin_tiles = [], []
    for parts in (1, 2, 4):
        cos_table, sin_table = dft_tables(parts * base_len)
        for i in range(parts):
            for j in range(parts):
                window = (
                    slice(i * base_len, (i + 1) * base_len),
                    slice(j * base_len, (j + 1) * base_len),
                )
                cos_tiles.append(cos_table[window])
                sin_tiles.append(sin_table[window])
    cos_tiles.append(np.zeros((base_len, base_len)))
    sin_tiles.append(np.zeros((base_len, base_len)))
    return np.stack(cos_tiles).astype(BF16), np.stack(sin_tiles).astype(BF16)


def tile_numbers(bucket_row, slots):
    parts = jnp.where(bucket_row < 3, 1 << jnp.minimum(bucket_row, 2), 0)
    ends = jnp.cumsum(parts)
    where = jnp.arange(slots, dtype=jnp.int32)
    segment = jnp.sum((where[:, None] >= ends[None, :]).astype(jnp.int32), axis=1)
    one_hot = (segment[:, None] == jnp.arange(slots)[None, :]).astype(jnp.int32)
    start = jnp.sum(one_hot * (ends - parts)[None, :], axis=1)
    size = jnp.sum(one_hot * parts[None, :], axis=1)
    first = jnp.where(size == 1, 0, jnp.where(size == 2, 1, 5))
    place = where - start
    numbers = first[:, None] + place[:, None] * size[:, None] + place[None, :]
    return jnp.where(segment[:, None] == segment[None, :], numbers, 21)


class Spot:
    def __init__(self):
        self.section = lax.axis_index("section")
        dp = lax.axis_index("dp")
        self.chip, self.core = dp // 2, dp % 2


def plane_bits(core):
    return 1 + core, 2 - core


def rows_at(start, size):
    return pl.ds(pl.multiple_of(start, size), size)


class Loader:
    def __init__(self, layer, sources, scratch, sems, by_rows):
        self.sems = sems
        self.started = 0
        chunks, width = scratch.shape[0], scratch.shape[2]
        self.chunks = []
        if len(sources) == 1:
            for chunk in range(chunks):
                part = pl.ds(chunk * width, width)
                source = sources[0].at[part, :] if by_rows else sources[0].at[:, part]
                self.chunks.append((chunk, [self.start(source, scratch.at[chunk])]))
            return
        spot = Spot()
        chips = lax.axis_size("dp") // 2
        piece = sources[1].shape[1]
        if by_rows:
            for apart in range(chips):
                chip = (spot.chip + chips - apart) % chips
                copies = []
                for other in range(2):
                    own, near, far = sources[3 * other : 3 * other + 3]
                    core = (spot.core + other) % 2
                    bit_one, bit_two = plane_bits(core)
                    target = scratch.at[chip]
                    if apart == 0:
                        shard = rows_at(core * 4 * piece, 4 * piece)
                        copies.append(self.start(own.at[layer], target.at[shard, :]))
                        continue
                    for source, quarter in (
                        (near.at[apart - 1], spot.section),
                        (near.at[chips + apart - 2], spot.section ^ bit_one),
                        (far.at[apart - 1], spot.section ^ bit_two),
                        (far.at[chips + apart - 2], spot.section ^ 3),
                    ):
                        rows = rows_at((core * 4 + quarter) * piece, piece)
                        copies.append(self.start(source, target.at[rows, :]))
                self.chunks.append((chip, copies))
            return
        first, rest = [], []
        for other in range(2):
            own, near, far = sources[3 * other : 3 * other + 3]
            core = (spot.core + other) % 2
            bit_one, bit_two = plane_bits(core)
            for apart in range(chips):
                chip = (spot.chip + chips - apart) % chips
                rows = rows_at((2 * chip + core) * piece, piece)
                for turn, flip in enumerate((0, bit_one, bit_two, 3)):
                    quarter = spot.section ^ flip
                    if apart == 0:
                        columns = rows_at(quarter * width, width)
                        source = own.at[layer, :, columns]
                    else:
                        source = (near, far)[turn // 2].at[(turn % 2) * (chips - 1) + apart - 1]
                    copy = self.start(source, scratch.at[quarter, rows, :])
                    (rest if turn else first).append(copy)
        self.chunks.append((spot.section, first))
        self.chunks.append((spot.section ^ 1, rest))
        self.chunks.append((spot.section ^ 2, []))
        self.chunks.append((spot.section ^ 3, []))

    def start(self, source, target):
        copy = pltpu.make_async_copy(source, target, self.sems.at[self.started])
        copy.start()
        self.started += 1
        return copy

    def __iter__(self):
        for chunk, copies in self.chunks:
            for copy in copies:
                copy.wait()
            yield chunk


class Storer:
    def __init__(self, outs, tiles, sems, by_rows):
        self.outs, self.tiles, self.sems, self.by_rows = outs, tiles, sems, by_rows
        self.copies = []

    def start(self, source, target):
        copy = pltpu.make_async_copy(source, target, self.sems.at[len(self.copies)])
        copy.start()
        self.copies.append(copy)

    def store(self, chunk):
        tile = self.tiles.at[chunk]
        width = tile.shape[0]
        if len(self.outs) == 1:
            part = pl.ds(chunk * width, width)
            out = self.outs[0]
            self.start(tile, out.at[part, :] if self.by_rows else out.at[:, part])
            return
        spot = Spot()
        chips = lax.axis_size("dp") // 2
        piece = self.outs[0].shape[2]
        for other in range(2):
            out = self.outs[other]
            core = (spot.core + other) % 2
            bit_one, _ = plane_bits(core)

            def slot_of(quarter):
                flip = quarter ^ spot.section
                side = jnp.where(flip == bit_one, 0, 2)
                return jnp.where(flip == 3, 1, jnp.where(flip == 0, 3, side))

            for part in range(4 if self.by_rows else chips):
                if self.by_rows:
                    chip, quarter = chunk, part
                    rows = rows_at((core * 4 + quarter) * piece, piece)
                else:
                    chip, quarter = part, chunk
                    rows = rows_at((2 * chip + core) * piece, piece)
                apart = (chip + chips - spot.chip) % chips
                self.start(tile.at[rows, :], out.at[slot_of(quarter), apart])

    def finish(self):
        for copy in self.copies:
            copy.wait()


def gather_weight(place, shard, by_rows):
    if by_rows:
        piece_rows = shard.shape[0] // 4
        piece = lax.dynamic_slice_in_dim(shard, place.section * piece_rows, piece_rows, 0)
    else:
        width = shard.shape[1] // 4
        piece = lax.dynamic_slice_in_dim(shard, place.section * width, width, 1)
    along = jnp.stack([place.shift_chip(piece, apart) for apart in range(1, place.chips)])
    near = jnp.concatenate([along, place.plane_one(along)])
    far = place.plane_two(near)
    return near, far, place.swap_core(near), place.swap_core(far)


def scatter_grad(place, own, other):
    from_core = place.swap_core(other)
    wide = lambda value: value.astype(F32)
    first = (wide(own[0:2]) + wide(from_core[0:2])).astype(BF16)
    from_one = place.plane_one(first)
    second = (wide(own[2]) + wide(from_core[2]) + wide(from_one[1])).astype(BF16)
    from_two = place.plane_two(second)
    mine = wide(own[3]) + wide(from_core[3]) + wide(from_one[0]) + wide(from_two)
    total = mine[0]
    for apart in range(1, place.chips):
        total = total + wide(place.shift_chip(mine[apart].astype(BF16), apart))
    return total.astype(BF16)


def share_sections(place, piece, row_pieces):
    from_one = place.plane_one(piece)
    from_two = place.plane_two(jnp.stack([piece, from_one]))
    core_zero = place.core == 0
    quarters = [
        piece,
        jnp.where(core_zero, from_one, from_two[0]),
        jnp.where(core_zero, from_two[0], from_one),
        from_two[1],
    ]
    low_bit = place.section % 2 == 1
    high_bit = place.section // 2 == 1
    quarters = [jnp.where(low_bit, quarters[i ^ 1], quarters[i]) for i in range(4)]
    quarters = [jnp.where(high_bit, quarters[i ^ 2], quarters[i]) for i in range(4)]
    return jnp.concatenate(quarters, axis=0 if row_pieces else 1).astype(F32)


def sum_small(place, packed):
    total = packed + place.swap_core(packed)
    total = total + place.permute(total, lambda s, z, c: (s ^ 1, z, c))
    total = total + place.permute(total, lambda s, z, c: (s ^ 2, z, c))
    total = total + place.permute(total, lambda s, z, c: (s, z ^ 1, c))
    total = total + place.permute(total, lambda s, z, c: (s, z ^ 2, c))
    return lax.dynamic_index_in_dim(total, place.dp, 0, keepdims=False)


ROW_STEP = 256


def dot(left, right, dims=((1,), (0,))):
    return lax.dot_general(left, right, (dims, ((), ())), preferred_element_type=F32)


def norm(values):
    center = jnp.mean(values, axis=-1, keepdims=True)
    offsets = values - center
    inverse = lax.rsqrt(jnp.mean(offsets * offsets, axis=-1, keepdims=True) + 1e-05)
    return offsets * inverse, inverse


def norm_back(upstream, unit, inverse, gain):
    scaled = upstream * gain
    center = jnp.mean(scaled, axis=-1, keepdims=True)
    along = jnp.mean(scaled * unit, axis=-1, keepdims=True)
    return inverse * (scaled - center - unit * along)


def gelu_both(v):
    scale = math.sqrt(2.0 / math.pi)
    square = v * v
    half = 0.5 + 0.5 * jnp.tanh(v * (scale + (scale * 0.044715) * square))
    spread = (2.0 * half) * (1.0 - half)
    return v * half, half + (v * spread) * (scale + (3.0 * scale * 0.044715) * square)


def row_steps(count):
    step = min(ROW_STEP, count)

    def run(function):
        def one(i, carry):
            function(rows_at(i * step, step))
            return carry

        lax.fori_loop(0, count // step, one, 0)

    return run


def column_sum(values):
    return jnp.sum(values, axis=0, keepdims=True)


def mix_forward(rows, hid_cos, hid_sin, seq_cos, seq_sin, gain, shift, real, imag, outs):
    unit, inverse, normed_low, normed_turned = outs

    @row_steps(rows.shape[0])
    def _(at):
        real[at, :] = dot(rows[at, :], hid_cos[...]).astype(BF16)
        imag[at, :] = dot(rows[at, :], hid_sin[...]).astype(BF16)

    @row_steps(rows.shape[0])
    def _(at):
        mixed = dot(seq_cos[at, :], real[...]) - dot(seq_sin[at, :], imag[...])
        unit_rows, inverse_rows = norm(rows[at, :].astype(F32) + mixed)
        unit[at, :] = unit_rows
        inverse[at, :] = inverse_rows
        normed = (unit_rows * gain[...] + shift[...]).astype(BF16)
        normed_low[at, :] = normed
        normed_turned[:, at] = normed.T


def first_mix_kernel(numbers, rows, hid_cos, hid_sin, cos_tiles, sin_tiles, gain, shift, *refs):
    seq_cos, seq_sin = refs[0:2]
    outs, (real, imag) = refs[2:6], refs[6:]
    base = cos_tiles.shape[1]
    slots = seq_cos.shape[0] // base
    for i in range(slots):
        for j in range(slots):
            window = (pl.ds(i * base, base), pl.ds(j * base, base))
            number = numbers[i * slots + j]
            seq_cos[window] = cos_tiles[number]
            seq_sin[window] = sin_tiles[number]
    mix_forward(rows, hid_cos, hid_sin, seq_cos, seq_sin, gain, shift, real, imag, outs)


def expand_kernel(layer, n_sources, normed_low, b_in, *refs):
    sources, (hidden, hidden_turned, slope, scratch, sems) = refs[:n_sources], refs[n_sources:]
    width = scratch.shape[2]
    for chunk in Loader(layer, sources, scratch, sems, False):
        at_chunk = rows_at(chunk * width, width)

        @row_steps(normed_low.shape[0])
        def _(at):
            value, rate = gelu_both(dot(normed_low[at, :], scratch[chunk]) + b_in[:, at_chunk])
            value = value.astype(BF16)
            hidden[at, at_chunk] = value
            slope[at, at_chunk] = rate.astype(BF16)
            hidden_turned[at_chunk, at] = value.T


def contract(layer, sources, scratch, sems, hidden, total):
    width = scratch.shape[2]
    for turn, chunk in enumerate(Loader(layer, sources, scratch, sems, True)):
        at_chunk = rows_at(chunk * width, width)

        @row_steps(hidden.shape[0])
        def _(at):
            part = dot(hidden[at, at_chunk], scratch[chunk])
            total[at, :] = part if turn == 0 else total[at, :] + part


def middle_kernel(layer, n_sources, *refs):
    hidden, unit_one, gain_one, shift_one, b_out, gain_two, shift_two = refs[:7]
    hid_cos, hid_sin, seq_cos, seq_sin, next_gain, next_shift = refs[7:13]
    sources, refs = refs[13 : 13 + n_sources], refs[13 + n_sources :]
    unit_two, inverse_two = refs[:2]
    outs, (scratch, total, mid, real, imag, sems) = refs[2:6], refs[6:]
    contract(layer, sources, scratch, sems, hidden, total)

    @row_steps(hidden.shape[0])
    def _(at):
        normed = unit_one[at, :] * gain_one[...] + shift_one[...]
        unit, inverse = norm(normed + (total[at, :] + b_out[...]))
        unit_two[at, :] = unit
        inverse_two[at, :] = inverse
        mid[at, :] = (unit * gain_two[...] + shift_two[...]).astype(BF16)

    mix_forward(mid, hid_cos, hid_sin, seq_cos, seq_sin, next_gain, next_shift, real, imag, outs)


def out_grad(hidden_turned, branch_grad, tiles, storer):
    width = tiles.shape[2]
    for chunk in range(tiles.shape[0]):

        @row_steps(width)
        def _(at):
            rows = pl.ds(pl.multiple_of(chunk * width + at.start, at.size), at.size)
            tiles[chunk, at, :] = dot(hidden_turned[rows, :], branch_grad[...]).astype(BF16)

        storer.store(chunk)


def turn_kernel(layer, n_sources, n_outs, *refs):
    hidden, hidden_turned, unit_one, gain_one, shift_one, b_out, gain_two, shift_two = refs[:8]
    cotangent = refs[8]
    sources, refs = refs[9 : 9 + n_sources], refs[9 + n_sources :]
    grads, refs = refs[:n_outs], refs[n_outs:]
    out_rows, d_second, branch_grad, small = refs[:4]
    scratch, total, tiles, load_sems, store_sems = refs[4:]
    contract(layer, sources, scratch, load_sems, hidden, total)
    small[...] = jnp.zeros_like(small)

    @row_steps(hidden.shape[0])
    def _(at):
        normed = unit_one[at, :] * gain_one[...] + shift_one[...]
        unit, inverse = norm(normed + (total[at, :] + b_out[...]))
        out_rows[at, :] = unit * gain_two[...] + shift_two[...]
        second_back(at, cotangent[at, :].astype(F32), unit, inverse, gain_two, d_second, branch_grad, small)

    storer = Storer(grads, tiles, store_sems, True)
    out_grad(hidden_turned, branch_grad, tiles, storer)
    storer.finish()


def second_back(at, upstream, unit, inverse, gain, d_second, branch_grad, small):
    grad = norm_back(upstream, unit, inverse, gain[...])
    low = grad.astype(BF16)
    d_second[at, :] = grad
    branch_grad[at, :] = low
    small[0:1, :] += column_sum(low.astype(F32))
    small[1:2, :] += column_sum(upstream * unit)
    small[2:3, :] += column_sum(upstream)


def shrink_kernel(layer, n_sources, n_outs, branch_grad, slope, normed_turned, *refs):
    sources, refs = refs[:n_sources], refs[n_sources:]
    grads, refs = refs[:n_outs], refs[n_outs:]
    act_grad, b_grad = refs[:2]
    scratch, tiles, load_sems, store_sems = refs[2:]
    width = scratch.shape[2]
    b_grad[...] = jnp.zeros_like(b_grad)
    for chunk in Loader(layer, sources, scratch, load_sems, True):
        at_chunk = rows_at(chunk * width, width)

        @row_steps(branch_grad.shape[0])
        def _(at):
            grad = dot(branch_grad[at, :], scratch[chunk], ((1,), (1,)))
            low = (grad * slope[at, at_chunk].astype(F32)).astype(BF16)
            act_grad[at, at_chunk] = low
            b_grad[:, at_chunk] += column_sum(low.astype(F32))

    storer = Storer(grads, tiles, store_sems, False)
    for chunk in range(tiles.shape[0]):
        at_chunk = pl.ds(chunk * width, width)

        @row_steps(width)
        def _(at):
            tiles[chunk, at, :] = dot(normed_turned[at, :], act_grad[:, at_chunk]).astype(BF16)

        storer.store(chunk)
    storer.finish()


def unmix(layer, sources, scratch, sems, refs, small, input_grad):
    act_grad, d_second, unit_one, inverse_one, gain_one, hid_cos, hid_sin, seq_cos, seq_sin = refs[:9]
    total, mix_grad, real, imag = refs[9:]
    width = scratch.shape[2]
    for turn, chunk in enumerate(Loader(layer, sources, scratch, sems, False)):
        at_chunk = rows_at(chunk * width, width)

        @row_steps(act_grad.shape[0])
        def _(at):
            part = dot(act_grad[at, at_chunk], scratch[chunk], ((1,), (1,)))
            total[at, :] = (d_second if turn == 0 else total)[at, :] + part

    small[...] = jnp.zeros_like(small)

    @row_steps(act_grad.shape[0])
    def _(at):
        upstream, unit = total[at, :], unit_one[at, :]
        grad = norm_back(upstream, unit, inverse_one[at, :], gain_one[...])
        total[at, :] = grad
        mix_grad[at, :] = grad.astype(BF16)
        small[0:1, :] += column_sum(upstream * unit)
        small[1:2, :] += column_sum(upstream)

    @row_steps(act_grad.shape[0])
    def _(at):
        real[at, :] = dot(seq_cos[at, :], mix_grad[...]).astype(BF16)
        imag[at, :] = (-dot(seq_sin[at, :], mix_grad[...])).astype(BF16)

    @row_steps(act_grad.shape[0])
    def _(at):
        grad = dot(real[at, :], hid_cos[...]) + dot(imag[at, :], hid_sin[...])
        input_grad[at, :] = total[at, :] + grad


def last_kernel(layer, n_sources, *refs):
    sources, ins, (input_grad, small, scratch, total, mix_grad, real, imag, sems) = (
        refs[9 : 9 + n_sources],
        refs[:9],
        refs[9 + n_sources :],
    )
    unmix(layer, sources, scratch, sems, ins + (total, mix_grad, real, imag), small, input_grad)


def relay_kernel(layer, n_sources, n_outs, *refs):
    ins = refs[:9]
    hidden_turned, unit_two, inverse_two, gain_two = refs[9:13]
    sources, refs = refs[13 : 13 + n_sources], refs[13 + n_sources :]
    grads, refs = refs[:n_outs], refs[n_outs:]
    small, d_second, branch_grad, small_two = refs[:4]
    scratch, total, mix_grad, real, imag, tiles, load_sems, store_sems = refs[4:]
    unmix(layer, sources, scratch, load_sems, ins + (total, mix_grad, real, imag), small, total)
    small_two[...] = jnp.zeros_like(small_two)

    @row_steps(total.shape[0])
    def _(at):
        upstream = total[at, :].astype(BF16).astype(F32)
        second_back(
            at, upstream, unit_two[at, :], inverse_two[at, :], gain_two, d_second, branch_grad, small_two
        )

    storer = Storer(grads, tiles, store_sems, True)
    out_grad(hidden_turned, branch_grad, tiles, storer)
    storer.finish()


VMEM = pl.BlockSpec(memory_space=pltpu.VMEM)
SMEM = pl.BlockSpec(memory_space=pltpu.SMEM)
ANY = pl.BlockSpec(memory_space=pl.ANY)
SEMS = 40


def call(kernel, ins, outs, scratch, flops, name):
    sized = [pltpu.SemaphoreType.DMA((SEMS,)) if s is None else pltpu.VMEM(*s) for s in scratch]
    moved = sum(array.size * array.dtype.itemsize for _, array in ins)
    return pl.pallas_call(
        kernel,
        in_specs=[spec for spec, _ in ins],
        out_specs=tuple(spec for spec, _, _ in outs),
        out_shape=tuple(jax.ShapeDtypeStruct(shape, dtype) for _, shape, dtype in outs),
        scratch_shapes=sized,
        compiler_params=pltpu.CompilerParams(vmem_limit_bytes=48 * 2**20),
        cost_estimate=pl.CostEstimate(flops=flops, bytes_accessed=moved, transcendentals=0),
        name=name,
    )(*(array for _, array in ins))


def body(boundary, bucket_ids, w_in, b_in, w_out, b_out, gain_one, shift_one, gain_two, shift_two):
    place = Place()
    layers = w_in.shape[0]
    is_first = place.section % 2 == 0
    micro_count = bucket_ids.shape[1]
    feat_width = boundary.shape[2]
    slab_len = boundary.shape[1] // micro_count
    slots = bucket_ids.shape[2]
    base_len = slab_len // slots
    by_permutes = place.n_section == 4 and place.chips == 4

    def swap_layer(value):
        return place.permute(value, lambda s, z, c: (s ^ 1, z, c))

    first_slab, second_slab = boundary[0, :slab_len], boundary[0, slab_len:]
    received = swap_layer(jnp.where(is_first, second_slab, first_slab))
    rows = jnp.where(is_first, first_slab, received)
    cotangent = jnp.where(is_first, received, second_slab)
    bucket_row = bucket_ids[place.section // 2, place.section % 2]

    if by_permutes:
        others_in, others_out = place.swap_core(w_in), place.swap_core(w_out)
        sources_in, sources_out = [], []
        for layer in range(layers):
            for w, others, sources, by_rows in (
                (w_in, others_in, sources_in, False),
                (w_out, others_out, sources_out, True),
            ):
                near, far, other_near, other_far = gather_weight(place, w[layer], by_rows)
                sources.append([(ANY, v) for v in (w, near, far, others, other_near, other_far)])
    else:
        sources_in, sources_out = (
            [
                [(ANY, lax.all_gather(w[layer], "dp", axis=0, tiled=True))]
                for layer in range(layers)
            ]
            for w in (w_in, w_out)
        )

    ff_width = w_in.shape[2]
    chunks = ff_width // feat_width
    hid = [(VMEM, jnp.asarray(table.astype(BF16))) for table in dft_tables(feat_width)]
    numbers = tile_numbers(bucket_row, slots).reshape(-1)
    tiles = [(VMEM, jnp.asarray(table)) for table in sequence_tiles(base_len)]
    block = (slab_len, feat_width)
    wide = (slab_len, ff_width)
    square = 2 * slab_len * feat_width * feat_width
    mix_cost = 2 * square + 4 * slab_len * slab_len * feat_width
    ff_cost = 2 * slab_len * feat_width * ff_width
    loaded = ((chunks, feat_width, feat_width), BF16)
    sums_shape = (VMEM, (8, feat_width), F32)

    def vmem(*arrays):
        return [(VMEM, array) for array in arrays]

    def param(array, layer):
        return (VMEM, array[layer][None])

    mix_outs = [
        (VMEM, block, F32),
        (VMEM, (slab_len, 1), F32),
        (VMEM, block, BF16),
        (VMEM, (feat_width, slab_len), BF16),
    ]
    if by_permutes:
        pieces = {
            True: (4, place.chips, w_out.shape[1] // 4, feat_width),
            False: (4, place.chips, w_in.shape[1], feat_width),
        }
        grad_outs = {key: [(ANY, shape, BF16)] * 2 for key, shape in pieces.items()}
    else:
        grad_outs = {
            True: [(ANY, (ff_width, feat_width), BF16)],
            False: [(ANY, (feat_width, ff_width), BF16)],
        }
    n_sources, n_outs = len(sources_in[0]), len(grad_outs[True])

    seq_cos, seq_sin, *mixed = call(
        first_mix_kernel,
        [(SMEM, numbers), (VMEM, rows)] + hid + tiles + [param(gain_one, 0), param(shift_one, 0)],
        [(VMEM, (slab_len, slab_len), BF16)] * 2 + mix_outs,
        [(block, BF16)] * 2,
        mix_cost,
        "first_mix",
    )
    tables = hid + vmem(seq_cos, seq_sin)

    saved = []
    for layer in range(layers):
        unit_one, inverse_one, normed_low, normed_turned = mixed
        hidden, hidden_turned, slope = call(
            partial(expand_kernel, layer, n_sources),
            vmem(normed_low) + [param(b_in, layer)] + sources_in[layer],
            [(VMEM, wide, BF16), (VMEM, (ff_width, slab_len), BF16), (VMEM, wide, BF16)],
            [loaded, None],
            ff_cost,
            "expand",
        )
        common = vmem(unit_one) + [
            param(p, layer) for p in (gain_one, shift_one, b_out, gain_two, shift_two)
        ]
        kept = [unit_one, inverse_one, normed_turned, hidden_turned, slope]
        if layer < layers - 1:
            unit_two, inverse_two, *mixed = call(
                partial(middle_kernel, layer, n_sources),
                vmem(hidden)
                + common
                + tables
                + [param(gain_one, layer + 1), param(shift_one, layer + 1)]
                + sources_out[layer],
                [(VMEM, block, F32), (VMEM, (slab_len, 1), F32)] + mix_outs,
                [loaded, (block, F32), (block, BF16), (block, BF16), (block, BF16), None],
                ff_cost + mix_cost,
                "middle",
            )
            kept += [unit_two, inverse_two]
        saved.append(kept)

    last = layers - 1
    *pieces, out_rows, d_second, branch_grad, sums_two = call(
        partial(turn_kernel, last, n_sources, n_outs),
        vmem(hidden, hidden_turned) + common + vmem(cotangent) + sources_out[last],
        grad_outs[True]
        + [(VMEM, block, F32), (VMEM, block, F32), (VMEM, block, BF16), sums_shape],
        [loaded, (block, F32), loaded, None, None],
        2 * ff_cost,
        "turn",
    )
    grads_out, grads_in, smalls = {last: pieces}, {}, {}
    for layer in reversed(range(layers)):
        unit_one, inverse_one, normed_turned, hidden_turned, slope = saved[layer][:5]
        *pieces, act_grad, b_grad = call(
            partial(shrink_kernel, layer, n_sources, n_outs),
            vmem(branch_grad, slope, normed_turned) + sources_out[layer],
            grad_outs[False] + [(VMEM, wide, BF16), (VMEM, (1, ff_width), F32)],
            [loaded, loaded, None, None],
            2 * ff_cost,
            "shrink",
        )
        grads_in[layer] = pieces
        ins = vmem(act_grad, d_second, unit_one, inverse_one) + [param(gain_one, layer)] + tables
        own_sums = sums_two
        work = [loaded, (block, F32), (block, BF16), (block, BF16), (block, BF16)]
        if layer > 0:
            below_turned, below_unit, below_inverse = [saved[layer - 1][i] for i in (3, 5, 6)]
            *pieces, sums_one, d_second, branch_grad, sums_two = call(
                partial(relay_kernel, layer, n_sources, n_outs),
                ins
                + vmem(below_turned, below_unit, below_inverse)
                + [param(gain_two, layer - 1)]
                + sources_in[layer],
                grad_outs[True]
                + [sums_shape, (VMEM, block, F32), (VMEM, block, BF16), sums_shape],
                work + [loaded, None, None],
                2 * ff_cost + mix_cost,
                "relay",
            )
            grads_out[layer - 1] = pieces
        else:
            input_grad, sums_one = call(
                partial(last_kernel, layer, n_sources),
                ins + sources_in[layer],
                [(VMEM, block, F32), sums_shape],
                work + [None],
                ff_cost + mix_cost,
                "last",
            )
        smalls[layer] = (b_grad[0], own_sums[0], sums_one[0], sums_one[1], own_sums[1], own_sums[2])

    def reduce_grad(pieces, by_rows):
        if by_permutes:
            return share_sections(place, scatter_grad(place, *pieces), by_rows)
        part = lax.psum_scatter(pieces[0], "dp", scatter_dimension=0, tiled=True)
        return lax.psum(part, "section").astype(F32)

    grads = [
        (reduce_grad(grads_in[layer], False), reduce_grad(grads_out[layer], True))
        for layer in range(layers)
    ]

    stacked = [jnp.stack([smalls[layer][i] for layer in range(layers)]) for i in range(6)]
    widths = [value.shape[1] // place.n_dp for value in stacked]
    packed = jnp.concatenate(
        [value.reshape(layers, place.n_dp, -1).transpose(1, 0, 2) for value in stacked], axis=2
    )
    if by_permutes:
        own_small = sum_small(place, packed)
    else:
        own_small = lax.psum(
            lax.psum_scatter(packed, "dp", scatter_dimension=0, tiled=False), "section"
        )
    small_out, start = [], 0
    for width in widths:
        small_out.append(own_small[:, start : start + width])
        start += width

    sent = jnp.where(is_first, out_rows, input_grad).astype(BF16)
    back = swap_layer(sent).astype(F32)
    result = jnp.stack(
        [jnp.where(is_first, input_grad, back), jnp.where(is_first, back, out_rows)]
    ).reshape(1, micro_count * slab_len, feat_width)
    return (
        result,
        jnp.stack([grads[layer][0] for layer in range(layers)]),
        small_out[0],
        jnp.stack([grads[layer][1] for layer in range(layers)]),
        small_out[1],
        small_out[2],
        small_out[3],
        small_out[4],
        small_out[5],
    )


def solution(mesh):
    return jax.shard_map(
        body,
        mesh=mesh,
        in_specs=(
            P("section", "dp", None),
            P(None, "dp", None),
            P(None, "dp", None),
            P(),
            P(None, "dp", None),
            P(),
            P(),
            P(),
            P(),
            P(),
        ),
        out_specs=(
            P("section", "dp", None),
            P(None, "dp", None),
            P(None, "dp"),
            P(None, "dp", None),
            P(None, "dp"),
            P(None, "dp"),
            P(None, "dp"),
            P(None, "dp"),
            P(None, "dp"),
        ),
        check_vma=False,
    )
```

```python
from functools import partial
import math

import jax
import jax.numpy as jnp
import numpy as np
from jax import lax
from jax.experimental import pallas as pl
from jax.experimental.pallas import tpu as pltpu
from jax.sharding import PartitionSpec as P

AXES = ("section", "dp")
F32 = jnp.float32
BF16 = jnp.bfloat16
BLOCKS = 4
ROW_STEP = 256
VMEM_SPARE = 4 * 2**20

VMEM = pl.BlockSpec(memory_space=pltpu.VMEM)
SMEM = pl.BlockSpec(memory_space=pltpu.SMEM)
HBM = pl.BlockSpec(memory_space=pltpu.HBM)
LATE, EARLY = "late", "early"


class Place:
    def __init__(self):
        self.n_section = lax.axis_size("section")
        self.n_dp = lax.axis_size("dp")
        self.chips = self.n_dp // 2
        self.section = lax.axis_index("section")
        self.dp = lax.axis_index("dp")
        self.core = self.dp % 2

    def permute(self, value, target):
        pairs = []
        for section in range(self.n_section):
            for chip in range(self.chips):
                for core in range(2):
                    to_section, to_chip, to_core = target(section, chip, core)
                    source = section * self.n_dp + chip * 2 + core
                    pairs.append((source, to_section * self.n_dp + to_chip * 2 + to_core))
        return lax.ppermute(value, AXES, pairs)

    def swap_core(self, value):
        return self.permute(value, lambda s, z, c: (s, z, 1 - c))

    def swap_layer(self, value):
        return self.permute(value, lambda s, z, c: (s ^ 1, z, c))

    def plane_one(self, value):
        return self.permute(value, lambda s, z, c: (s ^ (1 + c), z, c))

    def plane_two(self, value):
        return self.permute(value, lambda s, z, c: (s ^ (2 - c), z, c))

    def shift_chip(self, value, apart):
        return self.permute(value, lambda s, z, c: (s, (z + apart) % self.chips, c))


class Spot:
    def __init__(self, by_permutes=True):
        dp = lax.axis_index("dp")
        self.core = dp % 2
        if by_permutes:
            self.section, self.chip = lax.axis_index("section"), dp // 2
            self.chips = lax.axis_size("dp") // 2
            self.held = (1 + self.core, 3, 2 - self.core, 0)
        else:
            self.section, self.held = 0, (0, 1, 2, 3)

    def block(self, turn):
        return self.section ^ self.held[turn]

    def turn_of(self, block):
        flip = block ^ self.section
        side = jnp.where(flip == self.held[0], 0, 2)
        return jnp.where(flip == 3, 1, jnp.where(flip == 0, 3, side))


def dft_tables(length):
    positions = np.arange(length)
    angles = (positions[:, None] * positions[None, :] % length) * (2.0 * math.pi) / length
    scaling = 1.0 / math.sqrt(length)
    return (np.cos(angles) * scaling, np.sin(angles) * scaling)


def sequence_tiles(base_len):
    cos_tiles, sin_tiles = [], []
    for parts in (1, 2, 4):
        cos_table, sin_table = dft_tables(parts * base_len)
        for i in range(parts):
            for j in range(parts):
                window = (
                    slice(i * base_len, (i + 1) * base_len),
                    slice(j * base_len, (j + 1) * base_len),
                )
                cos_tiles.append(cos_table[window])
                sin_tiles.append(sin_table[window])
    cos_tiles.append(np.zeros((base_len, base_len)))
    sin_tiles.append(np.zeros((base_len, base_len)))
    return np.stack(cos_tiles).astype(BF16), np.stack(sin_tiles).astype(BF16)


def tile_numbers(bucket_row, slots):
    parts = jnp.where(bucket_row < 3, 1 << jnp.minimum(bucket_row, 2), 0)
    ends = jnp.cumsum(parts)
    where = jnp.arange(slots, dtype=jnp.int32)
    segment = jnp.sum((where[:, None] >= ends[None, :]).astype(jnp.int32), axis=1)
    one_hot = (segment[:, None] == jnp.arange(slots)[None, :]).astype(jnp.int32)
    start = jnp.sum(one_hot * (ends - parts)[None, :], axis=1)
    size = jnp.sum(one_hot * parts[None, :], axis=1)
    first = jnp.where(size == 1, 0, jnp.where(size == 2, 1, 5))
    place = where - start
    numbers = first[:, None] + place[:, None] * size[:, None] + place[None, :]
    return jnp.where(segment[:, None] == segment[None, :], numbers, 21)


def rows_at(start, size):
    return pl.ds(pl.multiple_of(start, size), size)


def dot(left, right, dims=((1,), (0,))):
    return lax.dot_general(left, right, (dims, ((), ())), preferred_element_type=F32)


def row_steps(count, step=ROW_STEP):
    step = step if count % step == 0 else count

    def run(function):
        for i in range(count // step):
            function(pl.ds(i * step, step))

    return run


def column_sum(values):
    return jnp.sum(values, axis=0, keepdims=True)


class Copies:
    def __init__(self, sems):
        self.sems, self.count = sems, 0

    def start(self, source, target):
        copy = pltpu.make_async_copy(source, target, self.sems.at[self.count])
        copy.start()
        self.count += 1
        return copy


class Late:
    def __init__(self, source, buffer, copies, parts):
        self.buffer = buffer
        if parts is None:
            self.waiting = [copies.start(source, buffer)]
        else:
            self.waiting = [copies.start(source.at[part], buffer.at[part]) for part in parts]

    def __call__(self, parts=None):
        for _ in range(len(self.waiting) if parts is None else parts):
            self.waiting.pop(0).wait()
        return self.buffer


class Early:
    def __init__(self, target, buffer, copies):
        self.target, self.buffer, self.copies, self.leaving = target, buffer, copies, []

    def push(self, part=None):
        source, target = self.buffer, self.target
        if part is not None:
            source, target = source.at[part], target.at[part]
        self.leaving.append(self.copies.start(source, target))


def tie(value, *others):
    return lax.optimization_barrier((value,) + others)[0]


def call(kernel, ins, outs, scratch, name, after=()):
    buffers = [pltpu.VMEM(a[1].shape, a[1].dtype) for a in ins if a[0] is LATE]
    buffers += [pltpu.VMEM(*out[1:]) for out in outs if out[0] is EARLY]
    n_ins, n_outs, n_after, n_scratch = len(ins), len(outs), len(after), len(scratch)
    counts = []

    def run(*refs):
        given, made = list(refs[:n_ins]), list(refs[n_ins + n_after :][:n_outs])
        refs = refs[n_ins + n_after + n_outs :]
        own, held, copies = refs[:n_scratch], list(refs[n_scratch:-1]), Copies(refs[-1])
        late = []
        for i, entry in enumerate(ins):
            if entry[0] is LATE:
                given[i] = Late(given[i], held.pop(0), copies, (entry + (None,))[2])
                late.append(given[i])
        early = []
        for i, out in enumerate(outs):
            if out[0] is EARLY:
                made[i] = Early(made[i], held.pop(0), copies)
                early.append(made[i])
        leaving = kernel(*given, *made, *own, copies) or []
        for value in late:
            value()
        for copy in leaving + [copy for out in early for copy in out.leaving]:
            copy.wait()
        counts.append(copies.count)

    def spec_of(spec):
        return HBM if spec in (LATE, EARLY) else spec

    held = list(scratch) + [(a[1].shape, a[1].dtype) for a in ins if a[0] in (LATE, VMEM)]
    held += [out[1:] for out in outs if out[0] in (EARLY, VMEM)]
    needed = sum(math.prod(shape) * jnp.dtype(dtype).itemsize for shape, dtype in held)

    def build(sems):
        return pl.pallas_call(
            run,
            in_specs=[spec_of(entry[0]) for entry in ins] + [HBM] * n_after,
            out_specs=tuple(spec_of(out[0]) for out in outs),
            out_shape=tuple(jax.ShapeDtypeStruct(*out[1:]) for out in outs),
            scratch_shapes=[pltpu.VMEM(*s) for s in scratch]
            + buffers
            + [pltpu.SemaphoreType.DMA((sems,))],
            compiler_params=pltpu.CompilerParams(vmem_limit_bytes=needed + VMEM_SPARE),
            cost_estimate=pl.CostEstimate(flops=10**11, bytes_accessed=1000, transcendentals=0),
            name=name,
        )

    arrays = [entry[1] for entry in ins] + list(after)
    jax.eval_shape(build(96), *arrays)
    return build(max(counts[-1], 1))(*arrays)


def move(name, terms, unit, outs, targets, after=()):
    count, n_terms = len(targets), len(terms)
    given = []
    for array, _ in terms:
        if not any(array is other for other in given):
            given.append(array)
    numbers = [next(i for i, other in enumerate(given) if other is array) for array, _ in terms]

    def run(*refs):
        ins, made = refs[: len(given)], refs[len(given) : len(given) + len(outs)]
        held, low, copies = refs[len(given) + len(outs) :]

        def at(ref, index):
            index = index(Spot()) if callable(index) else index
            return ref.at[index] if index else ref

        arriving = [
            [copies.start(at(ins[n], indices[i]), held.at[t, i]) for t, (n, (_, indices)) in enumerate(zip(numbers, terms))]
            for i in range(count)
        ]
        leaving = []
        for i, (number, index) in enumerate(targets):
            for copy in arriving[i]:
                copy.wait()
            source = held.at[0, i]
            if n_terms > 1:
                total = held[0, i].astype(F32)
                for t in range(1, n_terms):
                    total = total + held[t, i].astype(F32)
                low[i] = total.astype(BF16)
                source = low.at[i]
            leaving.append(copies.start(source, at(made[number], index)))
        return leaving

    return call(
        run,
        [(HBM, array) for array in given],
        [(HBM, shape, BF16) for shape in outs],
        [((n_terms, count) + tuple(unit), BF16), ((count,) + tuple(unit), BF16)],
        name,
        after,
    )


def pack(name, arrays, after=()):
    unit = arrays[0].shape[-2:]
    sizes = [1 if len(array.shape) == 2 else array.shape[0] for array in arrays]
    starts = [sum(sizes[:i]) for i in range(len(sizes))]

    def run(*refs):
        ins, (out, held, copies) = refs[: len(arrays)], refs[len(arrays) :]

        def part(ref, i):
            return ref.at[starts[i]] if len(arrays[i].shape) == 2 else ref.at[pl.ds(starts[i], sizes[i])]

        arriving = [copies.start(ref, part(held, i)) for i, ref in enumerate(ins)]
        leaving = []
        for i, copy in enumerate(arriving):
            copy.wait()
            leaving.append(copies.start(part(held, i), part(out, i)))
        return leaving

    whole = ((sum(sizes),) + unit, arrays[0].dtype)
    (packed,) = call(run, [(HBM, array) for array in arrays], [(HBM,) + whole], [whole], name, after)
    return packed


def choose(copies, first, second, buffer):
    is_first = lax.axis_index("section") % 2 == 0
    sem = copies.sems.at[copies.count]
    copies.count += 1
    pair = [pltpu.make_async_copy(source, buffer, sem) for source in (first, second)]
    pl.when(is_first)(pair[0].start)
    pl.when(jnp.logical_not(is_first))(pair[1].start)
    return pair[0]


def prepare_kernel(layers, by_permutes, boundary, w_in, w_out, given, *refs):
    outs, (slab, rows, pieces, copies) = refs[: -4], refs[-4:]
    count = slab.shape[0]
    first, second = (boundary.at[0, pl.ds(i * count, count)] for i in range(2))
    slab_copy = choose(copies, second, first, slab)
    leaving = []
    if by_permutes:
        other_rows, *out_pieces = outs
        spot = Spot()
        width = w_in.shape[2] // (2 * BLOCKS)
        arriving = []
        for block in range(BLOCKS):
            source = w_in.at[:, :, rows_at((2 * block + 1 - spot.core) * width, width)]
            arriving.append(copies.start(source, rows.at[:, :, pl.ds(block * width, width)]))
        high = w_out.shape[1] // BLOCKS
        for layer in range(layers):
            source = w_out.at[layer, rows_at(spot.section * high, high)]
            arriving.append(copies.start(source, pieces.at[layer]))
        for copy in arriving[:BLOCKS]:
            copy.wait()
        leaving.append(copies.start(rows, other_rows))
        for layer in range(layers):
            arriving[BLOCKS + layer].wait()
            leaving.append(copies.start(pieces.at[layer], out_pieces[layer]))
    slab_copy.wait()
    leaving.append(copies.start(slab, given))
    return leaving


class Gather:
    def __init__(self, place, name, w, other_rows, layer, by_rows):
        self.place, self.name, self.by_rows = place, name, by_rows
        self.w, self.other_rows, self.layer = w, other_rows, layer

    def join(self, after=()):
        layer, rows, width = self.layer, self.w.shape[1], self.w.shape[2] // (2 * BLOCKS)

        def run(w, other_rows, out, held, copies):
            spot = Spot()
            own = w.at[layer, :, rows_at((2 * spot.section + spot.core) * width, width)]
            other = other_rows.at[layer, :, rows_at(spot.section * width, width)]
            arriving = [copies.start(ref, held.at[i]) for i, ref in enumerate((own, other))]
            leaving = []
            for i, core in enumerate((spot.core, 1 - spot.core)):
                arriving[i].wait()
                leaving.append(copies.start(held.at[i], out.at[rows_at(core * rows, rows)]))
            return leaving

        (piece,) = call(
            run,
            [(HBM, self.w), (HBM, self.other_rows)],
            [(HBM, (2 * rows, width), BF16)],
            [((2, rows, width), BF16)],
            "piece_" + self.name,
            after,
        )
        return piece

    def shift(self, piece):
        self.piece = piece
        self.moved = [self.place.shift_chip(piece, i) for i in range(1, self.place.chips)]

    def one(self, after=()):
        self.along = pack("along_" + self.name, self.moved, after)
        self.from_one = self.place.plane_one(self.along)

    def two(self, after=()):
        self.near = pack("near_" + self.name, [self.along, self.from_one], after)
        self.far = self.place.plane_two(self.near)

    def sources(self):
        if self.by_rows:
            return [self.w, self.near, self.far]
        return [self.w, self.other_rows, self.near, self.far]


def load_in(layer, sources, scratch, copies):
    if len(sources) == 1:
        width = scratch.shape[2]
        return [[copies.start(sources[0].at[:, pl.ds(i * width, width)], scratch.at[i])] for i in range(2)]
    own, other, near, far = sources
    spot = Spot()
    rows, width = own.shape[1], near.shape[2]
    pairs = []
    for pair in range(2):
        started = []
        for side in range(2):
            turn = 2 * pair + side
            columns = pl.ds(side * width, width)
            block = spot.block(turn)
            source, first = ((near, 3), (far, 3), (far, 0), (near, 0))[turn]
            for apart in range(1, spot.chips):
                chip = (spot.chip + spot.chips - apart) % spot.chips
                target = scratch.at[pair, rows_at(chip * 2 * rows, 2 * rows), columns]
                started.append(copies.start(source.at[first + apart - 1], target))
            for core, ref, index in (
                (spot.core, own, rows_at((2 * block + spot.core) * width, width)),
                (1 - spot.core, other, rows_at(block * width, width)),
            ):
                target = scratch.at[pair, rows_at((2 * spot.chip + core) * rows, rows), columns]
                started.append(copies.start(ref.at[layer, :, index], target))
        pairs.append(started)
    return pairs


def load_out(layer, sources, scratch, copies):
    if len(sources) == 1:
        return [copies.start(sources[0], scratch)]
    own, near, far = sources
    spot = Spot()
    shard, rows = own.shape[1], near.shape[1]
    started = []
    for apart in range(spot.chips):
        chip = (spot.chip + spot.chips - apart) % spot.chips
        start = spot.turn_of(chip) * shard
        if apart == 0:
            started.append(copies.start(own.at[layer], scratch.at[rows_at(start, shard), :]))
            continue
        for turn, (source, first) in enumerate(((near, 3), (far, 3), (far, 0), (near, 0))):
            part = pl.ds(pl.multiple_of(start + spot.block(turn) * rows, rows), rows)
            started.append(copies.start(source.at[first + apart - 1], scratch.at[part, :]))
    return started


class Scatter:
    def __init__(self, place, name, first, rest, by_rows):
        self.place, self.name, self.rest, self.by_rows = place, name, rest, by_rows
        self.chips, self.unit = rest.shape[1], rest.shape[2:]
        self.from_one = place.plane_one(first)

    def two(self, after):
        half = self.chips // 2
        parts = [pl.ds(i * half, half) for i in range(2)]
        terms = [
            (self.rest, [(0, part) for part in parts]),
            (self.from_one, [(1, part) for part in parts]),
        ]
        unit = (half,) + self.unit
        targets = [(0, (part,)) for part in parts]
        shape = (self.chips,) + self.unit
        (second,) = move("two_" + self.name, terms, unit, [shape], targets, after)
        self.from_two = self.place.plane_two(second)
        return second

    def own_terms(self, aparts):
        return [
            (self.rest, [(1, i) for i in aparts]),
            (self.from_one, [(0, i) for i in aparts]),
            (self.from_two, [(i,) for i in aparts]),
        ]

    def three(self, after):
        aparts = range(1, self.chips)
        targets = [(i - 1, ()) for i in aparts]
        outs = [self.unit] * (self.chips - 1)
        pieces = move("three_" + self.name, self.own_terms(aparts), self.unit, outs, targets, after)
        self.moved = [self.place.shift_chip(piece, i) for piece, i in zip(pieces, aparts)]
        return pieces[0]

    def four(self, after):
        if self.by_rows:
            terms = self.own_terms([0]) + [(piece, [()]) for piece in self.moved]
            (self.sum,) = move("four_" + self.name, terms, self.unit, [self.unit], [(0, ())], after)
            return self.sum
        rows, width = self.unit[0] // 2, self.unit[1]
        parts = [
            lambda spot: (rows_at(spot.core * rows, rows),),
            lambda spot: (rows_at((1 - spot.core) * rows, rows),),
        ]

        def of(head):
            return [lambda spot, part=part: head + part(spot) for part in parts]

        terms = [
            (self.rest, of((1, 0))),
            (self.from_one, of((0, 0))),
            (self.from_two, of((0,))),
        ] + [(piece, of(())) for piece in self.moved]
        targets = [(0, ()), (1, ())]
        self.kept, given = move("four_" + self.name, terms, (rows, width), [(rows, width)] * 2, targets, after)
        self.from_core = self.place.swap_core(given)
        return self.kept


def join(name, scatters, after):
    given = []
    for scatter in scatters:
        given += [scatter.sum] if scatter.by_rows else [scatter.kept, scatter.from_core]
    rows, width = scatters[0].kept.shape if not scatters[0].by_rows else scatters[0].sum.shape
    width = 2 * width if not scatters[0].by_rows else width

    def run(*refs):
        ins, (out, held, copies) = list(refs[: len(given)]), refs[len(given) :]
        spot = Spot()
        arriving = []
        for i, scatter in enumerate(scatters):
            if scatter.by_rows:
                arriving.append(copies.start(ins.pop(0), held.at[i]))
                continue
            for core in (spot.core, 1 - spot.core):
                half = rows_at(core * (width // 2), width // 2)
                arriving.append(copies.start(ins.pop(0), held.at[i, :, half]))
        for copy in arriving:
            copy.wait()
        return [copies.start(held, out)]

    whole = ((len(scatters), rows, width), BF16)
    (joined,) = call(run, [(HBM, array) for array in given], [(HBM,) + whole], [whole], name, after)
    return joined


def collect_kernel(groups, *refs):
    n = 3 * len(groups)
    ins, (grad_in, grad_out, held, high, copies) = refs[:n], refs[n:]
    spot = Spot()
    rows, width = held.shape[1:]
    parts = []
    for g, group in enumerate(groups):
        mine, one, two = ins[3 * g : 3 * g + 3]
        size = len(group)
        for i, (layer, by_rows) in enumerate(group):
            sources = ((mine.at[i], 3), (one.at[i], 0), (two.at[i], 2), (two.at[size + i], 1))
            for source, turn in sources:
                quarter = spot.block(turn)
                if by_rows:
                    target = grad_out.at[layer, rows_at(quarter * rows, rows), :]
                else:
                    target = grad_in.at[layer, :, rows_at(quarter * width, width)]
                parts.append((copies.start(source, held.at[len(parts)]), target))
    leaving = []
    for i, (copy, target) in enumerate(parts):
        copy.wait()
        high[i] = held[i].astype(F32)
        leaving.append(copies.start(high.at[i], target))
    return leaving


SMALL_HOPS = (
    lambda s, z, c: (s, z, 1 - c),
    lambda s, z, c: (s ^ 1, z, c),
    lambda s, z, c: (s ^ 2, z, c),
    lambda s, z, c: (s, z ^ 1, c),
    lambda s, z, c: (s, z ^ 2, c),
)


def norm(values):
    center = jnp.mean(values, axis=-1, keepdims=True)
    offsets = values - center
    inverse = lax.rsqrt(jnp.mean(offsets * offsets, axis=-1, keepdims=True) + 1e-05)
    return offsets * inverse, inverse


def norm_back(upstream, unit, inverse, gain):
    scaled = upstream * gain
    center = jnp.mean(scaled, axis=-1, keepdims=True)
    along = jnp.mean(scaled * unit, axis=-1, keepdims=True)
    return inverse * (scaled - center - unit * along)


def gelu_both(v):
    scale = math.sqrt(2.0 / math.pi)
    square = v * v
    half = 0.5 + 0.5 * jnp.tanh(v * (scale + (scale * 0.044715) * square))
    spread = (2.0 * half) * (1.0 - half)
    return v * half, half + (v * spread) * (scale + (3.0 * scale * 0.044715) * square)


def mix_forward(rows, hid, seq, gain, shift, real, imag, outs):
    unit, inverse, normed_low = outs
    hid_cos, hid_sin = hid[0](), hid[1]()

    @row_steps(rows.shape[0])
    def _(at):
        real[at, :] = dot(rows[at, :], hid_cos[...]).astype(BF16)
        imag[at, :] = dot(rows[at, :], hid_sin[...]).astype(BF16)

    seq_cos, seq_sin = seq[0](), seq[1]()

    @row_steps(rows.shape[0])
    def _(at):
        mixed = dot(seq_cos[at, :], real[...]) - dot(seq_sin[at, :], imag[...])
        unit_rows, inverse_rows = norm(rows[at, :].astype(F32) + mixed)
        unit.buffer[at, :] = unit_rows
        inverse[at, :] = inverse_rows
        normed_low.buffer[at, :] = (unit_rows * gain[...] + shift[...]).astype(BF16)
        normed_low.push(at)
        unit.push(at)


def first_mix_kernel(numbers, boundary, received, hid_cos, hid_sin, cos_tiles, sin_tiles, gain, shift, *refs):
    seq_cos, seq_sin = refs[0:2]
    outs, (rows, real, imag, copies) = refs[2:5], refs[5:]
    chosen = choose(copies, boundary.at[0, pl.ds(0, rows.shape[0])], received, rows)
    cos_tiles, sin_tiles = cos_tiles(), sin_tiles()
    base = cos_tiles.shape[1]
    slots = seq_cos.buffer.shape[0] // base
    for i in range(slots):
        for j in range(slots):
            window = (pl.ds(i * base, base), pl.ds(j * base, base))
            number = numbers[i * slots + j]
            seq_cos.buffer[window] = cos_tiles[number]
            seq_sin.buffer[window] = sin_tiles[number]
    seq_cos.push()
    seq_sin.push()
    seq = (lambda: seq_cos.buffer, lambda: seq_sin.buffer)
    chosen.wait()
    mix_forward(rows, (hid_cos, hid_sin), seq, gain, shift, real, imag, outs)


def expand_kernel(layer, by_permutes, n_sources, normed, other_normed, b_in, *refs):
    sources, (hidden, slope, whole, copies) = refs[:n_sources], refs[n_sources:]
    scratch = whole.buffer
    loaded = load_in(layer, sources, scratch, copies)
    spot = Spot(by_permutes)
    width = scratch.shape[2]
    count = normed.buffer.shape[0]
    for pair in range(2):
        biases = [b_in[:, rows_at(spot.block(2 * pair + i) * (width // 2), width // 2)] for i in range(2)]
        bias = jnp.concatenate(biases, axis=1)
        for copy in loaded[pair]:
            copy.wait()
        whole.push(pair)
        for place, rows in enumerate((normed, other_normed)):
            rows = rows()

            @row_steps(count)
            def _(at):
                value, rate = gelu_both(dot(rows[at, :], scratch[pair]) + bias)
                to = pl.ds(place * count + at.start, at.size)
                hidden.buffer[pair, to, :] = value.astype(BF16)
                slope.buffer[pair, to, :] = rate.astype(BF16)

        hidden.push(pair)
        slope.push(pair)


def contract_kernel(layer, n_sources, hidden, *refs):
    sources, (own, other, whole, copies) = refs[:n_sources], refs[n_sources:]
    scratch = whole.buffer
    loaded = load_out(layer, sources, scratch, copies)
    count, width = own.buffer.shape[0], hidden.buffer.shape[2]
    for copy in loaded:
        copy.wait()
    whole.push()
    for place, out in ((1, other), (0, own)):

        @row_steps(count)
        def _(at):
            rows = pl.ds(place * count + at.start, at.size)
            hidden(1)
            held = hidden.buffer
            total = dot(held[0, rows, :], scratch[0:width, :]) + dot(held[1, rows, :], scratch[width:, :])
            out.buffer[at, :] = total.astype(out.buffer.dtype)
            out.push(at)


def second_norm(at, own, received, unit_one, gain_one, shift_one, b_out):
    normed = unit_one[at, :] * gain_one[...] + shift_one[...]
    return norm(normed + (own[at, :] + received[at, :].astype(F32) + b_out[...]))


def middle_kernel(own, received, unit_one, gain_one, shift_one, b_out, gain_two, shift_two, *refs):
    hid, seq, (next_gain, next_shift) = refs[:2], refs[2:4], refs[4:6]
    unit_two, inverse_two = refs[6:8]
    outs, (mid, real, imag, _) = refs[8:11], refs[11:]
    own, received, unit_one = own(), received(), unit_one()

    @row_steps(mid.shape[0])
    def _(at):
        unit, inverse = second_norm(at, own, received, unit_one, gain_one, shift_one, b_out)
        unit_two.buffer[at, :] = unit
        inverse_two[at, :] = inverse
        mid[at, :] = (unit * gain_two[...] + shift_two[...]).astype(BF16)

    unit_two.push()
    mix_forward(mid, hid, seq, next_gain, next_shift, real, imag, outs)


def second_back(at, upstream, unit, inverse, gain, d_second, branch_grad, small):
    grad = norm_back(upstream, unit, inverse, gain[...])
    low = grad.astype(BF16)
    branch_grad.buffer[at, :] = low
    branch_grad.push(at)
    d_second.buffer[at, :] = grad
    d_second.push(at)
    small[0:1, :] += column_sum(low.astype(F32))
    small[1:2, :] += column_sum(upstream * unit)
    small[2:3, :] += column_sum(upstream)


def turn_kernel(own, received, unit_one, gain_one, shift_one, b_out, gain_two, shift_two, *refs):
    boundary, given, out_rows, d_second, branch_grad, small, cotangent, copies = refs
    count = cotangent.shape[0]
    chosen = choose(copies, given, boundary.at[0, pl.ds(count, count)], cotangent)
    own, received, unit_one = own(), received(), unit_one()
    small[...] = jnp.zeros_like(small)
    chosen.wait()

    @row_steps(own.shape[0])
    def _(at):
        unit, inverse = second_norm(at, own, received, unit_one, gain_one, shift_one, b_out)
        out_rows.buffer[at, :] = (unit * gain_two[...] + shift_two[...]).astype(BF16)
        upstream = cotangent[at, :].astype(F32)
        second_back(at, upstream, unit, inverse, gain_two, d_second, branch_grad, small)
        out_rows.push(at)


def grad_out_kernel(by_permutes, hidden_parts, branch_grad, other_grad, *refs):
    outs, (tiles, both, copies) = refs[:-3], refs[-3:]
    spot = Spot(by_permutes)
    count = both.shape[0] // 2
    shard, width = tiles.shape[1:]
    arriving = [copies.start(ref, both.at[pl.ds(i * count, count)]) for i, ref in enumerate((branch_grad, other_grad))]
    for copy in arriving:
        copy.wait()
    leaving = []
    for turn in range(BLOCKS):
        columns = pl.ds((turn % 2) * shard, shard)
        hidden = hidden_parts(1)
        tiles[turn] = dot(hidden[turn // 2, :, columns], both[...], ((0,), (0,))).astype(BF16)
        if not by_permutes:
            leaving.append(copies.start(tiles.at[turn], outs[0].at[pl.ds(turn * shard, shard), :]))
            continue
        rows = outs[0].shape[2]
        apart = (spot.block(turn) + spot.chips - spot.chip) % spot.chips
        for slot in range(BLOCKS):
            source = tiles.at[turn, rows_at(spot.block(slot) * rows, rows), :]
            leaving.append(copies.start(source, outs[slot // 2].at[slot % 2, apart]))
    return leaving


def shrink_kernel(by_permutes, n_outs, branch_grad, other_grad, slope, normed, other_normed, whole_out, whole_in, *refs):
    outs, (b_grad, own, other, tiles, act_grad, both_grads, both_normed, copies) = refs[:n_outs], refs[n_outs:]
    spot = Spot(by_permutes)
    count = both_grads.shape[0] // 2
    width = tiles.shape[2]
    half = width // 2
    arriving = []
    for refs, both in (((branch_grad, other_grad), both_grads), ((normed, other_normed), both_normed)):
        arriving.append([copies.start(ref, both.at[pl.ds(i * count, count)]) for i, ref in enumerate(refs)])
    for copy in arriving[0]:
        copy.wait()
    b_grad[...] = jnp.zeros_like(b_grad)
    leaving = []
    for pair in range(2):
        weights = whole_out(1)[pl.ds(pair * width, width), :]
        rates = slope(1)
        sums = []

        @row_steps(2 * count)
        def _(at):
            grad = dot(both_grads[at, :], weights, ((1,), (1,)))
            low = (grad * rates[pair, at, :].astype(F32)).astype(BF16)
            act_grad[pair, at, :] = low
            sums.append(column_sum(low.astype(F32)))

        total = sum(sums[1:], sums[0])
        for side in range(2):
            block = spot.block(2 * pair + side)
            b_grad[:, rows_at((2 * block + spot.core) * half, half)] = total[:, side * half : (side + 1) * half]
        if pair == 0:
            for copy in arriving[1]:
                copy.wait()

        @row_steps(tiles.shape[1])
        def _(at):
            tiles[pair, at, :] = dot(both_normed[:, at], act_grad[pair], ((0,), (0,))).astype(BF16)

        if not by_permutes:
            leaving.append(copies.start(tiles.at[pair], outs[0].at[:, pl.ds(pair * width, width)]))
            continue
        rows = outs[0].shape[2]
        for side in range(2):
            for chip in range(spot.chips):
                apart = (chip + spot.chips - spot.chip) % spot.chips
                source = tiles.at[pair, pl.ds(chip * rows, rows), pl.ds(side * half, half)]
                leaving.append(copies.start(source, outs[pair].at[side, apart]))
    whole_in = whole_in()
    for place, out in ((1, other), (0, own)):

        @row_steps(count)
        def _(at):
            rows = pl.ds(place * count + at.start, at.size)
            total = dot(act_grad[0, rows, :], whole_in[0], ((1,), (1,)))
            total = total + dot(act_grad[1, rows, :], whole_in[1], ((1,), (1,)))
            out.buffer[at, :] = total.astype(out.buffer.dtype)
            out.push(at)

    return leaving


def unmix(refs, total, mix_grad, real, imag, small, input_grad):
    own, received, d_second, unit_one, inverse_one, gain_one, hid_cos, hid_sin, seq_cos, seq_sin = refs
    own, received, d_second, unit_one = own(), received(), d_second(), unit_one()
    small[...] = jnp.zeros_like(small)

    @row_steps(total.shape[0])
    def _(at):
        upstream = d_second[at, :] + own[at, :] + received[at, :].astype(F32)
        unit = unit_one[at, :]
        grad = norm_back(upstream, unit, inverse_one[at, :], gain_one[...])
        total[at, :] = grad
        mix_grad[at, :] = grad.astype(BF16)
        small[0:1, :] += column_sum(upstream * unit)
        small[1:2, :] += column_sum(upstream)

    seq_cos, seq_sin = seq_cos(), seq_sin()

    @row_steps(total.shape[0])
    def _(at):
        real[at, :] = dot(seq_cos[at, :], mix_grad[...]).astype(BF16)
        imag[at, :] = (-dot(seq_sin[at, :], mix_grad[...])).astype(BF16)

    hid_cos, hid_sin = hid_cos(), hid_sin()

    @row_steps(total.shape[0])
    def _(at):
        grad = dot(real[at, :], hid_cos[...]) + dot(imag[at, :], hid_sin[...])
        input_grad(at, total[at, :] + grad)


def last_kernel(*refs):
    ins, (out_rows, *smalls) = refs[:10], refs[10:17]
    sent, kept, packed, total, mix_grad, real, imag, small, _ = refs[17:]
    is_first = lax.axis_index("section") % 2 == 0
    rows = out_rows()

    def input_grad(at, values):
        low = values.astype(BF16)
        sent.buffer[at, :] = jnp.where(is_first, rows[at, :], low)
        kept.buffer[at, :] = jnp.where(is_first, low, rows[at, :])
        sent.push(at)
        kept.push(at)

    unmix(ins, total, mix_grad, real, imag, small, input_grad)
    width = small.shape[1]
    packed[...] = jnp.zeros_like(packed)
    for layer in range(2):
        b_grad, sums_two = smalls[3 * layer : 3 * layer + 2]
        sums_one = smalls[3 * layer + 2] if layer else small
        start = layer * (packed.shape[0] // 2)
        for i in range(BLOCKS):
            packed[start + i : start + i + 1, :] = b_grad[:, i * width : (i + 1) * width]
        for i, row in enumerate((sums_two[0:1], sums_one[0:1], sums_one[1:2], sums_two[1:2], sums_two[2:3])):
            packed[start + BLOCKS + i : start + BLOCKS + i + 1, :] = row


def finish_kernel(kept, back, result, held, high, copies):
    layer = lax.axis_index("section") % 2
    count = held.shape[1]
    arriving = [copies.start(ref, held.at[i]) for i, ref in enumerate((kept, back))]
    leaving = []
    for i, block in enumerate((layer, 1 - layer)):
        arriving[i].wait()
        high[i] = held[i].astype(F32)
        leaving.append(copies.start(high.at[i], result.at[0, rows_at(block * count, count)]))
    return leaving


def relay_kernel(*refs):
    ins, (unit_two, inverse_two, gain_two) = refs[:10], refs[10:13]
    small, d_second, branch_grad, small_two, total, mix_grad, real, imag, _ = refs[13:]
    small_two[...] = jnp.zeros_like(small_two)

    def input_grad(at, values):
        upstream = values.astype(BF16).astype(F32)
        unit = unit_two()[at, :]
        second_back(at, upstream, unit, inverse_two[at, :], gain_two, d_second, branch_grad, small_two)

    unmix(ins, total, mix_grad, real, imag, small, input_grad)


def body(boundary, bucket_ids, w_in, b_in, w_out, b_out, gain_one, shift_one, gain_two, shift_two):
    place = Place()
    layers = w_in.shape[0]
    micro_count = bucket_ids.shape[1]
    feat_width = boundary.shape[2]
    ff_width = w_in.shape[2]
    slab_len = boundary.shape[1] // micro_count
    slots = bucket_ids.shape[2]
    base_len = slab_len // slots
    half_block = ff_width // (2 * BLOCKS)
    by_permutes = place.n_section == 4 and place.chips == 4
    last = layers - 1

    bucket_row = bucket_ids[place.section // 2, place.section % 2]
    half_bias = lax.dynamic_index_in_dim(
        b_in.reshape(layers, BLOCKS, 2, half_block), place.core, 2, keepdims=False
    ).reshape(layers, -1)

    block = (slab_len, feat_width)
    both = (2 * slab_len, feat_width)
    wide_block = (2, 2 * slab_len, ff_width // 4)
    whole_in_shape = (2, feat_width, ff_width // 4)
    whole_out_shape = (ff_width // 2, feat_width)
    column = (VMEM, (slab_len, 1), F32)
    sums_shape = (VMEM, (8, feat_width), F32)
    mix_outs = [(EARLY, block, F32), column, (EARLY, block, BF16)]
    hid = [(LATE, jnp.asarray(table.astype(BF16))) for table in dft_tables(feat_width)]

    def late(*arrays):
        return [(LATE, array) for array in arrays]

    def plain(*arrays):
        return [(HBM, array) for array in arrays]

    def param(array, layer):
        return (VMEM, array[layer][None])

    shard_rows, piece_rows = w_in.shape[1], w_out.shape[1] // BLOCKS
    prepared = [(HBM, block, BF16)]
    if by_permutes:
        prepared += [(HBM, (layers, shard_rows, ff_width // 2), BF16)]
        prepared += [(HBM, (piece_rows, feat_width), BF16)] * layers
    given, *prepared = call(
        partial(prepare_kernel, layers, by_permutes),
        plain(boundary, w_in, w_out),
        prepared,
        [
            (block, BF16),
            ((layers, shard_rows, ff_width // 2), BF16),
            ((layers, piece_rows, feat_width), BF16),
        ],
        "prepare",
    )
    sources_in, sources_out = [None] * layers, [None] * layers
    if by_permutes:
        other_rows = place.swap_core(prepared[0])
    received = place.swap_layer(given)
    if by_permutes:
        in_zero, out_zero, in_one, out_one = (
            Gather(place, name + str(layer), w, other_rows, layer, by_rows)
            for layer in range(layers)
            for name, w, by_rows in (("in", w_in, False), ("out", w_out, True))
        )
        in_zero.shift(in_zero.join())
        in_zero.one([received])
        out_zero.shift(tie(prepared[1], in_zero.along))
        first_after = [in_zero.along]
    else:
        for layer in range(layers):
            whole_in, whole_out = (
                lax.all_gather(w[layer], "dp", axis=0, tiled=True) for w in (w_in, w_out)
            )
            whole_in = whole_in.reshape(feat_width, BLOCKS, 2, half_block)
            whole_out = whole_out.reshape(BLOCKS, 2, half_block, feat_width)
            whole_in = lax.dynamic_index_in_dim(whole_in, place.core, 2, keepdims=False)
            whole_out = lax.dynamic_index_in_dim(whole_out, place.core, 1, keepdims=False)
            sources_in[layer] = [whole_in.reshape(feat_width, -1)]
            sources_out[layer] = [whole_out.reshape(-1, feat_width)]
        first_after = []

    numbers = tile_numbers(bucket_row, slots).reshape(-1)
    tiles = [(LATE, jnp.asarray(table)) for table in sequence_tiles(base_len)]
    seq_cos, seq_sin, *mixed = call(
        first_mix_kernel,
        [(SMEM, numbers)]
        + plain(boundary, received)
        + hid
        + tiles
        + [param(gain_one, 0), param(shift_one, 0)],
        [(EARLY, (slab_len, slab_len), BF16)] * 2 + mix_outs,
        [(block, BF16)] * 3,
        "first_mix",
        first_after,
    )
    tables = hid + late(seq_cos, seq_sin)

    both_pairs, all_rows = pl.ds(0, 2), pl.ds(0, 2 * slab_len)
    steps = slab_len // ROW_STEP
    row_parts = [
        (both_pairs, pl.ds(slab_len * place_ + i * ROW_STEP, ROW_STEP))
        for place_ in (1, 0)
        for i in range(steps)
    ]
    block_parts = [
        (pair, all_rows, pl.ds(side * half_block, half_block)) for pair in range(2) for side in range(2)
    ]
    pair_parts = [(pl.ds(pair, 1),) for pair in range(2)]
    half_parts = [(pl.ds(pair * 2 * half_block, 2 * half_block),) for pair in range(2)]

    saved, wholes_in, wholes_out = [], [], []
    for layer in range(layers):
        unit_one, inverse_one, normed = mixed
        expand_after, contract_after, middle_after = [], [], []
        if by_permutes and layer == 0:
            in_zero.two([normed])
            other_normed = place.swap_core(tie(normed, in_zero.near))
            out_zero.one([in_zero.near])
            in_one.shift(in_one.join([out_zero.along, in_zero.far, other_normed]))
            out_zero.two([in_one.piece])
            sources_in[0] = in_zero.sources()
            expand_after = [out_zero.near]
        else:
            other_normed = place.swap_core(normed)
        if by_permutes and layer == 1:
            out_one.two([normed, in_one.far])
            sources_in[1] = in_one.sources()
            expand_after = [out_one.near]
        hidden, slope, whole_in = call(
            partial(expand_kernel, layer, by_permutes, len(sources_in[layer])),
            late(normed, other_normed)
            + [(VMEM, half_bias[layer][None])]
            + plain(*sources_in[layer]),
            [(EARLY, wide_block, BF16), (EARLY, wide_block, BF16), (EARLY, whole_in_shape, BF16)],
            [],
            "expand",
            expand_after,
        )
        if by_permutes and layer == 0:
            in_one.one([hidden])
            out_one.shift(tie(prepared[2], in_one.along))
            sources_out[0] = out_zero.sources()
            contract_after = [in_one.along]
        if by_permutes and layer == 1:
            sources_out[1] = out_one.sources()
        own_part, other_part, whole_out = call(
            partial(contract_kernel, layer, len(sources_out[layer])),
            [(LATE, hidden, row_parts)] + plain(*sources_out[layer]),
            [(EARLY, block, F32), (EARLY, block, BF16), (EARLY, whole_out_shape, BF16)],
            [],
            "contract",
            contract_after,
        )
        from_other = place.swap_core(other_part)
        if by_permutes and layer == 0:
            in_one.two([own_part])
            out_one.one([in_one.near])
            middle_after = [out_one.along]
        wholes_in.append(whole_in)
        wholes_out.append(whole_out)
        common = late(own_part, from_other, unit_one) + [
            param(p, layer) for p in (gain_one, shift_one, b_out, gain_two, shift_two)
        ]
        kept = [unit_one, inverse_one, normed, other_normed, hidden, slope]
        if layer < last:
            unit_two, inverse_two, *mixed = call(
                middle_kernel,
                common + tables + [param(gain_one, layer + 1), param(shift_one, layer + 1)],
                [(EARLY, block, F32), column] + mix_outs,
                [(block, BF16), (block, BF16), (block, BF16)],
                "middle",
                middle_after,
            )
            kept += [unit_two, inverse_two]
        saved.append(kept)

    out_rows, d_second, branch_grad, sums_two = call(
        turn_kernel,
        common + plain(boundary, received),
        [(EARLY, block, BF16), (EARLY, block, F32), (EARLY, block, BF16), sums_shape],
        [(block, BF16)],
        "turn",
    )

    if by_permutes:
        piece_out = (2, place.chips, w_out.shape[1] // BLOCKS, feat_width)
        piece_in = (2, place.chips, 2 * w_in.shape[1], half_block)
        grad_outs = {True: [(HBM, piece_out, BF16)] * 2, False: [(HBM, piece_in, BF16)] * 2}
    else:
        grad_outs = {
            True: [(HBM, (ff_width // 2, feat_width), BF16)],
            False: [(HBM, (feat_width, ff_width // 2), BF16)],
        }
    n_outs = len(grad_outs[True])
    grads, smalls, running = {}, {}, []

    def reduce_grad(pieces, layer, by_rows):
        name = ("out" if by_rows else "in") + str(layer)
        if by_permutes:
            grads[layer, by_rows] = Scatter(place, name, *pieces, by_rows)
            running.append(grads[layer, by_rows])
            return
        (half,) = pieces
        if by_rows:
            whole = jnp.zeros((BLOCKS, 2, half_block, feat_width), BF16)
            half = half.reshape(BLOCKS, 1, half_block, feat_width)
            whole = lax.dynamic_update_slice_in_dim(whole, half, place.core, 1)
            whole = whole.reshape(ff_width, feat_width)
        else:
            whole = jnp.zeros((feat_width, BLOCKS, 2, half_block), BF16)
            half = half.reshape(feat_width, BLOCKS, 1, half_block)
            whole = lax.dynamic_update_slice_in_dim(whole, half, place.core, 2)
            whole = whole.reshape(feat_width, ff_width)
        part = lax.psum_scatter(whole, "dp", scatter_dimension=0, tiled=True)
        grads[layer, by_rows] = lax.psum(part, "section").astype(F32)

    reached = []
    for layer in reversed(range(layers)):
        unit_one, inverse_one, normed, other_normed, hidden, slope = saved[layer][:6]
        other_grad = place.swap_core(branch_grad)
        if by_permutes and layer == 0:
            reached = [running[1].two([d_second])]
            reached = [running[0].three(reached)]
        pieces = call(
            partial(grad_out_kernel, by_permutes),
            [(LATE, hidden, block_parts)] + plain(branch_grad, other_grad),
            grad_outs[True],
            [((BLOCKS, half_block, feat_width), BF16), (both, BF16)],
            "grad_out",
            reached,
        )
        reduce_grad(pieces, layer, True)
        *pieces, b_grad, own_part, other_part = call(
            partial(shrink_kernel, by_permutes, n_outs),
            plain(branch_grad, other_grad)
            + [(LATE, slope, pair_parts)]
            + plain(normed, other_normed)
            + [(LATE, wholes_out[layer], half_parts)]
            + late(wholes_in[layer]),
            grad_outs[False]
            + [(VMEM, (1, ff_width), F32), (EARLY, block, F32), (EARLY, block, BF16)],
            [
                ((2, feat_width, ff_width // 4), BF16),
                (wide_block, BF16),
                (both, BF16),
                (both, BF16),
            ],
            "shrink",
            [pieces[0]],
        )
        reached = [own_part]
        if by_permutes and layer == 0:
            reached = [running[0].four([own_part, running[1].from_two])]
            other_part, *pieces = (tie(part, *reached) for part in (other_part, *pieces))
        from_other = place.swap_core(other_part)
        reduce_grad(pieces, layer, False)
        if by_permutes:
            reached = [running[-2].two(reached)]
            if layer == 0:
                reached = [running[1].three(reached + [from_other])]
        ins = (
            late(own_part, from_other, d_second, unit_one)
            + [(VMEM, inverse_one), param(gain_one, layer)]
            + tables
        )
        work = [(block, F32), (block, BF16), (block, BF16), (block, BF16)]
        smalls[layer] = [b_grad, sums_two]
        if layer > 0:
            below_unit, below_inverse = saved[layer - 1][6:8]
            sums_one, d_second, branch_grad, sums_two = call(
                relay_kernel,
                ins + late(below_unit) + [(VMEM, below_inverse), param(gain_two, layer - 1)],
                [sums_shape, (EARLY, block, F32), (EARLY, block, BF16), sums_shape],
                work,
                "relay",
                reached,
            )
            smalls[layer].append(sums_one)
    vectors = smalls[0] + [smalls[1][2]] + smalls[1]
    sent, kept_rows, packed = call(
        last_kernel,
        ins + late(out_rows) + [(VMEM, vector) for vector in vectors],
        [(EARLY, block, BF16), (EARLY, block, BF16), (VMEM, (32, feat_width), F32)],
        work + [((8, feat_width), F32)],
        "last",
        reached,
    )

    if by_permutes:

        def hop(i, *reached):
            nonlocal packed
            packed = packed + place.permute(tie(packed, *reached), SMALL_HOPS[i])
            return packed

        out_last, in_last, out_first, in_first = running
        step = in_first.two([kept_rows, out_first.from_two])
        hop(0, step)
        step = in_last.four([step, packed])
        step = out_first.three([step])
        hop(1, step, in_first.from_two, in_last.from_core)
        step = out_first.four([step, packed])
        step = in_first.three([step])
        mine = join("join_rest", [in_last, out_last, out_first], [step])
        from_one = place.plane_one(mine)
        back = place.swap_layer(tie(sent, mine))
        both_sums = pack("five_rest", [mine, from_one], [])
        from_two = place.plane_two(both_sums)
        hop(2, both_sums)
        step = in_first.four([both_sums, packed])
        hop(3, step)
        last_mine = join("join_last", [in_first], [packed])
        last_one = place.plane_one(last_mine)
        hop(4, last_mine)
        last_both = pack("five_last", [last_mine, last_one], [packed])
        last_two = place.plane_two(last_both)
        groups = [[(last, False), (last, True), (0, True)], [(0, False)]]
        held = ((8 * layers, shard_rows, ff_width // BLOCKS),)
        grad_in, grad_out = call(
            partial(collect_kernel, groups),
            plain(mine, from_one, from_two, last_mine, last_one, last_two),
            [(HBM, w_in.shape, F32), (HBM, w_out.shape, F32)],
            [held + (BF16,), held + (F32,)],
            "collect",
        )
    else:
        back = place.swap_layer(sent)
        grad_in, grad_out = (
            jnp.stack([grads[layer, by_rows] for layer in range(layers)])
            for by_rows in (False, True)
        )
        packed = lax.psum(packed, AXES)
    (result,) = call(
        finish_kernel,
        plain(kept_rows, back),
        [(HBM, (1, 2 * slab_len, feat_width), F32)],
        [((2,) + block, BF16), ((2,) + block, F32)],
        "finish",
        [packed],
    )
    half = packed.shape[0] // layers
    sums = packed.reshape(layers, half, feat_width)
    b_part = ff_width // place.n_dp
    b_sums = sums[:, :BLOCKS].reshape(layers, ff_width)
    part = feat_width // place.n_dp
    sums = lax.dynamic_slice_in_dim(sums[:, BLOCKS : BLOCKS + 5], place.dp * part, part, 2)
    small_out = [lax.dynamic_slice_in_dim(b_sums, place.dp * b_part, b_part, 1)]
    small_out += [sums[:, i] for i in range(5)]
    return (result, grad_in, small_out[0], grad_out, *small_out[1:])


def solution(mesh):
    return jax.shard_map(
        body,
        mesh=mesh,
        in_specs=(
            P("section", "dp", None),
            P(None, "dp", None),
            P(None, "dp", None),
            P(),
            P(None, "dp", None),
            P(),
            P(),
            P(),
            P(),
            P(),
        ),
        out_specs=(
            P("section", "dp", None),
            P(None, "dp", None),
            P(None, "dp"),
            P(None, "dp", None),
            P(None, "dp"),
            P(None, "dp"),
            P(None, "dp"),
            P(None, "dp"),
            P(None, "dp"),
        ),
        check_vma=False,
    )
```

```python
from functools import partial
import math

import jax
import jax.numpy as jnp
import numpy as np
from jax import lax
from jax.experimental import pallas as pl
from jax.experimental.pallas import tpu as pltpu
from jax.sharding import PartitionSpec as P

AXES = ("section", "dp")
F32 = jnp.float32
BF16 = jnp.bfloat16
BLOCKS = 4
ROW_STEP = 256

VMEM = pl.BlockSpec(memory_space=pltpu.VMEM)
SMEM = pl.BlockSpec(memory_space=pltpu.SMEM)
HBM = pl.BlockSpec(memory_space=pltpu.HBM)
LATE, EARLY = "late", "early"


class Place:
    def __init__(self):
        self.n_section = lax.axis_size("section")
        self.n_dp = lax.axis_size("dp")
        self.chips = self.n_dp // 2
        self.section = lax.axis_index("section")
        self.dp = lax.axis_index("dp")
        self.core = self.dp % 2

    def permute(self, value, target):
        pairs = []
        for section in range(self.n_section):
            for chip in range(self.chips):
                for core in range(2):
                    to_section, to_chip, to_core = target(section, chip, core)
                    source = section * self.n_dp + chip * 2 + core
                    pairs.append((source, to_section * self.n_dp + to_chip * 2 + to_core))
        return lax.ppermute(value, AXES, pairs)

    def swap_core(self, value):
        return self.permute(value, lambda s, z, c: (s, z, 1 - c))

    def swap_layer(self, value):
        return self.permute(value, lambda s, z, c: (s ^ 1, z, c))

    def plane_one(self, value):
        return self.permute(value, lambda s, z, c: (s ^ (1 + c), z, c))

    def plane_two(self, value):
        return self.permute(value, lambda s, z, c: (s ^ (2 - c), z, c))

    def along_z(self, value, flip):
        return self.permute(value, lambda s, z, c: (s, z ^ flip, c))


class Spot:
    def __init__(self, by_permutes=True):
        dp = lax.axis_index("dp")
        self.core = dp % 2
        if by_permutes:
            self.section, self.chip = lax.axis_index("section"), dp // 2
            self.chips = lax.axis_size("dp") // 2
            self.held = (1 + self.core, 3, 2 - self.core, 0)
        else:
            self.section, self.held = 0, (0, 1, 2, 3)

    def block(self, turn):
        return self.section ^ self.held[turn]

    def turn_of(self, block):
        flip = block ^ self.section
        side = jnp.where(flip == self.held[0], 0, 2)
        return jnp.where(flip == 3, 1, jnp.where(flip == 0, 3, side))


def dft_tables(length):
    positions = np.arange(length)
    angles = (positions[:, None] * positions[None, :] % length) * (2.0 * math.pi) / length
    scaling = 1.0 / math.sqrt(length)
    return (np.cos(angles) * scaling, np.sin(angles) * scaling)


def sequence_tiles(base_len):
    cos_tiles, sin_tiles = [], []
    for parts in (1, 2, 4):
        cos_table, sin_table = dft_tables(parts * base_len)
        for i in range(parts):
            for j in range(parts):
                window = (
                    slice(i * base_len, (i + 1) * base_len),
                    slice(j * base_len, (j + 1) * base_len),
                )
                cos_tiles.append(cos_table[window])
                sin_tiles.append(sin_table[window])
    cos_tiles.append(np.zeros((base_len, base_len)))
    sin_tiles.append(np.zeros((base_len, base_len)))
    return np.stack(cos_tiles).astype(BF16), np.stack(sin_tiles).astype(BF16)


def tile_numbers(bucket_row, slots):
    parts = jnp.where(bucket_row < 3, 1 << jnp.minimum(bucket_row, 2), 0)
    ends = jnp.cumsum(parts)
    where = jnp.arange(slots, dtype=jnp.int32)
    segment = jnp.sum((where[:, None] >= ends[None, :]).astype(jnp.int32), axis=1)
    one_hot = (segment[:, None] == jnp.arange(slots)[None, :]).astype(jnp.int32)
    start = jnp.sum(one_hot * (ends - parts)[None, :], axis=1)
    size = jnp.sum(one_hot * parts[None, :], axis=1)
    first = jnp.where(size == 1, 0, jnp.where(size == 2, 1, 5))
    place = where - start
    numbers = first[:, None] + place[:, None] * size[:, None] + place[None, :]
    return jnp.where(segment[:, None] == segment[None, :], numbers, 21)


def rows_at(start, size):
    return pl.ds(pl.multiple_of(start, size), size)


def dot(left, right, dims=((1,), (0,))):
    return lax.dot_general(left, right, (dims, ((), ())), preferred_element_type=F32)


def row_steps(count, step=ROW_STEP):
    step = step if count % step == 0 else count

    def run(function):
        for i in range(count // step):
            function(pl.ds(i * step, step))

    return run


def column_sum(values):
    return jnp.sum(values, axis=0, keepdims=True)


class Copies:
    def __init__(self, sems):
        self.sems, self.count = sems, 0

    def start(self, source, target):
        copy = pltpu.make_async_copy(source, target, self.sems.at[self.count])
        copy.start()
        self.count += 1
        return copy


class Late:
    def __init__(self, source, buffer, copies, parts):
        self.buffer = buffer
        if parts is None:
            self.waiting = [copies.start(source, buffer)]
        else:
            self.waiting = [copies.start(source.at[part], buffer.at[part]) for part in parts]

    def __call__(self, parts=None):
        for _ in range(len(self.waiting) if parts is None else parts):
            self.waiting.pop(0).wait()
        return self.buffer


class Early:
    def __init__(self, target, buffer, copies):
        self.target, self.buffer, self.copies, self.leaving = target, buffer, copies, []

    def push(self, part=None):
        source, target = self.buffer, self.target
        if part is not None:
            source, target = source.at[part], target.at[part]
        self.leaving.append(self.copies.start(source, target))


def tie(value, *others):
    return lax.optimization_barrier((value,) + others)[0]


class Order:
    token = None

    @classmethod
    def begin(cls):
        cls.token = jnp.zeros((8, 128), F32)

    @classmethod
    def wait(cls, *arrays):
        cls.token = tie(cls.token, *arrays)

    @classmethod
    def mark(cls, *arrays):
        cls.wait(*arrays)
        call(lambda *refs: None, [], [], [], "mark")
        return cls.token


def call(kernel, ins, outs, scratch, name, flops=3 * 10**9, aliases=None, spare=4 * 2**20):
    buffers = [pltpu.VMEM(a[1].shape, a[1].dtype) for a in ins if a[0] is LATE]
    buffers += [pltpu.VMEM(*out[1:]) for out in outs if out[0] is EARLY]
    n_ins, n_outs, n_scratch = len(ins), len(outs), len(scratch)
    counts = []

    def run(*refs):
        given, made = list(refs[:n_ins]), list(refs[n_ins + 1 :][:n_outs])
        token_out, refs = refs[n_ins + 1 + n_outs], refs[n_ins + 2 + n_outs :]
        own, held, copies = refs[:n_scratch], list(refs[n_scratch:-1]), Copies(refs[-1])
        late = []
        for i, entry in enumerate(ins):
            if entry[0] is LATE:
                given[i] = Late(given[i], held.pop(0), copies, (entry + (None,))[2])
                late.append(given[i])
        early = []
        for i, out in enumerate(outs):
            if out[0] is EARLY:
                made[i] = Early(made[i], held.pop(0), copies)
                early.append(made[i])
        leaving = kernel(*given, *made, *own, copies) or []
        token_out[...] = jnp.zeros_like(token_out)
        for value in late:
            value()
        for copy in leaving + [copy for out in early for copy in out.leaving]:
            copy.wait()
        counts.append(copies.count)

    def spec_of(spec):
        return HBM if spec in (LATE, EARLY) else spec

    held = list(scratch) + [(a[1].shape, a[1].dtype) for a in ins if a[0] in (LATE, VMEM)]
    held += [out[1:] for out in outs if out[0] in (EARLY, VMEM)]
    needed = sum(math.prod(shape) * jnp.dtype(dtype).itemsize for shape, dtype in held)

    def build(sems):
        return pl.pallas_call(
            run,
            in_specs=[spec_of(entry[0]) for entry in ins] + [HBM],
            out_specs=tuple(spec_of(out[0]) for out in outs) + (VMEM,),
            out_shape=tuple(jax.ShapeDtypeStruct(*out[1:]) for out in outs)
            + (jax.ShapeDtypeStruct((8, 128), F32),),
            scratch_shapes=[pltpu.VMEM(*s) for s in scratch]
            + buffers
            + [pltpu.SemaphoreType.DMA((sems,))],
            compiler_params=pltpu.CompilerParams(vmem_limit_bytes=needed + spare),
            cost_estimate=pl.CostEstimate(flops=flops, bytes_accessed=1000, transcendentals=0),
            input_output_aliases=aliases or {},
            name=name,
        )

    arrays = [entry[1] for entry in ins] + [Order.token]
    jax.eval_shape(build(96), *arrays)
    *made, Order.token = build(max(counts[-1], 1))(*arrays)
    return made


def move(name, terms, unit, outs, targets, flops=3 * 10**9, extra=None):
    jobs = [
        ([(array, indices[i]) for array, indices in terms], unit, target)
        for i, target in enumerate(targets)
    ]
    if extra is not None:
        jobs.append(extra)
    given = []
    for job_terms, _, _ in jobs:
        for array, _ in job_terms:
            if not any(array is other for other in given):
                given.append(array)
    scratch = []
    for job_terms, shape, _ in jobs:
        scratch += [((len(job_terms),) + tuple(shape), BF16), (tuple(shape), BF16)]

    def run(*refs):
        ins, made = refs[: len(given)], refs[len(given) : len(given) + len(outs)]
        *held, copies = refs[len(given) + len(outs) :]

        def at(ref, index):
            index = index(Spot()) if callable(index) else index
            return ref.at[index] if index else ref

        arriving = []
        for i, (job_terms, _, _) in enumerate(jobs):
            sources = [
                at(next(ref for ref, other in zip(ins, given) if other is array), index)
                for array, index in job_terms
            ]
            arriving.append(
                [copies.start(source, held[2 * i].at[t]) for t, source in enumerate(sources)]
            )
        leaving = []
        for i, (job_terms, _, (number, index)) in enumerate(jobs):
            for copy in arriving[i]:
                copy.wait()
            source = held[2 * i].at[0]
            if len(job_terms) > 1:
                total = held[2 * i][0].astype(F32)
                for t in range(1, len(job_terms)):
                    total = total + held[2 * i][t].astype(F32)
                source = held[2 * i + 1]
                source[...] = total.astype(BF16)
            leaving.append(copies.start(source, at(made[number], index)))
        return leaving

    return call(
        run,
        [(HBM, array) for array in given],
        [(HBM, shape, BF16) for shape in outs],
        scratch,
        name,
        flops,
    )


def pack(name, entries):
    entries = [entry if isinstance(entry, tuple) else (entry, None, None) for entry in entries]
    unit = entries[0][0].shape[-2:]
    sizes = [
        count or (1 if len(array.shape) == 2 else array.shape[0]) for array, _, count in entries
    ]
    starts = [sum(sizes[:i]) for i in range(len(sizes))]

    def run(*refs):
        ins, (out, held, copies) = refs[: len(entries)], refs[len(entries) :]

        def part(ref, i):
            if len(entries[i][0].shape) == 2:
                return ref.at[starts[i]]
            return ref.at[pl.ds(starts[i], sizes[i])]

        arriving = []
        for i, (ref, (_, start, count)) in enumerate(zip(ins, entries)):
            source = ref if start is None else ref.at[pl.ds(start, count)]
            arriving.append(copies.start(source, part(held, i)))
        leaving = []
        for i, copy in enumerate(arriving):
            copy.wait()
            leaving.append(copies.start(part(held, i), part(out, i)))
        return leaving

    whole = ((sum(sizes),) + unit, entries[0][0].dtype)
    (packed,) = call(
        run, [(HBM, entry[0]) for entry in entries], [(HBM,) + whole], [whole], name
    )
    return packed


def choose(copies, first, second, buffer):
    is_first = lax.axis_index("section") % 2 == 0
    sem = copies.sems.at[copies.count]
    copies.count += 1
    pair = [pltpu.make_async_copy(source, buffer, sem) for source in (first, second)]
    pl.when(is_first)(pair[0].start)
    pl.when(jnp.logical_not(is_first))(pair[1].start)
    return pair[0]


def prepare_kernel(layers, by_permutes, boundary, w_in, w_out, given, *refs):
    outs, (slab, rows, pieces, copies) = refs[: -4], refs[-4:]
    count = slab.shape[0]
    first, second = (boundary.at[0, pl.ds(i * count, count)] for i in range(2))
    slab_copy = choose(copies, second, first, slab)
    leaving = []
    if by_permutes:
        other_rows, *out_pieces = outs
        spot = Spot()
        width = w_in.shape[2] // (2 * BLOCKS)
        arriving = []
        for block in range(BLOCKS):
            source = w_in.at[:, :, rows_at((2 * block + 1 - spot.core) * width, width)]
            arriving.append(copies.start(source, rows.at[:, :, pl.ds(block * width, width)]))
        high = w_out.shape[1] // BLOCKS
        for layer in range(layers):
            source = w_out.at[layer, rows_at(spot.section * high, high)]
            arriving.append(copies.start(source, pieces.at[layer]))
        for copy in arriving[:BLOCKS]:
            copy.wait()
        leaving.append(copies.start(rows, other_rows))
        for layer in range(layers):
            arriving[BLOCKS + layer].wait()
            leaving.append(copies.start(pieces.at[layer], out_pieces[layer]))
    slab_copy.wait()
    leaving.append(copies.start(slab, given))
    return leaving


class Gather:
    def __init__(self, place, name, w, other_rows, layer, by_rows):
        self.place, self.name, self.by_rows = place, name, by_rows
        self.w, self.other_rows, self.layer = w, other_rows, layer

    def join(self, halves, out_piece=None):
        layer, rows, width = self.layer, self.w.shape[1], self.w.shape[2] // (2 * BLOCKS)
        beside = out_piece is not None
        shape = (2, rows, 2 * width) if beside else (2 * rows, width)

        def run(w, other, *refs):
            out_ref, (out, held, copies) = refs[:-3], refs[-3:]
            spot = Spot()
            own = w.at[layer, :, rows_at((2 * spot.section + spot.core) * width, width)]
            other = other.at[layer, :, rows_at(spot.section * width, width)]
            arriving = []
            for source, core in ((own, spot.core), (other, 1 - spot.core)):
                target = held.at[rows_at(core * rows, rows)]
                if beside:
                    target = held.at[0, :, rows_at(core * width, width)]
                arriving.append(copies.start(source, target))
            if beside:
                arriving.append(copies.start(out_ref[0], held.at[1]))
            for copy in arriving:
                copy.wait()
            return [copies.start(held, out)]

        (piece,) = call(
            run,
            [(HBM, self.w), (HBM, halves)] + ([(HBM, out_piece)] if beside else []),
            [(HBM, shape, BF16)],
            [(shape, BF16)],
            "piece_" + self.name,
        )
        return piece

    def shift(self, piece):
        self.moved = [self.place.along_z(piece, flip) for flip in (1, 2, 3)]

    def one(self):
        self.along = pack("along_" + self.name, self.moved)
        self.from_one = self.place.plane_one(self.along)
        self.from_two = self.place.plane_two(self.along)

    def two(self, *others):
        self.far = self.place.plane_two(tie(self.from_one, *others))

    def sources(self):
        moved = [self.along, self.from_one, self.from_two, self.far]
        return [self.w] + moved if self.by_rows else [self.w, self.other_rows] + moved


def pairs(own, moved):
    _, rows, width = own.shape

    def run(own, moved, pair_in, pair_out, held_in, held_out, copies):
        arriving = []
        for i, ref in enumerate((own, moved)):
            for core in range(2):
                half = pl.ds(core * (width // 2), width // 2)
                target = held_in.at[i, pl.ds(core * rows, rows)]
                arriving.append(copies.start(ref.at[0, :, half], target))
            arriving.append(copies.start(ref.at[1], held_out.at[i]))
        for copy in arriving:
            copy.wait()
        return [copies.start(held_in, pair_in), copies.start(held_out, pair_out)]

    shapes = [((2, 2 * rows, width // 2), BF16), ((2, rows, width), BF16)]
    return call(run, [(HBM, own), (HBM, moved)], [(HBM,) + s for s in shapes], shapes, "pairs")


def load_in(layer, sources, scratch, copies):
    if len(sources) == 1:
        width = scratch.shape[2]
        return [[copies.start(sources[0].at[:, pl.ds(i * width, width)], scratch.at[i])] for i in range(2)]
    own, other, along, one, two, far = sources
    spot = Spot()
    rows, width = own.shape[1], along.shape[2]
    pairs = []
    for pair in range(2):
        started = []
        for side in range(2):
            turn = 2 * pair + side
            columns = pl.ds(side * width, width)
            block = spot.block(turn)
            source = (one, far, two, along)[turn]
            for apart in range(1, spot.chips):
                chip = spot.chip ^ apart
                target = scratch.at[pair, rows_at(chip * 2 * rows, 2 * rows), columns]
                started.append(copies.start(source.at[apart - 1], target))
            for core, ref, index in (
                (spot.core, own, rows_at((2 * block + spot.core) * width, width)),
                (1 - spot.core, other, rows_at(block * width, width)),
            ):
                target = scratch.at[pair, rows_at((2 * spot.chip + core) * rows, rows), columns]
                started.append(copies.start(ref.at[layer, :, index], target))
        pairs.append(started)
    return pairs


def load_out(layer, sources, scratch, copies):
    if len(sources) == 1:
        return [copies.start(sources[0], scratch)]
    own, along, one, two, far = sources
    spot = Spot()
    shard, rows = own.shape[1], along.shape[1]
    started = []
    for apart in range(spot.chips):
        chip = spot.chip ^ apart
        start = spot.turn_of(chip) * shard
        if apart == 0:
            started.append(copies.start(own.at[layer], scratch.at[rows_at(start, shard), :]))
            continue
        for turn, source in enumerate((one, far, two, along)):
            part = pl.ds(pl.multiple_of(start + spot.block(turn) * rows, rows), rows)
            started.append(copies.start(source.at[apart - 1], scratch.at[part, :]))
    return started


class Scatter:
    def __init__(self, place, name, first, rest, by_rows):
        self.place, self.name, self.rest, self.by_rows = place, name, rest, by_rows
        self.chips, self.unit = rest.shape[1], rest.shape[2:]
        self.from_one = place.plane_one(first)
        self.small = None

    def move(self, stage, terms, sent, flops):
        rows, width = self.unit
        extra, height = None, sent * rows
        if self.small is not None:
            self.small_rows = self.small[0][1].size
            terms_small = [(array, (at,)) for array, at in self.small]
            target = (0, (pl.ds(height, self.small_rows),))
            extra = (terms_small, (self.small_rows, width), target)
            height += self.small_rows
        targets = [(0, (pl.ds(i * rows, rows),)) for i in range(sent)]
        name = stage + "_" + self.name
        (made,) = move(name, terms, self.unit, [(height, width)], targets, flops, extra)
        return made

    def heard(self, sent, received, count):
        if self.small is not None:
            at = pl.ds(count * self.unit[0], self.small_rows)
            self.small = [(sent, at), (received, at)]

    def part(self, i):
        return (pl.ds(i * self.unit[0], self.unit[0]),)

    def two(self, flops=3 * 10**9):
        terms = [
            (self.rest, [(0, i) for i in range(self.chips)]),
            (self.from_one, [(1, i) for i in range(self.chips)]),
        ]
        second = self.move("two", terms, self.chips, flops)
        self.from_two = self.place.plane_two(second)
        self.heard(second, self.from_two, self.chips)
        return second

    def own_terms(self, aparts):
        return [
            (self.rest, [(1, i) for i in aparts]),
            (self.from_one, [(0, i) for i in aparts]),
            (self.from_two, [self.part(i) for i in aparts]),
        ]

    def three(self, flops=3 * 10**9):
        pair = self.move("three", self.own_terms([2, 3]), 2, flops)
        self.from_pair = self.place.along_z(pair, 2)
        self.heard(pair, self.from_pair, 2)
        return pair

    def neighbour(self, flops=3 * 10**9):
        terms = self.own_terms([1]) + [(self.from_pair, [self.part(1)])]
        piece = self.move("next", terms, 1, flops)
        self.from_next = self.place.along_z(piece, 1)
        self.heard(piece, self.from_next, 1)
        return piece

    def four(self, flops=3 * 10**9):
        if self.by_rows:
            terms = self.own_terms([0]) + [
                (self.from_pair, [self.part(0)]),
                (self.from_next, [self.part(0)]),
            ]
            (self.sum,) = move(
                "four_" + self.name, terms, self.unit, [self.unit], [(0, ())], flops
            )
            return self.sum
        rows, width = self.unit[0] // 2, self.unit[1]
        parts = [
            lambda spot: (rows_at(spot.core * rows, rows),),
            lambda spot: (rows_at((1 - spot.core) * rows, rows),),
        ]

        def of(head):
            return [lambda spot, part=part: head + part(spot) for part in parts]

        terms = [
            (self.rest, of((1, 0))),
            (self.from_one, of((0, 0))),
            (self.from_two, of(())),
            (self.from_pair, of(())),
            (self.from_next, of(())),
        ]
        targets = [(0, ()), (1, ())]
        self.kept, given = move(
            "four_" + self.name, terms, (rows, width), [(rows, width)] * 2, targets, flops
        )
        self.from_core = self.place.swap_core(given)
        return self.kept


def join(name, scatters):
    given = []
    for scatter in scatters:
        given += [scatter.sum] if scatter.by_rows else [scatter.kept, scatter.from_core]
    rows, width = scatters[0].kept.shape
    width = 2 * width
    small = next((scatter.small for scatter in scatters if scatter.small is not None), [])
    given += [array for array, _ in small]
    small_rows = small[0][1].size // 2 if small else 0
    count = len(scatters)

    def run(*refs):
        ins, (out, held, small_held, copies) = list(refs[: len(given)]), refs[len(given) :]
        spot = Spot()
        arriving = []
        for i, scatter in enumerate(scatters):
            part = pl.ds(i * rows, rows)
            if scatter.by_rows:
                arriving.append(copies.start(ins.pop(0), held.at[part]))
                continue
            for core in (spot.core, 1 - spot.core):
                half = rows_at(core * (width // 2), width // 2)
                arriving.append(copies.start(ins.pop(0), held.at[part, half]))
        for t, (_, at) in enumerate(small):
            arriving.append(copies.start(ins.pop(0).at[at], small_held.at[t]))
        for copy in arriving:
            copy.wait()
        if small:
            total = small_held[0].astype(F32) + small_held[1].astype(F32)
            for i in range(2):
                part = (pl.ds(count * rows, small_rows), pl.ds(i * (width // 2), width // 2))
                held[part] = total[i * small_rows : (i + 1) * small_rows].astype(BF16)
        return [copies.start(held, out)]

    whole = ((count * rows + small_rows, width), BF16)
    small_shape = (2, max(2 * small_rows, 16), width // 2)
    scratch = [whole, (small_shape, BF16)]
    (joined,) = call(run, [(HBM, array) for array in given], [(HBM,) + whole], scratch, name)
    return joined


def collect_kernel(group, n_started, *refs):
    (mine, one, two, far), refs = refs[:4], refs[4 + n_started :]
    (*outs, held, high, copies) = refs
    spot = Spot()
    rows, width = held.shape[1:]
    parts = []
    for i, (layer, by_rows) in enumerate(group):
        part = pl.ds(i * rows, rows)
        for source, turn in ((mine, 3), (one, 0), (two, 2), (far, 1)):
            quarter = spot.block(turn)
            if by_rows:
                target = outs[1].at[layer, rows_at(quarter * rows, rows), :]
            else:
                target = outs[0].at[layer, :, rows_at(quarter * width, width)]
            parts.append((copies.start(source.at[part], held.at[len(parts)]), target))
    leaving = []
    for i, (copy, target) in enumerate(parts):
        copy.wait()
        high[i] = held[i].astype(F32)
        leaving.append(copies.start(high.at[i], target))
    return leaving


def norm(values):
    center = jnp.mean(values, axis=-1, keepdims=True)
    offsets = values - center
    inverse = lax.rsqrt(jnp.mean(offsets * offsets, axis=-1, keepdims=True) + 1e-05)
    return offsets * inverse, inverse


def norm_back(upstream, unit, inverse, gain):
    scaled = upstream * gain
    center = jnp.mean(scaled, axis=-1, keepdims=True)
    along = jnp.mean(scaled * unit, axis=-1, keepdims=True)
    return inverse * (scaled - center - unit * along)


def gelu_both(v):
    scale = math.sqrt(2.0 / math.pi)
    square = v * v
    half = 0.5 + 0.5 * jnp.tanh(v * (scale + (scale * 0.044715) * square))
    spread = (2.0 * half) * (1.0 - half)
    return v * half, half + (v * spread) * (scale + (3.0 * scale * 0.044715) * square)


def mix_forward(rows, hid, seq, gain, shift, real, imag, outs):
    unit, inverse, normed_low = outs
    hid_cos, hid_sin = hid[0](), hid[1]()

    @row_steps(rows.shape[0])
    def _(at):
        real[at, :] = dot(rows[at, :], hid_cos[...]).astype(BF16)
        imag[at, :] = dot(rows[at, :], hid_sin[...]).astype(BF16)

    seq_cos, seq_sin = seq[0](), seq[1]()

    @row_steps(rows.shape[0])
    def _(at):
        mixed = dot(seq_cos[at, :], real[...]) - dot(seq_sin[at, :], imag[...])
        unit_rows, inverse_rows = norm(rows[at, :].astype(F32) + mixed)
        unit.buffer[at, :] = unit_rows
        inverse[at, :] = inverse_rows
        normed_low.buffer[at, :] = (unit_rows * gain[...] + shift[...]).astype(BF16)
        normed_low.push(at)
        unit.push(at)


def first_mix_kernel(numbers, boundary, received, hid_cos, hid_sin, cos_tiles, sin_tiles, gain, shift, *refs):
    seq_cos, seq_sin = refs[0:2]
    outs, (rows, real, imag, copies) = refs[2:5], refs[5:]
    chosen = choose(copies, boundary.at[0, pl.ds(0, rows.shape[0])], received, rows)
    cos_tiles, sin_tiles = cos_tiles(), sin_tiles()
    base = cos_tiles.shape[1]
    slots = seq_cos.buffer.shape[0] // base
    for i in range(slots):
        for j in range(slots):
            window = (pl.ds(i * base, base), pl.ds(j * base, base))
            number = numbers[i * slots + j]
            seq_cos.buffer[window] = cos_tiles[number]
            seq_sin.buffer[window] = sin_tiles[number]
    seq_cos.push()
    seq_sin.push()
    seq = (lambda: seq_cos.buffer, lambda: seq_sin.buffer)
    chosen.wait()
    mix_forward(rows, (hid_cos, hid_sin), seq, gain, shift, real, imag, outs)


def expand_kernel(layer, by_permutes, n_sources, normed, other_normed, b_in, *refs):
    sources, (hidden, slope, whole, copies) = refs[:n_sources], refs[n_sources:]
    scratch = whole.buffer
    loaded = load_in(layer, sources, scratch, copies)
    spot = Spot(by_permutes)
    width = scratch.shape[2]
    count = normed.buffer.shape[0]
    for pair in range(2):
        biases = [b_in[:, rows_at(spot.block(2 * pair + i) * (width // 2), width // 2)] for i in range(2)]
        bias = jnp.concatenate(biases, axis=1)
        for copy in loaded[pair]:
            copy.wait()
        whole.push(pair)
        for place, rows in enumerate((normed, other_normed)):
            rows = rows()

            @row_steps(count)
            def _(at):
                value, rate = gelu_both(dot(rows[at, :], scratch[pair]) + bias)
                to = pl.ds(place * count + at.start, at.size)
                hidden.buffer[pair, to, :] = value.astype(BF16)
                slope.buffer[pair, to, :] = rate.astype(BF16)

        hidden.push(pair)
        slope.push(pair)


def contract_kernel(layer, n_sources, hidden, *refs):
    sources, (own, other, whole, copies) = refs[:n_sources], refs[n_sources:]
    scratch = whole.buffer
    loaded = load_out(layer, sources, scratch, copies)
    count, width = own.buffer.shape[0], hidden.buffer.shape[2]
    for copy in loaded:
        copy.wait()
    whole.push()
    for place, out in ((1, other), (0, own)):

        @row_steps(count)
        def _(at):
            rows = pl.ds(place * count + at.start, at.size)
            hidden(1)
            held = hidden.buffer
            total = dot(held[0, rows, :], scratch[0:width, :]) + dot(held[1, rows, :], scratch[width:, :])
            out.buffer[at, :] = total.astype(out.buffer.dtype)
            out.push(at)


def second_norm(at, own, received, unit_one, gain_one, shift_one, b_out):
    normed = unit_one[at, :] * gain_one[...] + shift_one[...]
    return norm(normed + (own[at, :] + received[at, :].astype(F32) + b_out[...]))


def middle_kernel(own, received, unit_one, gain_one, shift_one, b_out, gain_two, shift_two, *refs):
    hid, seq, (next_gain, next_shift) = refs[:2], refs[2:4], refs[4:6]
    unit_two, inverse_two = refs[6:8]
    outs, (mid, real, imag, _) = refs[8:11], refs[11:]
    own, received, unit_one = own(), received(), unit_one()

    @row_steps(mid.shape[0])
    def _(at):
        unit, inverse = second_norm(at, own, received, unit_one, gain_one, shift_one, b_out)
        unit_two.buffer[at, :] = unit
        inverse_two[at, :] = inverse
        mid[at, :] = (unit * gain_two[...] + shift_two[...]).astype(BF16)

    unit_two.push()
    mix_forward(mid, hid, seq, next_gain, next_shift, real, imag, outs)


def second_back(at, upstream, unit, inverse, gain, d_second, branch_grad, small):
    grad = norm_back(upstream, unit, inverse, gain[...])
    low = grad.astype(BF16)
    branch_grad.buffer[at, :] = low
    branch_grad.push(at)
    d_second.buffer[at, :] = grad
    d_second.push(at)
    small[0:1, :] += column_sum(low.astype(F32))
    small[1:2, :] += column_sum(upstream * unit)
    small[2:3, :] += column_sum(upstream)


def turn_kernel(own, received, unit_one, gain_one, shift_one, b_out, gain_two, shift_two, *refs):
    boundary, given, out_rows, d_second, branch_grad, small, cotangent, copies = refs
    count = cotangent.shape[0]
    chosen = choose(copies, given, boundary.at[0, pl.ds(count, count)], cotangent)
    own, received, unit_one = own(), received(), unit_one()
    small[...] = jnp.zeros_like(small)
    chosen.wait()

    @row_steps(own.shape[0])
    def _(at):
        unit, inverse = second_norm(at, own, received, unit_one, gain_one, shift_one, b_out)
        out_rows.buffer[at, :] = (unit * gain_two[...] + shift_two[...]).astype(BF16)
        upstream = cotangent[at, :].astype(F32)
        second_back(at, upstream, unit, inverse, gain_two, d_second, branch_grad, small)
        out_rows.push(at)


def grad_out_kernel(by_permutes, hidden_parts, branch_grad, other_grad, *refs):
    outs, (tiles, both, copies) = refs[:-3], refs[-3:]
    spot = Spot(by_permutes)
    count = both.shape[0] // 2
    shard, width = tiles.shape[1:]
    arriving = [copies.start(ref, both.at[pl.ds(i * count, count)]) for i, ref in enumerate((branch_grad, other_grad))]
    for copy in arriving:
        copy.wait()
    leaving = []
    for turn in range(BLOCKS):
        columns = pl.ds((turn % 2) * shard, shard)
        hidden = hidden_parts(1)
        tiles[turn] = dot(hidden[turn // 2, :, columns], both[...], ((0,), (0,))).astype(BF16)
        if not by_permutes:
            leaving.append(copies.start(tiles.at[turn], outs[0].at[pl.ds(turn * shard, shard), :]))
            continue
        rows = outs[0].shape[2]
        apart = spot.block(turn) ^ spot.chip
        for slot in range(BLOCKS):
            source = tiles.at[turn, rows_at(spot.block(slot) * rows, rows), :]
            leaving.append(copies.start(source, outs[slot // 2].at[slot % 2, apart]))
    return leaving


def shrink_kernel(by_permutes, n_outs, branch_grad, other_grad, slope, normed, other_normed, whole_out, whole_in, *refs):
    outs, (b_grad, own, other, tiles, act_grad, both_grads, both_normed, copies) = refs[:n_outs], refs[n_outs:]
    spot = Spot(by_permutes)
    count = both_grads.shape[0] // 2
    width = tiles.shape[2]
    half = width // 2
    arriving = []
    for refs, both in (((branch_grad, other_grad), both_grads), ((normed, other_normed), both_normed)):
        arriving.append([copies.start(ref, both.at[pl.ds(i * count, count)]) for i, ref in enumerate(refs)])
    for copy in arriving[0]:
        copy.wait()
    b_grad[...] = jnp.zeros_like(b_grad)
    leaving = []
    for pair in range(2):
        weights = whole_out(1)[pl.ds(pair * width, width), :]
        rates = slope(1)
        sums = []

        @row_steps(2 * count)
        def _(at):
            grad = dot(both_grads[at, :], weights, ((1,), (1,)))
            low = (grad * rates[pair, at, :].astype(F32)).astype(BF16)
            act_grad[pair, at, :] = low
            sums.append(column_sum(low.astype(F32)))

        total = sum(sums[1:], sums[0])
        for side in range(2):
            block = spot.block(2 * pair + side)
            b_grad[:, rows_at((2 * block + spot.core) * half, half)] = total[:, side * half : (side + 1) * half]
        if pair == 0:
            for copy in arriving[1]:
                copy.wait()

        @row_steps(tiles.shape[1])
        def _(at):
            tiles[pair, at, :] = dot(both_normed[:, at], act_grad[pair], ((0,), (0,))).astype(BF16)

        if not by_permutes:
            leaving.append(copies.start(tiles.at[pair], outs[0].at[:, pl.ds(pair * width, width)]))
            continue
        rows = outs[0].shape[2]
        for side in range(2):
            for chip in range(spot.chips):
                apart = chip ^ spot.chip
                source = tiles.at[pair, pl.ds(chip * rows, rows), pl.ds(side * half, half)]
                leaving.append(copies.start(source, outs[pair].at[side, apart]))
    whole_in = whole_in()
    for place, out in ((1, other), (0, own)):

        @row_steps(count)
        def _(at):
            rows = pl.ds(place * count + at.start, at.size)
            total = dot(act_grad[0, rows, :], whole_in[0], ((1,), (1,)))
            total = total + dot(act_grad[1, rows, :], whole_in[1], ((1,), (1,)))
            out.buffer[at, :] = total.astype(out.buffer.dtype)
            out.push(at)

    return leaving


def unmix(refs, total, mix_grad, real, imag, small, input_grad):
    own, received, d_second, unit_one, inverse_one, gain_one, hid_cos, hid_sin, seq_cos, seq_sin = refs
    own, received, d_second, unit_one = own(), received(), d_second(), unit_one()
    small[...] = jnp.zeros_like(small)

    @row_steps(total.shape[0])
    def _(at):
        upstream = d_second[at, :] + own[at, :] + received[at, :].astype(F32)
        unit = unit_one[at, :]
        grad = norm_back(upstream, unit, inverse_one[at, :], gain_one[...])
        total[at, :] = grad
        mix_grad[at, :] = grad.astype(BF16)
        small[0:1, :] += column_sum(upstream * unit)
        small[1:2, :] += column_sum(upstream)

    seq_cos, seq_sin = seq_cos(), seq_sin()

    @row_steps(total.shape[0])
    def _(at):
        real[at, :] = dot(seq_cos[at, :], mix_grad[...]).astype(BF16)
        imag[at, :] = (-dot(seq_sin[at, :], mix_grad[...])).astype(BF16)

    hid_cos, hid_sin = hid_cos(), hid_sin()

    @row_steps(total.shape[0])
    def _(at):
        grad = dot(real[at, :], hid_cos[...]) + dot(imag[at, :], hid_sin[...])
        input_grad(at, total[at, :] + grad)


def last_kernel(*refs):
    ins, (out_rows, *smalls) = refs[:10], refs[10:17]
    sent, kept, packed, total, mix_grad, real, imag, small, _ = refs[17:]
    is_first = lax.axis_index("section") % 2 == 0
    rows = out_rows()

    def input_grad(at, values):
        low = values.astype(BF16)
        sent.buffer[at, :] = jnp.where(is_first, rows[at, :], low)
        kept.buffer[at, :] = jnp.where(is_first, low, rows[at, :])
        sent.push(at)
        kept.push(at)

    unmix(ins, total, mix_grad, real, imag, small, input_grad)
    width = packed.shape[1]
    packed[...] = jnp.zeros_like(packed)
    for layer in range(2):
        b_grad, sums_two = smalls[3 * layer : 3 * layer + 2]
        sums_one = smalls[3 * layer + 2] if layer else small
        at = layer * (packed.shape[0] // 2)
        sums = (sums_two[0:1], sums_one[0:1], sums_one[1:2], sums_two[1:2], sums_two[2:3])
        for vector in (b_grad[...],) + sums:
            for i in range(vector.shape[1] // width):
                packed[at : at + 1, :] = vector[:, i * width : (i + 1) * width].astype(packed.dtype)
                at += 1


def finish_kernel(kept, back, result, held, high, copies):
    layer = lax.axis_index("section") % 2
    count = held.shape[1]
    arriving = [copies.start(ref, held.at[i]) for i, ref in enumerate((kept, back))]
    leaving = []
    for i, block in enumerate((layer, 1 - layer)):
        arriving[i].wait()
        high[i] = held[i].astype(F32)
        leaving.append(copies.start(high.at[i], result.at[0, rows_at(block * count, count)]))
    return leaving


def relay_kernel(*refs):
    ins, (unit_two, inverse_two, gain_two) = refs[:10], refs[10:13]
    small, d_second, branch_grad, small_two, total, mix_grad, real, imag, _ = refs[13:]
    small_two[...] = jnp.zeros_like(small_two)

    def input_grad(at, values):
        upstream = values.astype(BF16).astype(F32)
        unit = unit_two()[at, :]
        second_back(at, upstream, unit, inverse_two[at, :], gain_two, d_second, branch_grad, small_two)

    unmix(ins, total, mix_grad, real, imag, small, input_grad)


def body(boundary, bucket_ids, w_in, b_in, w_out, b_out, gain_one, shift_one, gain_two, shift_two):
    place = Place()
    Order.begin()
    layers = w_in.shape[0]
    micro_count = bucket_ids.shape[1]
    feat_width = boundary.shape[2]
    ff_width = w_in.shape[2]
    slab_len = boundary.shape[1] // micro_count
    slots = bucket_ids.shape[2]
    base_len = slab_len // slots
    half_block = ff_width // (2 * BLOCKS)
    by_permutes = place.n_section == 4 and place.chips == 4
    last = layers - 1

    bucket_row = bucket_ids[place.section // 2, place.section % 2]
    half_bias = lax.dynamic_index_in_dim(
        b_in.reshape(layers, BLOCKS, 2, half_block), place.core, 2, keepdims=False
    ).reshape(layers, -1)

    block = (slab_len, feat_width)
    both = (2 * slab_len, feat_width)
    wide_block = (2, 2 * slab_len, ff_width // 4)
    whole_in_shape = (2, feat_width, ff_width // 4)
    whole_out_shape = (ff_width // 2, feat_width)
    column = (VMEM, (slab_len, 1), F32)
    sums_shape = (VMEM, (8, feat_width), F32)
    mix_outs = [(EARLY, block, F32), column, (EARLY, block, BF16)]
    hid = [(LATE, jnp.asarray(table.astype(BF16))) for table in dft_tables(feat_width)]

    def late(*arrays):
        return [(LATE, array) for array in arrays]

    def plain(*arrays):
        return [(HBM, array) for array in arrays]

    def param(array, layer):
        return (VMEM, array[layer][None])

    shard_rows, piece_rows = w_in.shape[1], w_out.shape[1] // BLOCKS
    prepared = [(HBM, block, BF16)]
    if by_permutes:
        prepared += [(HBM, (layers, shard_rows, ff_width // 2), BF16)]
        prepared += [(HBM, (piece_rows, feat_width), BF16)] * layers
    given, *prepared = call(
        partial(prepare_kernel, layers, by_permutes),
        plain(boundary, w_in, w_out),
        prepared,
        [
            (block, BF16),
            ((layers, shard_rows, ff_width // 2), BF16),
            ((layers, piece_rows, feat_width), BF16),
        ],
        "prepare",
        spare=54 * 2**20,
    )
    sources_in, sources_out = [None] * layers, [None] * layers
    if by_permutes:
        for_other, out_zero_piece, out_one_piece = prepared
        in_zero, out_zero, in_one, out_one = (
            Gather(place, name + str(layer), w, None, layer, by_rows)
            for layer in range(layers)
            for name, w, by_rows in (("in", w_in, False), ("out", w_out, True))
        )
        other_rows = place.swap_core(for_other)
        received = place.swap_layer(given)
        in_zero.other_rows = in_one.other_rows = other_rows
        piece = in_zero.join(other_rows)
        in_zero.shift(piece)
        out_zero_moved = place.along_z(tie(out_zero_piece, piece), 1)
        pieces_one = in_one.join(other_rows, out_one_piece)
        Order.wait(received)
        in_zero.one()
        out_zero_pair = pack("pair_out0", [out_zero_piece, out_zero_moved])
        out_zero.moved = [out_zero_moved, place.along_z(out_zero_pair, 2)]
        moved_one = place.along_z(tie(pieces_one, Order.token), 1)
    else:
        received = place.swap_layer(given)
        for layer in range(layers):
            whole_in, whole_out = (
                lax.all_gather(w[layer], "dp", axis=0, tiled=True) for w in (w_in, w_out)
            )
            whole_in = whole_in.reshape(feat_width, BLOCKS, 2, half_block)
            whole_out = whole_out.reshape(BLOCKS, 2, half_block, feat_width)
            whole_in = lax.dynamic_index_in_dim(whole_in, place.core, 2, keepdims=False)
            whole_out = lax.dynamic_index_in_dim(whole_out, place.core, 1, keepdims=False)
            sources_in[layer] = [whole_in.reshape(feat_width, -1)]
            sources_out[layer] = [whole_out.reshape(-1, feat_width)]

    numbers = tile_numbers(bucket_row, slots).reshape(-1)
    tiles = [(LATE, jnp.asarray(table)) for table in sequence_tiles(base_len)]
    seq_cos, seq_sin, *mixed = call(
        first_mix_kernel,
        [(SMEM, numbers)]
        + plain(boundary, received)
        + hid
        + tiles
        + [param(gain_one, 0), param(shift_one, 0)],
        [(EARLY, (slab_len, slab_len), BF16)] * 2 + mix_outs,
        [(block, BF16)] * 3,
        "first_mix",
    )
    tables = hid + late(seq_cos, seq_sin)

    both_pairs, all_rows = pl.ds(0, 2), pl.ds(0, 2 * slab_len)
    steps = slab_len // ROW_STEP
    row_parts = [
        (both_pairs, pl.ds(slab_len * place_ + i * ROW_STEP, ROW_STEP))
        for place_ in (1, 0)
        for i in range(steps)
    ]
    block_parts = [
        (pair, all_rows, pl.ds(side * half_block, half_block)) for pair in range(2) for side in range(2)
    ]
    pair_parts = [(pl.ds(pair, 1),) for pair in range(2)]
    half_parts = [(pl.ds(pair * 2 * half_block, 2 * half_block),) for pair in range(2)]

    saved, wholes_in, wholes_out = [], [], []
    for layer in range(layers):
        unit_one, inverse_one, normed = mixed
        if by_permutes and layer == 0:
            mark = Order.mark(in_zero.from_one, in_zero.from_two)
            in_zero.two(mark)
            other_normed = place.swap_core(tie(normed, mark))
            out_zero.one()
            pair_in, pair_out = pairs(pieces_one, moved_one)
            in_one.moved = [(pair_in, 1, 1), place.along_z(pair_in, 2)]
            sources_in[0] = in_zero.sources()
        else:
            other_normed = place.swap_core(normed)
        if by_permutes and layer == 1:
            mark = Order.mark(in_one.far, out_one.from_one, out_one.from_two)
            out_one.two(mark)
            sources_in[1] = in_one.sources()
        hidden, slope, whole_in = call(
            partial(expand_kernel, layer, by_permutes, len(sources_in[layer])),
            late(normed, other_normed)
            + [(VMEM, half_bias[layer][None])]
            + plain(*sources_in[layer]),
            [(EARLY, wide_block, BF16), (EARLY, wide_block, BF16), (EARLY, whole_in_shape, BF16)],
            [],
            "expand",
        )
        if by_permutes and layer == 0:
            mark = Order.mark(out_zero.from_one, out_zero.from_two)
            out_zero.two(mark)
            in_one.one()
            out_one.moved = [(pair_out, 1, 1), place.along_z(tie(pair_out, in_one.along), 2)]
            sources_out[0] = out_zero.sources()
        if by_permutes and layer == 1:
            sources_out[1] = out_one.sources()
        own_part, other_part, whole_out = call(
            partial(contract_kernel, layer, len(sources_out[layer])),
            [(LATE, hidden, row_parts)] + plain(*sources_out[layer]),
            [(EARLY, block, F32), (EARLY, block, BF16), (EARLY, whole_out_shape, BF16)],
            [],
            "contract",
        )
        from_other = place.swap_core(other_part)
        if by_permutes and layer == 0:
            mark = Order.mark(in_one.from_one, in_one.from_two)
            in_one.two(mark)
            out_one.one()
        wholes_in.append(whole_in)
        wholes_out.append(whole_out)
        common = late(own_part, from_other, unit_one) + [
            param(p, layer) for p in (gain_one, shift_one, b_out, gain_two, shift_two)
        ]
        kept = [unit_one, inverse_one, normed, other_normed, hidden, slope]
        if layer < last:
            unit_two, inverse_two, *mixed = call(
                middle_kernel,
                common + tables + [param(gain_one, layer + 1), param(shift_one, layer + 1)],
                [(EARLY, block, F32), column] + mix_outs,
                [(block, BF16), (block, BF16), (block, BF16)],
                "middle",
            )
            kept += [unit_two, inverse_two]
        saved.append(kept)

    out_rows, d_second, branch_grad, sums_two = call(
        turn_kernel,
        common + plain(boundary, received),
        [(EARLY, block, BF16), (EARLY, block, F32), (EARLY, block, BF16), sums_shape],
        [(block, BF16)],
        "turn",
    )

    if by_permutes:
        piece_out = (2, place.chips, w_out.shape[1] // BLOCKS, feat_width)
        piece_in = (2, place.chips, 2 * w_in.shape[1], half_block)
        grad_outs = {True: [(HBM, piece_out, BF16)] * 2, False: [(HBM, piece_in, BF16)] * 2}
    else:
        grad_outs = {
            True: [(HBM, (ff_width // 2, feat_width), BF16)],
            False: [(HBM, (feat_width, ff_width // 2), BF16)],
        }
    n_outs = len(grad_outs[True])
    grads, smalls, running = {}, {}, []

    def reduce_grad(pieces, layer, by_rows):
        name = ("out" if by_rows else "in") + str(layer)
        if by_permutes:
            grads[layer, by_rows] = Scatter(place, name, *pieces, by_rows)
            running.append(grads[layer, by_rows])
            return
        (half,) = pieces
        if by_rows:
            whole = jnp.zeros((BLOCKS, 2, half_block, feat_width), BF16)
            half = half.reshape(BLOCKS, 1, half_block, feat_width)
            whole = lax.dynamic_update_slice_in_dim(whole, half, place.core, 1)
            whole = whole.reshape(ff_width, feat_width)
        else:
            whole = jnp.zeros((feat_width, BLOCKS, 2, half_block), BF16)
            half = half.reshape(feat_width, BLOCKS, 1, half_block)
            whole = lax.dynamic_update_slice_in_dim(whole, half, place.core, 2)
            whole = whole.reshape(feat_width, ff_width)
        part = lax.psum_scatter(whole, "dp", scatter_dimension=0, tiled=True)
        grads[layer, by_rows] = lax.psum(part, "section").astype(F32)

    for layer in reversed(range(layers)):
        unit_one, inverse_one, normed, other_normed, hidden, slope = saved[layer][:6]
        other_grad = place.swap_core(branch_grad)
        if by_permutes and layer == 0:
            running[0].two()
            running[1].two()
        pieces = call(
            partial(grad_out_kernel, by_permutes),
            [(LATE, hidden, block_parts)] + plain(branch_grad, other_grad),
            grad_outs[True],
            [((BLOCKS, half_block, feat_width), BF16), (both, BF16)],
            "grad_out",
        )
        reduce_grad(pieces, layer, True)
        if by_permutes and layer == 0:
            running[0].three()
        *pieces, b_grad, own_part, other_part = call(
            partial(shrink_kernel, by_permutes, n_outs),
            plain(branch_grad, other_grad)
            + [(LATE, slope, pair_parts)]
            + plain(normed, other_normed)
            + [(LATE, wholes_out[layer], half_parts)]
            + late(wholes_in[layer]),
            grad_outs[False]
            + [(VMEM, (1, ff_width), F32), (EARLY, block, F32), (EARLY, block, BF16)],
            [
                ((2, feat_width, ff_width // 4), BF16),
                (wide_block, BF16),
                (both, BF16),
                (both, BF16),
            ],
            "shrink",
        )
        from_other = place.swap_core(other_part)
        reduce_grad(pieces, layer, False)
        if by_permutes and layer == last:
            Order.mark(running[0].from_one)
        if by_permutes and layer == 0:
            running[0].neighbour()
            running[2].two()
            running[1].three()
        ins = (
            late(own_part, from_other, d_second, unit_one)
            + [(VMEM, inverse_one), param(gain_one, layer)]
            + tables
        )
        work = [(block, F32), (block, BF16), (block, BF16), (block, BF16)]
        smalls[layer] = [b_grad, sums_two]
        if layer > 0:
            below_unit, below_inverse = saved[layer - 1][6:8]
            sums_one, d_second, branch_grad, sums_two = call(
                relay_kernel,
                ins + late(below_unit) + [(VMEM, below_inverse), param(gain_two, layer - 1)],
                [sums_shape, (EARLY, block, F32), (EARLY, block, BF16), sums_shape],
                work,
                "relay",
            )
            smalls[layer].append(sums_one)
    vectors = smalls[0] + [smalls[1][2]] + smalls[1]
    small_type = BF16 if by_permutes else F32
    sent, kept_rows, packed = call(
        last_kernel,
        ins + late(out_rows) + [(VMEM, vector) for vector in vectors],
        [(EARLY, block, BF16), (EARLY, block, BF16), (VMEM, (64, half_block), small_type)],
        work + [((8, feat_width), F32)],
        "last",
    )

    def finish():
        return call(
            finish_kernel,
            plain(kept_rows, back),
            [(HBM, (1, 2 * slab_len, feat_width), F32)],
            [((2,) + block, BF16), ((2,) + block, F32)],
            "finish",
        )

    if by_permutes:

        def share(mine):
            return [place.plane_one(mine), place.plane_two(mine)]

        out_last, in_last, out_first, in_first = running
        in_first.small = [(packed, pl.ds(0, packed.shape[0]))]
        in_first.two()
        out_last.four()
        Order.mark(out_first.from_two)
        in_last.neighbour()
        out_first.three()
        in_first.three()
        back = place.swap_layer(tie(sent, Order.token))
        in_last.four()
        out_first.neighbour()
        in_first.neighbour()
        mine = join("join_rest", [in_last, out_last])
        rest = share(mine)
        (result,) = finish()
        out_first.four()
        in_first.four()
        rest.append(place.plane_two(tie(rest[0], Order.token)))
        Order.wait(rest[1])
        last_mine = join("join_last", [in_first, out_first])
        last_rest = share(last_mine)
        groups = [[(last, False), (last, True)], [(0, False), (0, True)]]
        unit = (shard_rows, ff_width // BLOCKS)

        def collect(group, arrays, started):
            held = ((4 * len(group),) + unit,)
            return call(
                partial(collect_kernel, group, len(started)),
                plain(*arrays, *started),
                [(HBM, w_in.shape, F32), (HBM, w_out.shape, F32)],
                [held + (BF16,), held + (F32,)],
                "collect",
                aliases={4: 0, 5: 1} if started else None,
            )

        started = collect(groups[0], [mine] + rest, ())
        last_rest.append(place.plane_two(tie(last_rest[0], Order.token)))
        at = 2 * shard_rows
        packed = last_mine[at:].astype(F32) + last_rest[0][at:].astype(F32)
        packed = packed.astype(BF16)
        packed = packed.astype(F32) + place.swap_core(tie(packed, Order.token)).astype(F32)
        packed = packed.reshape(-1, 2, half_block).transpose(1, 0, 2).reshape(-1, half_block)
        grad_in, grad_out = collect(groups[1], [last_mine] + last_rest, tuple(started))
    else:
        back = place.swap_layer(sent)
        grad_in, grad_out = (
            jnp.stack([grads[layer, by_rows] for layer in range(layers)])
            for by_rows in (False, True)
        )
        packed = lax.psum(packed, AXES)
        (result,) = finish()
    b_part, part = ff_width // place.n_dp, feat_width // place.n_dp
    flat = packed.reshape(layers, -1)
    small_out = [lax.dynamic_slice_in_dim(flat, place.dp * b_part, b_part, 1)]
    sums = flat[:, ff_width : ff_width + 5 * feat_width].reshape(layers, 5, feat_width)
    sums = lax.dynamic_slice_in_dim(sums, place.dp * part, part, 2)
    small_out += [sums[:, i] for i in range(5)]
    return (result, grad_in, small_out[0], grad_out, *small_out[1:])


def solution(mesh):
    return jax.shard_map(
        body,
        mesh=mesh,
        in_specs=(
            P("section", "dp", None),
            P(None, "dp", None),
            P(None, "dp", None),
            P(),
            P(None, "dp", None),
            P(),
            P(),
            P(),
            P(),
            P(),
        ),
        out_specs=(
            P("section", "dp", None),
            P(None, "dp", None),
            P(None, "dp"),
            P(None, "dp", None),
            P(None, "dp"),
            P(None, "dp"),
            P(None, "dp"),
            P(None, "dp"),
            P(None, "dp"),
        ),
        check_vma=False,
    )
```

```python
from functools import partial
import math

import jax
import jax.numpy as jnp
import numpy as np
from jax import lax
from jax.experimental import pallas as pl
from jax.experimental.pallas import tpu as pltpu
from jax.sharding import PartitionSpec as P

AXES = ("section", "dp")
F32 = jnp.float32
BF16 = jnp.bfloat16
BLOCKS = 4
FORWARD_COST, BACKWARD_COST = 10**10, 10**10
ROW_STEP = 256

VMEM = pl.BlockSpec(memory_space=pltpu.VMEM)
SMEM = pl.BlockSpec(memory_space=pltpu.SMEM)
HBM = pl.BlockSpec(memory_space=pltpu.HBM)
LATE, EARLY = "late", "early"


class Place:
    def __init__(self):
        self.n_section = lax.axis_size("section")
        self.n_dp = lax.axis_size("dp")
        self.chips = self.n_dp // 2
        self.section = lax.axis_index("section")
        self.dp = lax.axis_index("dp")
        self.core = self.dp % 2

    def permute(self, value, target):
        pairs = []
        for section in range(self.n_section):
            for chip in range(self.chips):
                for core in range(2):
                    to_section, to_chip, to_core = target(section, chip, core)
                    source = section * self.n_dp + chip * 2 + core
                    pairs.append((source, to_section * self.n_dp + to_chip * 2 + to_core))
        return lax.ppermute(value, AXES, pairs)

    def swap_core(self, value):
        return self.permute(value, lambda s, z, c: (s, z, 1 - c))

    def swap_layer(self, value):
        return self.permute(value, lambda s, z, c: (s ^ 1, z, c))

    def plane_one(self, value):
        return self.permute(value, lambda s, z, c: (s ^ (1 + c), z, c))

    def plane_two(self, value):
        return self.permute(value, lambda s, z, c: (s ^ (2 - c), z, c))

    def along_z(self, value, flip):
        return self.permute(value, lambda s, z, c: (s, z ^ flip, c))


class Spot:
    def __init__(self, by_permutes=True):
        dp = lax.axis_index("dp")
        self.core = dp % 2
        if by_permutes:
            self.section, self.chip = lax.axis_index("section"), dp // 2
            self.chips = lax.axis_size("dp") // 2
            self.held = (1 + self.core, 3, 2 - self.core, 0)
        else:
            self.section, self.held = 0, (0, 1, 2, 3)

    def block(self, turn):
        return self.section ^ self.held[turn]

    def turn_of(self, block):
        flip = block ^ self.section
        side = jnp.where(flip == self.held[0], 0, 2)
        return jnp.where(flip == 3, 1, jnp.where(flip == 0, 3, side))


def dft_tables(length):
    positions = np.arange(length)
    angles = (positions[:, None] * positions[None, :] % length) * (2.0 * math.pi) / length
    scaling = 1.0 / math.sqrt(length)
    return (np.cos(angles) * scaling, np.sin(angles) * scaling)


def sequence_tiles(base_len):
    cos_tiles, sin_tiles = [], []
    for parts in (1, 2, 4):
        cos_table, sin_table = dft_tables(parts * base_len)
        for i in range(parts):
            for j in range(parts):
                window = (
                    slice(i * base_len, (i + 1) * base_len),
                    slice(j * base_len, (j + 1) * base_len),
                )
                cos_tiles.append(cos_table[window])
                sin_tiles.append(sin_table[window])
    cos_tiles.append(np.zeros((base_len, base_len)))
    sin_tiles.append(np.zeros((base_len, base_len)))
    return np.stack(cos_tiles).astype(BF16), np.stack(sin_tiles).astype(BF16)


def tile_numbers(bucket_row, slots):
    parts = jnp.where(bucket_row < 3, 1 << jnp.minimum(bucket_row, 2), 0)
    ends = jnp.cumsum(parts)
    where = jnp.arange(slots, dtype=jnp.int32)
    segment = jnp.sum((where[:, None] >= ends[None, :]).astype(jnp.int32), axis=1)
    one_hot = (segment[:, None] == jnp.arange(slots)[None, :]).astype(jnp.int32)
    start = jnp.sum(one_hot * (ends - parts)[None, :], axis=1)
    size = jnp.sum(one_hot * parts[None, :], axis=1)
    first = jnp.where(size == 1, 0, jnp.where(size == 2, 1, 5))
    place = where - start
    numbers = first[:, None] + place[:, None] * size[:, None] + place[None, :]
    return jnp.where(segment[:, None] == segment[None, :], numbers, 21)


def rows_at(start, size):
    return pl.ds(pl.multiple_of(start, size), size)


def dot(left, right, dims=((1,), (0,))):
    return lax.dot_general(left, right, (dims, ((), ())), preferred_element_type=F32)


def row_steps(count, step=ROW_STEP):
    step = step if count % step == 0 else count

    def run(function):
        for i in range(count // step):
            function(pl.ds(i * step, step))

    return run


def column_sum(values):
    return jnp.sum(values, axis=0, keepdims=True)


class Copies:
    def __init__(self, sems):
        self.sems, self.count = sems, 0

    def start(self, source, target):
        copy = pltpu.make_async_copy(source, target, self.sems.at[self.count])
        copy.start()
        self.count += 1
        return copy


class Late:
    def __init__(self, ref):
        self.buffer = ref

    def __call__(self, parts=None):
        return self.buffer


class Early:
    def __init__(self, ref):
        self.buffer, self.leaving = ref, []

    def push(self, part=None):
        pass


def tie(value, *others):
    return lax.optimization_barrier((value,) + others)[0]


class Order:
    token = None
    cost = FORWARD_COST

    @classmethod
    def begin(cls):
        cls.token = jnp.zeros((8, 128), F32)
        cls.cost = FORWARD_COST

    @classmethod
    def wait(cls, *arrays):
        cls.token = tie(cls.token, *arrays)

    @classmethod
    def mark(cls, *arrays):
        cls.wait(*arrays)
        call(lambda *refs: None, [], [], [], "mark")
        return cls.token


def call(kernel, ins, outs, scratch, name, aliases=None, spare=4 * 2**20):
    buffers = []
    n_ins, n_outs, n_scratch = len(ins), len(outs), len(scratch)
    counts = []

    def run(*refs):
        given, made = list(refs[:n_ins]), list(refs[n_ins + 1 :][:n_outs])
        token_out, refs = refs[n_ins + 1 + n_outs], refs[n_ins + 2 + n_outs :]
        own, held, copies = refs[:n_scratch], list(refs[n_scratch:-1]), Copies(refs[-1])
        late = []
        for i, entry in enumerate(ins):
            if entry[0] is LATE:
                given[i] = Late(given[i])
                late.append(given[i])
        early = []
        for i, out in enumerate(outs):
            if out[0] is EARLY:
                made[i] = Early(made[i])
                early.append(made[i])
        leaving = kernel(*given, *made, *own, copies) or []
        token_out[...] = jnp.zeros_like(token_out)
        for value in late:
            value()
        for copy in leaving + [copy for out in early for copy in out.leaving]:
            copy.wait()
        counts.append(copies.count)

    def spec_of(spec):
        return VMEM if spec in (LATE, EARLY) else spec

    held = list(scratch) + [(a[1].shape, a[1].dtype) for a in ins if a[0] in (LATE, VMEM)]
    held += [out[1:] for out in outs if out[0] in (EARLY, VMEM)]
    needed = sum(math.prod(shape) * jnp.dtype(dtype).itemsize for shape, dtype in held)

    def build(sems):
        return pl.pallas_call(
            run,
            in_specs=[spec_of(entry[0]) for entry in ins] + [HBM],
            out_specs=tuple(spec_of(out[0]) for out in outs) + (VMEM,),
            out_shape=tuple(jax.ShapeDtypeStruct(*out[1:]) for out in outs)
            + (jax.ShapeDtypeStruct((8, 128), F32),),
            scratch_shapes=[pltpu.VMEM(*s) for s in scratch]
            + buffers
            + [pltpu.SemaphoreType.DMA((sems,))],
            compiler_params=pltpu.CompilerParams(vmem_limit_bytes=needed + spare),
            cost_estimate=pl.CostEstimate(flops=Order.cost, bytes_accessed=1000, transcendentals=0),
            input_output_aliases=aliases or {},
            name=name,
        )

    arrays = [entry[1] for entry in ins] + [Order.token]
    jax.eval_shape(build(96), *arrays)
    *made, Order.token = build(max(counts[-1], 1))(*arrays)
    return made


def move(name, terms, unit, outs, targets, extra=None):
    jobs = [
        ([(array, indices[i]) for array, indices in terms], unit, target)
        for i, target in enumerate(targets)
    ]
    if extra is not None:
        jobs.append(extra)
    given = []
    for job_terms, _, _ in jobs:
        for array, _ in job_terms:
            if not any(array is other for other in given):
                given.append(array)

    def run(*refs):
        ins, made = refs[: len(given)], refs[len(given) : len(given) + len(outs)]

        def at(index):
            index = index(Spot()) if callable(index) else index
            return index if index else Ellipsis

        for job_terms, _, (number, target) in jobs:
            parts = [
                next(ref for ref, other in zip(ins, given) if other is array)[at(index)]
                for array, index in job_terms
            ]
            if len(parts) > 1:
                parts = [sum((part.astype(F32) for part in parts[1:]), parts[0].astype(F32))]
            made[number][at(target)] = parts[0].astype(BF16)

    return call(
        run,
        [(VMEM, array) for array in given],
        [(VMEM, shape, BF16) for shape in outs],
        [],
        name,
    )


def pack(name, entries):
    entries = [entry if isinstance(entry, tuple) else (entry, None, None) for entry in entries]
    unit = entries[0][0].shape[-2:]
    sizes = [
        count or (1 if len(array.shape) == 2 else array.shape[0]) for array, _, count in entries
    ]
    starts = [sum(sizes[:i]) for i in range(len(sizes))]

    def run(*refs):
        out = refs[len(entries)]
        for i, (ref, (_, start, count)) in enumerate(zip(refs, entries)):
            source = ref[...] if start is None else ref[pl.ds(start, count)]
            out[pl.ds(starts[i], sizes[i])] = source.reshape((sizes[i],) + unit)

    whole = ((sum(sizes),) + unit, entries[0][0].dtype)
    (packed,) = call(
        run, [(VMEM, entry[0]) for entry in entries], [(VMEM,) + whole], [], name
    )
    return packed


def choose(copies, first, second, buffer):
    is_first = lax.axis_index("section") % 2 == 0
    sem = copies.sems.at[copies.count]
    copies.count += 1
    pair = [pltpu.make_async_copy(source, buffer, sem) for source in (first, second)]
    pl.when(is_first)(pair[0].start)
    pl.when(jnp.logical_not(is_first))(pair[1].start)
    return pair[0]


def prepare_kernel(layers, by_permutes, boundary, w_in, w_out, given, *refs):
    outs, (slab, rows, pieces, copies) = refs[: -4], refs[-4:]
    count = slab.shape[0]
    first, second = (boundary.at[0, pl.ds(i * count, count)] for i in range(2))
    slab_copy = choose(copies, second, first, slab)
    leaving = []
    if by_permutes:
        other_rows, *out_pieces = outs
        spot = Spot()
        width = w_in.shape[2] // (2 * BLOCKS)
        arriving = []
        for block in range(BLOCKS):
            source = w_in.at[:, :, rows_at((2 * block + 1 - spot.core) * width, width)]
            arriving.append(copies.start(source, rows.at[:, :, pl.ds(block * width, width)]))
        high = w_out.shape[1] // BLOCKS
        for layer in range(layers):
            source = w_out.at[layer, rows_at(spot.section * high, high)]
            arriving.append(copies.start(source, pieces.at[layer]))
        for copy in arriving[:BLOCKS]:
            copy.wait()
        leaving.append(copies.start(rows, other_rows))
        for layer in range(layers):
            arriving[BLOCKS + layer].wait()
            leaving.append(copies.start(pieces.at[layer], out_pieces[layer]))
    slab_copy.wait()
    leaving.append(copies.start(slab, given))
    return leaving


class Gather:
    def __init__(self, place, name, w, other_rows, layer, by_rows):
        self.place, self.name, self.by_rows = place, name, by_rows
        self.w, self.other_rows, self.layer = w, other_rows, layer

    def join(self, halves, out_piece=None):
        layer, rows, width = self.layer, self.w.shape[1], self.w.shape[2] // (2 * BLOCKS)
        beside = out_piece is not None
        shape = (2, rows, 2 * width) if beside else (2 * rows, width)

        def run(w, other, *refs):
            out_ref, (out, held, copies) = refs[:-3], refs[-3:]
            spot = Spot()
            own = w.at[layer, :, rows_at((2 * spot.section + spot.core) * width, width)]
            other = other.at[layer, :, rows_at(spot.section * width, width)]
            arriving = []
            for source, core in ((own, spot.core), (other, 1 - spot.core)):
                target = held.at[rows_at(core * rows, rows)]
                if beside:
                    target = held.at[0, :, rows_at(core * width, width)]
                arriving.append(copies.start(source, target))
            if beside:
                arriving.append(copies.start(out_ref[0], held.at[1]))
            for copy in arriving:
                copy.wait()
            return [copies.start(held, out)]

        (piece,) = call(
            run,
            [(HBM, self.w), (HBM, halves)] + ([(HBM, out_piece)] if beside else []),
            [(HBM, shape, BF16)],
            [(shape, BF16)],
            "piece_" + self.name,
        )
        return piece

    def shift(self, piece):
        self.moved = [self.place.along_z(piece, flip) for flip in (1, 2, 3)]

    def one(self):
        self.along = pack("along_" + self.name, self.moved)
        self.from_one = self.place.plane_one(self.along)
        self.from_two = self.place.plane_two(self.along)

    def two(self, *others):
        self.far = self.place.plane_two(tie(self.from_one, *others))

    def sources(self):
        moved = [self.along, self.from_one, self.from_two, self.far]
        return [self.w] + moved if self.by_rows else [self.w, self.other_rows] + moved


def pairs(own, moved):
    _, rows, width = own.shape

    def run(own, moved, pair_in, pair_out, copies):
        for i, ref in enumerate((own, moved)):
            for core in range(2):
                half = pl.ds(core * (width // 2), width // 2)
                pair_in[i, pl.ds(core * rows, rows)] = ref[0, :, half]
            pair_out[i] = ref[1]

    shapes = [((2, 2 * rows, width // 2), BF16), ((2, rows, width), BF16)]
    return call(run, [(VMEM, own), (VMEM, moved)], [(VMEM,) + s for s in shapes], [], "pairs")


def load_in(layer, sources, scratch, copies):
    if len(sources) == 1:
        width = scratch.shape[2]
        return [[copies.start(sources[0].at[:, pl.ds(i * width, width)], scratch.at[i])] for i in range(2)]
    own, other, along, one, two, far = sources
    spot = Spot()
    rows, width = own.shape[1], along.shape[2]
    pairs = []
    for pair in range(2):
        started = []
        for side in range(2):
            turn = 2 * pair + side
            columns = pl.ds(side * width, width)
            block = spot.block(turn)
            source = (one, far, two, along)[turn]
            for apart in range(1, spot.chips):
                chip = spot.chip ^ apart
                target = scratch.at[pair, rows_at(chip * 2 * rows, 2 * rows), columns]
                started.append(copies.start(source.at[apart - 1], target))
            for core, ref, index in (
                (spot.core, own, rows_at((2 * block + spot.core) * width, width)),
                (1 - spot.core, other, rows_at(block * width, width)),
            ):
                target = scratch.at[pair, rows_at((2 * spot.chip + core) * rows, rows), columns]
                started.append(copies.start(ref.at[layer, :, index], target))
        pairs.append(started)
    return pairs


def load_out(layer, sources, scratch, copies):
    if len(sources) == 1:
        return [copies.start(sources[0], scratch)]
    own, along, one, two, far = sources
    spot = Spot()
    shard, rows = own.shape[1], along.shape[1]
    started = []
    for apart in range(spot.chips):
        chip = spot.chip ^ apart
        start = spot.turn_of(chip) * shard
        if apart == 0:
            started.append(copies.start(own.at[layer], scratch.at[rows_at(start, shard), :]))
            continue
        for turn, source in enumerate((one, far, two, along)):
            part = pl.ds(pl.multiple_of(start + spot.block(turn) * rows, rows), rows)
            started.append(copies.start(source.at[apart - 1], scratch.at[part, :]))
    return started


class Scatter:
    def __init__(self, place, name, first, rest, by_rows):
        self.place, self.name, self.rest, self.by_rows = place, name, rest, by_rows
        self.chips, self.unit = rest.shape[1], rest.shape[2:]
        self.from_one = place.plane_one(first)
        self.small = None

    def move(self, stage, terms, sent):
        rows, width = self.unit
        extra, height = None, sent * rows
        if self.small is not None:
            self.small_rows = self.small[0][1].size
            terms_small = [(array, (at,)) for array, at in self.small]
            target = (0, (pl.ds(height, self.small_rows),))
            extra = (terms_small, (self.small_rows, width), target)
            height += self.small_rows
        targets = [(0, (pl.ds(i * rows, rows),)) for i in range(sent)]
        name = stage + "_" + self.name
        (made,) = move(name, terms, self.unit, [(height, width)], targets, extra)
        return made

    def heard(self, sent, received, count):
        if self.small is not None:
            at = pl.ds(count * self.unit[0], self.small_rows)
            self.small = [(sent, at), (received, at)]

    def part(self, i):
        return (pl.ds(i * self.unit[0], self.unit[0]),)

    def two(self):
        terms = [
            (self.rest, [(0, i) for i in range(self.chips)]),
            (self.from_one, [(1, i) for i in range(self.chips)]),
        ]
        second = self.move("two", terms, self.chips)
        self.from_two = self.place.plane_two(second)
        self.heard(second, self.from_two, self.chips)
        return second

    def own_terms(self, aparts):
        return [
            (self.rest, [(1, i) for i in aparts]),
            (self.from_one, [(0, i) for i in aparts]),
            (self.from_two, [self.part(i) for i in aparts]),
        ]

    def three(self):
        pair = self.move("three", self.own_terms([2, 3]), 2)
        self.from_pair = self.place.along_z(pair, 2)
        self.heard(pair, self.from_pair, 2)
        return pair

    def neighbour(self):
        terms = self.own_terms([1]) + [(self.from_pair, [self.part(1)])]
        piece = self.move("next", terms, 1)
        self.from_next = self.place.along_z(piece, 1)
        self.heard(piece, self.from_next, 1)
        return piece

    def four(self):
        if self.by_rows:
            terms = self.own_terms([0]) + [
                (self.from_pair, [self.part(0)]),
                (self.from_next, [self.part(0)]),
            ]
            (self.sum,) = move(
                "four_" + self.name, terms, self.unit, [self.unit], [(0, ())]
            )
            return self.sum
        rows, width = self.unit[0] // 2, self.unit[1]
        parts = [
            lambda spot: (rows_at(spot.core * rows, rows),),
            lambda spot: (rows_at((1 - spot.core) * rows, rows),),
        ]

        def of(head):
            return [lambda spot, part=part: head + part(spot) for part in parts]

        terms = [
            (self.rest, of((1, 0))),
            (self.from_one, of((0, 0))),
            (self.from_two, of(())),
            (self.from_pair, of(())),
            (self.from_next, of(())),
        ]
        targets, extra, height = [(0, ()), (1, (pl.ds(0, rows),))], None, rows
        if self.small is not None:
            height += self.small_rows
            terms_small = [(array, (at,)) for array, at in self.small]
            extra = (terms_small, (self.small_rows, width), (1, (pl.ds(rows, self.small_rows),)))
        self.kept, self.given = move(
            "four_" + self.name, terms, (rows, width), [(rows, width), (height, width)], targets, extra
        )
        self.from_core = self.place.swap_core(self.given)
        return self.kept


def join(name, scatters):
    given = []
    for scatter in scatters:
        given += [scatter.sum] if scatter.by_rows else [scatter.kept, scatter.from_core]
    rows, width = scatters[0].kept.shape
    half, width = width, 2 * width
    with_small = [scatter for scatter in scatters if scatter.small is not None]
    given += [scatter.given for scatter in with_small]
    small_rows = with_small[0].small_rows // 2 if with_small else 0
    count = len(scatters)

    def run(*refs):
        ins, out = list(refs[: len(given)]), refs[len(given)]
        spot = Spot()

        def small(ref, at):
            for i in range(2):
                part = ref[pl.ds(rows + i * small_rows, small_rows)]
                out[pl.ds(at, small_rows), pl.ds(i * half, half)] = part

        for i, scatter in enumerate(scatters):
            part = pl.ds(i * rows, rows)
            if scatter.by_rows:
                out[part] = ins.pop(0)[...]
                continue
            for turn, core in enumerate((spot.core, 1 - spot.core)):
                ref = ins.pop(0)
                out[part, rows_at(core * half, half)] = ref[pl.ds(0, rows)]
                if turn == 1 and scatter.small is not None:
                    small(ref, count * rows + small_rows)
        for ref in ins:
            small(ref, count * rows)

    whole = ((count * rows + 2 * small_rows, width), BF16)
    (joined,) = call(run, [(VMEM, array) for array in given], [(VMEM,) + whole], [], name)
    return joined


def collect_kernel(group, turns, n_started, *refs):
    arrays, refs = refs[: len(turns)], refs[len(turns) + n_started :]
    (*outs, held, high, copies) = refs
    spot = Spot()
    rows, width = held.shape[1:]
    parts = []
    for i, (layer, by_rows) in enumerate(group):
        part = pl.ds(i * rows, rows)
        for source, turn in zip(arrays, turns):
            quarter = spot.block(turn)
            if by_rows:
                target = outs[1].at[layer, rows_at(quarter * rows, rows), :]
            else:
                target = outs[0].at[layer, :, rows_at(quarter * width, width)]
            parts.append((copies.start(source.at[part], held.at[len(parts)]), target))
    leaving = []
    for i, (copy, target) in enumerate(parts):
        copy.wait()
        high[i] = held[i].astype(F32)
        leaving.append(copies.start(high.at[i], target))
    return leaving


def norm(values):
    center = jnp.mean(values, axis=-1, keepdims=True)
    offsets = values - center
    inverse = lax.rsqrt(jnp.mean(offsets * offsets, axis=-1, keepdims=True) + 1e-05)
    return offsets * inverse, inverse


def norm_back(upstream, unit, inverse, gain):
    scaled = upstream * gain
    center = jnp.mean(scaled, axis=-1, keepdims=True)
    along = jnp.mean(scaled * unit, axis=-1, keepdims=True)
    return inverse * (scaled - center - unit * along)


def gelu_both(v):
    scale = math.sqrt(2.0 / math.pi)
    square = v * v
    half = 0.5 + 0.5 * jnp.tanh(v * (scale + (scale * 0.044715) * square))
    spread = (2.0 * half) * (1.0 - half)
    return v * half, half + (v * spread) * (scale + (3.0 * scale * 0.044715) * square)


def mix_forward(rows, hid, seq, gain, shift, real, imag, outs):
    unit, inverse, normed_low = outs
    hid_cos, hid_sin = hid[0](), hid[1]()

    @row_steps(rows.shape[0])
    def _(at):
        real[at, :] = dot(rows[at, :], hid_cos[...]).astype(BF16)
        imag[at, :] = dot(rows[at, :], hid_sin[...]).astype(BF16)

    seq_cos, seq_sin = seq[0](), seq[1]()

    @row_steps(rows.shape[0])
    def _(at):
        mixed = dot(seq_cos[at, :], real[...]) - dot(seq_sin[at, :], imag[...])
        unit_rows, inverse_rows = norm(rows[at, :].astype(F32) + mixed)
        unit.buffer[at, :] = unit_rows
        inverse[at, :] = inverse_rows
        normed_low.buffer[at, :] = (unit_rows * gain[...] + shift[...]).astype(BF16)
        normed_low.push(at)
        unit.push(at)


def first_mix_kernel(numbers, boundary, received, hid_cos, hid_sin, cos_tiles, sin_tiles, gain, shift, *refs):
    seq_cos, seq_sin = refs[0:2]
    outs, (rows, real, imag, copies) = refs[2:5], refs[5:]
    chosen = choose(copies, boundary.at[0, pl.ds(0, rows.shape[0])], received, rows)
    cos_tiles, sin_tiles = cos_tiles(), sin_tiles()
    base = cos_tiles.shape[1]
    slots = seq_cos.buffer.shape[0] // base
    for i in range(slots):
        for j in range(slots):
            window = (pl.ds(i * base, base), pl.ds(j * base, base))
            number = numbers[i * slots + j]
            seq_cos.buffer[window] = cos_tiles[number]
            seq_sin.buffer[window] = sin_tiles[number]
    seq_cos.push()
    seq_sin.push()
    seq = (lambda: seq_cos.buffer, lambda: seq_sin.buffer)
    chosen.wait()
    mix_forward(rows, (hid_cos, hid_sin), seq, gain, shift, real, imag, outs)


def expand_kernel(layer, by_permutes, n_sources, normed, other_normed, b_in, *refs):
    sources, (hidden, slope, whole, copies) = refs[:n_sources], refs[n_sources:]
    scratch = whole.buffer
    loaded = load_in(layer, sources, scratch, copies)
    spot = Spot(by_permutes)
    width = scratch.shape[2]
    count = normed.buffer.shape[0]
    for pair in range(2):
        biases = [b_in[:, rows_at(spot.block(2 * pair + i) * (width // 2), width // 2)] for i in range(2)]
        bias = jnp.concatenate(biases, axis=1)
        for copy in loaded[pair]:
            copy.wait()
        whole.push(pair)
        for place, rows in enumerate((normed, other_normed)):
            rows = rows()

            @row_steps(count)
            def _(at):
                value, rate = gelu_both(dot(rows[at, :], scratch[pair]) + bias)
                to = pl.ds(place * count + at.start, at.size)
                hidden.buffer[pair, to, :] = value.astype(BF16)
                slope.buffer[pair, to, :] = rate.astype(BF16)

        hidden.push(pair)
        slope.push(pair)


def contract_kernel(layer, n_sources, hidden, *refs):
    sources, (own, other, whole, copies) = refs[:n_sources], refs[n_sources:]
    scratch = whole.buffer
    loaded = load_out(layer, sources, scratch, copies)
    count, width = own.buffer.shape[0], hidden.buffer.shape[2]
    for copy in loaded:
        copy.wait()
    whole.push()
    for place, out in ((1, other), (0, own)):

        @row_steps(count)
        def _(at):
            rows = pl.ds(place * count + at.start, at.size)
            hidden(1)
            held = hidden.buffer
            total = dot(held[0, rows, :], scratch[0:width, :]) + dot(held[1, rows, :], scratch[width:, :])
            out.buffer[at, :] = total.astype(out.buffer.dtype)
            out.push(at)


def second_norm(at, own, received, unit_one, gain_one, shift_one, b_out):
    normed = unit_one[at, :] * gain_one[...] + shift_one[...]
    return norm(normed + (own[at, :] + received[at, :].astype(F32) + b_out[...]))


def middle_kernel(own, received, unit_one, gain_one, shift_one, b_out, gain_two, shift_two, *refs):
    hid, seq, (next_gain, next_shift) = refs[:2], refs[2:4], refs[4:6]
    unit_two, inverse_two = refs[6:8]
    outs, (mid, real, imag, _) = refs[8:11], refs[11:]
    own, received, unit_one = own(), received(), unit_one()

    @row_steps(mid.shape[0])
    def _(at):
        unit, inverse = second_norm(at, own, received, unit_one, gain_one, shift_one, b_out)
        unit_two.buffer[at, :] = unit
        inverse_two[at, :] = inverse
        mid[at, :] = (unit * gain_two[...] + shift_two[...]).astype(BF16)

    unit_two.push()
    mix_forward(mid, hid, seq, next_gain, next_shift, real, imag, outs)


def second_back(at, upstream, unit, inverse, gain, d_second, branch_grad, small):
    grad = norm_back(upstream, unit, inverse, gain[...])
    low = grad.astype(BF16)
    branch_grad.buffer[at, :] = low
    branch_grad.push(at)
    d_second.buffer[at, :] = grad
    d_second.push(at)
    small[0:1, :] += column_sum(low.astype(F32))
    small[1:2, :] += column_sum(upstream * unit)
    small[2:3, :] += column_sum(upstream)


def turn_kernel(own, received, unit_one, gain_one, shift_one, b_out, gain_two, shift_two, *refs):
    boundary, given, out_rows, d_second, branch_grad, small, cotangent, copies = refs
    count = cotangent.shape[0]
    chosen = choose(copies, given, boundary.at[0, pl.ds(count, count)], cotangent)
    own, received, unit_one = own(), received(), unit_one()
    small[...] = jnp.zeros_like(small)
    chosen.wait()

    @row_steps(own.shape[0])
    def _(at):
        unit, inverse = second_norm(at, own, received, unit_one, gain_one, shift_one, b_out)
        out_rows.buffer[at, :] = (unit * gain_two[...] + shift_two[...]).astype(BF16)
        upstream = cotangent[at, :].astype(F32)
        second_back(at, upstream, unit, inverse, gain_two, d_second, branch_grad, small)
        out_rows.push(at)


def grad_out_kernel(by_permutes, hidden, branch_grad, other_grad, *refs):
    outs, (tiles, copies) = refs[:-2], refs[-2:]
    spot = Spot(by_permutes)
    count = branch_grad.shape[0]
    shard = tiles.shape[1]
    for turn in range(BLOCKS):
        columns = pl.ds((turn % 2) * shard, shard)
        grad = 0.0
        for i, ref in enumerate((branch_grad, other_grad)):
            rows = hidden[turn // 2, pl.ds(i * count, count), columns]
            grad = grad + dot(rows, ref[...], ((0,), (0,)))
        if not by_permutes:
            outs[0][pl.ds(turn * shard, shard), :] = grad.astype(BF16)
            continue
        tiles[turn] = grad.astype(BF16)
        rows = outs[0].shape[2]
        apart = spot.block(turn) ^ spot.chip
        for slot in range(BLOCKS):
            part = tiles[turn, rows_at(spot.block(slot) * rows, rows), :]
            outs[slot // 2][slot % 2, apart] = part


def shrink_kernel(by_permutes, n_outs, branch_grad, other_grad, slope, normed, other_normed, whole_out, whole_in, *refs):
    outs, (b_grad, own, other, tiles, act_grad, copies) = refs[:n_outs], refs[n_outs:]
    spot = Spot(by_permutes)
    count = branch_grad.shape[0]
    width = tiles.shape[2]
    half = width // 2
    b_grad[...] = jnp.zeros_like(b_grad)
    for pair in range(2):
        sums = []
        for place, ref in enumerate((branch_grad, other_grad)):

            @row_steps(count)
            def _(at):
                rows = pl.ds(place * count + at.start, at.size)
                grad = dot(ref[at, :], whole_out[pl.ds(pair * width, width), :], ((1,), (1,)))
                low = (grad * slope[pair, rows, :].astype(F32)).astype(BF16)
                act_grad[pair, rows, :] = low
                sums.append(column_sum(low.astype(F32)))

        total = sum(sums[1:], sums[0])
        for side in range(2):
            block = spot.block(2 * pair + side)
            b_grad[:, rows_at((2 * block + spot.core) * half, half)] = total[:, side * half : (side + 1) * half]

        @row_steps(tiles.shape[1])
        def _(at):
            grad = 0.0
            for place, ref in enumerate((normed, other_normed)):
                grads = act_grad[pair, pl.ds(place * count, count), :]
                grad = grad + dot(ref[:, at], grads, ((0,), (0,)))
            if by_permutes:
                tiles[pair, at, :] = grad.astype(BF16)
            else:
                outs[0][at, pl.ds(pair * width, width)] = grad.astype(BF16)

        if by_permutes:
            rows = outs[0].shape[2]
            for side in range(2):
                for chip in range(spot.chips):
                    part = tiles[pair, pl.ds(chip * rows, rows), pl.ds(side * half, half)]
                    outs[pair][side, chip ^ spot.chip] = part
    for place, out in ((1, other), (0, own)):

        @row_steps(count)
        def _(at):
            rows = pl.ds(place * count + at.start, at.size)
            total = dot(act_grad[0, rows, :], whole_in[0], ((1,), (1,)))
            total = total + dot(act_grad[1, rows, :], whole_in[1], ((1,), (1,)))
            out[at, :] = total.astype(out.dtype)


def unmix(refs, total, mix_grad, real, imag, small, input_grad):
    own, received, d_second, unit_one, inverse_one, gain_one, hid_cos, hid_sin, seq_cos, seq_sin = refs
    own, received, d_second, unit_one = own(), received(), d_second(), unit_one()
    small[...] = jnp.zeros_like(small)

    @row_steps(total.shape[0])
    def _(at):
        upstream = d_second[at, :] + own[at, :] + received[at, :].astype(F32)
        unit = unit_one[at, :]
        grad = norm_back(upstream, unit, inverse_one[at, :], gain_one[...])
        total[at, :] = grad
        mix_grad[at, :] = grad.astype(BF16)
        small[0:1, :] += column_sum(upstream * unit)
        small[1:2, :] += column_sum(upstream)

    seq_cos, seq_sin = seq_cos(), seq_sin()

    @row_steps(total.shape[0])
    def _(at):
        real[at, :] = dot(seq_cos[at, :], mix_grad[...]).astype(BF16)
        imag[at, :] = (-dot(seq_sin[at, :], mix_grad[...])).astype(BF16)

    hid_cos, hid_sin = hid_cos(), hid_sin()

    @row_steps(total.shape[0])
    def _(at):
        grad = dot(real[at, :], hid_cos[...]) + dot(imag[at, :], hid_sin[...])
        input_grad(at, total[at, :] + grad)


def last_kernel(*refs):
    ins, (out_rows, *smalls) = refs[:10], refs[10:17]
    sent, kept, packed, total, mix_grad, real, imag, small, _ = refs[17:]
    is_first = lax.axis_index("section") % 2 == 0
    rows = out_rows()

    def input_grad(at, values):
        low = values.astype(BF16)
        sent.buffer[at, :] = jnp.where(is_first, rows[at, :], low)
        kept.buffer[at, :] = jnp.where(is_first, low, rows[at, :])
        sent.push(at)
        kept.push(at)

    unmix(ins, total, mix_grad, real, imag, small, input_grad)
    width = packed.shape[1]
    packed[...] = jnp.zeros_like(packed)
    for layer in range(2):
        b_grad, sums_two = smalls[3 * layer : 3 * layer + 2]
        sums_one = smalls[3 * layer + 2] if layer else small
        at = layer * (packed.shape[0] // 2)
        sums = (sums_two[0:1], sums_one[0:1], sums_one[1:2], sums_two[1:2], sums_two[2:3])
        for vector in (b_grad[...],) + sums:
            for i in range(vector.shape[1] // width):
                packed[at : at + 1, :] = vector[:, i * width : (i + 1) * width].astype(packed.dtype)
                at += 1


def finish_kernel(kept, back, result, held, high, copies):
    layer = lax.axis_index("section") % 2
    count = held.shape[1]
    arriving = [copies.start(ref, held.at[i]) for i, ref in enumerate((kept, back))]
    leaving = []
    for i, block in enumerate((layer, 1 - layer)):
        arriving[i].wait()
        high[i] = held[i].astype(F32)
        leaving.append(copies.start(high.at[i], result.at[0, rows_at(block * count, count)]))
    return leaving


def relay_kernel(*refs):
    ins, (unit_two, inverse_two, gain_two) = refs[:10], refs[10:13]
    small, d_second, branch_grad, small_two, total, mix_grad, real, imag, _ = refs[13:]
    small_two[...] = jnp.zeros_like(small_two)

    def input_grad(at, values):
        upstream = values.astype(BF16).astype(F32)
        unit = unit_two()[at, :]
        second_back(at, upstream, unit, inverse_two[at, :], gain_two, d_second, branch_grad, small_two)

    unmix(ins, total, mix_grad, real, imag, small, input_grad)


def body(boundary, bucket_ids, w_in, b_in, w_out, b_out, gain_one, shift_one, gain_two, shift_two):
    place = Place()
    Order.begin()
    layers = w_in.shape[0]
    micro_count = bucket_ids.shape[1]
    feat_width = boundary.shape[2]
    ff_width = w_in.shape[2]
    slab_len = boundary.shape[1] // micro_count
    slots = bucket_ids.shape[2]
    base_len = slab_len // slots
    half_block = ff_width // (2 * BLOCKS)
    by_permutes = place.n_section == 4 and place.chips == 4
    last = layers - 1

    bucket_row = bucket_ids[place.section // 2, place.section % 2]
    half_bias = lax.dynamic_index_in_dim(
        b_in.reshape(layers, BLOCKS, 2, half_block), place.core, 2, keepdims=False
    ).reshape(layers, -1)

    block = (slab_len, feat_width)
    both = (2 * slab_len, feat_width)
    wide_block = (2, 2 * slab_len, ff_width // 4)
    whole_in_shape = (2, feat_width, ff_width // 4)
    whole_out_shape = (ff_width // 2, feat_width)
    column = (VMEM, (slab_len, 1), F32)
    sums_shape = (VMEM, (8, feat_width), F32)
    mix_outs = [(EARLY, block, F32), column, (EARLY, block, BF16)]
    hid = [(LATE, jnp.asarray(table.astype(BF16))) for table in dft_tables(feat_width)]

    def late(*arrays):
        return [(LATE, array) for array in arrays]

    def plain(*arrays):
        return [(HBM, array) for array in arrays]

    def param(array, layer):
        return (VMEM, array[layer][None])

    shard_rows, piece_rows = w_in.shape[1], w_out.shape[1] // BLOCKS
    prepared = [(HBM, block, BF16)]
    if by_permutes:
        prepared += [(HBM, (layers, shard_rows, ff_width // 2), BF16)]
        prepared += [(HBM, (piece_rows, feat_width), BF16)] * layers
    given, *prepared = call(
        partial(prepare_kernel, layers, by_permutes),
        plain(boundary, w_in, w_out),
        prepared,
        [
            (block, BF16),
            ((layers, shard_rows, ff_width // 2), BF16),
            ((layers, piece_rows, feat_width), BF16),
        ],
        "prepare",
        spare=54 * 2**20,
    )
    sources_in, sources_out = [None] * layers, [None] * layers
    if by_permutes:
        for_other, out_zero_piece, out_one_piece = prepared
        in_zero, out_zero, in_one, out_one = (
            Gather(place, name + str(layer), w, None, layer, by_rows)
            for layer in range(layers)
            for name, w, by_rows in (("in", w_in, False), ("out", w_out, True))
        )
        other_rows = place.swap_core(for_other)
        received = place.swap_layer(given)
        in_zero.other_rows = in_one.other_rows = other_rows
        out_zero_moved = place.along_z(out_zero_piece, 1)
        in_zero.shift(in_zero.join(other_rows))
        pieces_one = in_one.join(other_rows, out_one_piece)
        out_zero_pair = pack("pair_out0", [out_zero_piece, out_zero_moved])
        out_zero.moved = [out_zero_moved, place.along_z(out_zero_pair, 2)]
        Order.wait(received)
        in_zero.one()
        moved_one = place.along_z(tie(pieces_one, Order.token), 1)
    else:
        received = place.swap_layer(given)
        for layer in range(layers):
            whole_in, whole_out = (
                lax.all_gather(w[layer], "dp", axis=0, tiled=True) for w in (w_in, w_out)
            )
            whole_in = whole_in.reshape(feat_width, BLOCKS, 2, half_block)
            whole_out = whole_out.reshape(BLOCKS, 2, half_block, feat_width)
            whole_in = lax.dynamic_index_in_dim(whole_in, place.core, 2, keepdims=False)
            whole_out = lax.dynamic_index_in_dim(whole_out, place.core, 1, keepdims=False)
            sources_in[layer] = [whole_in.reshape(feat_width, -1)]
            sources_out[layer] = [whole_out.reshape(-1, feat_width)]

    numbers = tile_numbers(bucket_row, slots).reshape(-1)
    tiles = [(LATE, jnp.asarray(table)) for table in sequence_tiles(base_len)]
    seq_cos, seq_sin, *mixed = call(
        first_mix_kernel,
        [(SMEM, numbers)]
        + plain(boundary, received)
        + hid
        + tiles
        + [param(gain_one, 0), param(shift_one, 0)],
        [(EARLY, (slab_len, slab_len), BF16)] * 2 + mix_outs,
        [(block, BF16)] * 3,
        "first_mix",
    )
    tables = hid + late(seq_cos, seq_sin)

    both_pairs, all_rows = pl.ds(0, 2), pl.ds(0, 2 * slab_len)
    steps = slab_len // ROW_STEP
    row_parts = [
        (both_pairs, pl.ds(slab_len * place_ + i * ROW_STEP, ROW_STEP))
        for place_ in (1, 0)
        for i in range(steps)
    ]
    block_parts = [
        (pair, all_rows, pl.ds(side * half_block, half_block)) for pair in range(2) for side in range(2)
    ]
    pair_parts = [(pl.ds(pair, 1),) for pair in range(2)]
    half_parts = [(pl.ds(pair * 2 * half_block, 2 * half_block),) for pair in range(2)]

    saved, wholes_in, wholes_out = [], [], []
    for layer in range(layers):
        unit_one, inverse_one, normed = mixed
        if by_permutes and layer == 0:
            mark = Order.mark(in_zero.from_one, in_zero.from_two)
            in_zero.two(mark)
            other_normed = place.swap_core(tie(normed, mark))
            pair_in, pair_out = pairs(pieces_one, moved_one)
            out_zero.one()
            in_one.moved = [(pair_in, 1, 1), place.along_z(pair_in, 2)]
            sources_in[0] = in_zero.sources()
        else:
            other_normed = place.swap_core(normed)
        if by_permutes and layer == 1:
            Order.mark(in_one.far)
            mark = Order.mark(out_one.from_one, out_one.from_two)
            out_one.two(mark)
            sources_in[1] = in_one.sources()
        hidden, slope, whole_in = call(
            partial(expand_kernel, layer, by_permutes, len(sources_in[layer])),
            late(normed, other_normed)
            + [(VMEM, half_bias[layer][None])]
            + plain(*sources_in[layer]),
            [(EARLY, wide_block, BF16), (EARLY, wide_block, BF16), (EARLY, whole_in_shape, BF16)],
            [],
            "expand",
        )
        if by_permutes and layer == 0:
            mark = Order.mark(out_zero.from_one, out_zero.from_two)
            out_zero.two(mark)
            in_one.one()
            out_one.moved = [(pair_out, 1, 1), place.along_z(tie(pair_out, in_one.along), 2)]
            sources_out[0] = out_zero.sources()
        if by_permutes and layer == 1:
            sources_out[1] = out_one.sources()
        own_part, other_part, whole_out = call(
            partial(contract_kernel, layer, len(sources_out[layer])),
            [(LATE, hidden, row_parts)] + plain(*sources_out[layer]),
            [(EARLY, block, F32), (EARLY, block, BF16), (EARLY, whole_out_shape, BF16)],
            [],
            "contract",
        )
        from_other = place.swap_core(other_part)
        if by_permutes and layer == 0:
            mark = Order.mark(in_one.from_one, in_one.from_two)
            in_one.two(mark)
            out_one.one()
        wholes_in.append(whole_in)
        wholes_out.append(whole_out)
        common = late(own_part, from_other, unit_one) + [
            param(p, layer) for p in (gain_one, shift_one, b_out, gain_two, shift_two)
        ]
        kept = [unit_one, inverse_one, normed, other_normed, hidden, slope]
        if layer < last:
            unit_two, inverse_two, *mixed = call(
                middle_kernel,
                common + tables + [param(gain_one, layer + 1), param(shift_one, layer + 1)],
                [(EARLY, block, F32), column] + mix_outs,
                [(block, BF16), (block, BF16), (block, BF16)],
                "middle",
            )
            kept += [unit_two, inverse_two]
        saved.append(kept)

    Order.cost = BACKWARD_COST
    out_rows, d_second, branch_grad, sums_two = call(
        turn_kernel,
        common + plain(boundary, received),
        [(EARLY, block, BF16), (EARLY, block, F32), (EARLY, block, BF16), sums_shape],
        [(block, BF16)],
        "turn",
    )

    if by_permutes:
        piece_out = (2, place.chips, w_out.shape[1] // BLOCKS, feat_width)
        piece_in = (2, place.chips, 2 * w_in.shape[1], half_block)
        grad_outs = {True: [(VMEM, piece_out, BF16)] * 2, False: [(VMEM, piece_in, BF16)] * 2}
    else:
        grad_outs = {
            True: [(VMEM, (ff_width // 2, feat_width), BF16)],
            False: [(VMEM, (feat_width, ff_width // 2), BF16)],
        }
    n_outs = len(grad_outs[True])
    grads, smalls, running = {}, {}, []

    def reduce_grad(pieces, layer, by_rows):
        name = ("out" if by_rows else "in") + str(layer)
        if by_permutes:
            grads[layer, by_rows] = Scatter(place, name, *pieces, by_rows)
            running.append(grads[layer, by_rows])
            return
        (half,) = pieces
        if by_rows:
            whole = jnp.zeros((BLOCKS, 2, half_block, feat_width), BF16)
            half = half.reshape(BLOCKS, 1, half_block, feat_width)
            whole = lax.dynamic_update_slice_in_dim(whole, half, place.core, 1)
            whole = whole.reshape(ff_width, feat_width)
        else:
            whole = jnp.zeros((feat_width, BLOCKS, 2, half_block), BF16)
            half = half.reshape(feat_width, BLOCKS, 1, half_block)
            whole = lax.dynamic_update_slice_in_dim(whole, half, place.core, 2)
            whole = whole.reshape(feat_width, ff_width)
        part = lax.psum_scatter(whole, "dp", scatter_dimension=0, tiled=True)
        grads[layer, by_rows] = lax.psum(part, "section").astype(F32)

    for layer in reversed(range(layers)):
        unit_one, inverse_one, normed, other_normed, hidden, slope = saved[layer][:6]
        other_grad = place.swap_core(branch_grad)
        if by_permutes and layer == 0:
            running[0].two()
            running[1].two()
        pieces = call(
            partial(grad_out_kernel, by_permutes),
            [(VMEM, hidden), (VMEM, branch_grad), (VMEM, other_grad)],
            grad_outs[True],
            [((BLOCKS, half_block, feat_width), BF16)],
            "grad_out",
        )
        reduce_grad(pieces, layer, True)
        if by_permutes and layer == 0:
            running[0].three()
            Order.mark(running[1].from_two)
        *pieces, b_grad, own_part, other_part = call(
            partial(shrink_kernel, by_permutes, n_outs),
            [
                (VMEM, array)
                for array in (branch_grad, other_grad, slope, normed, other_normed)
                + (wholes_out[layer], wholes_in[layer])
            ],
            grad_outs[False]
            + [(VMEM, (1, ff_width), F32), (VMEM, block, F32), (VMEM, block, BF16)],
            [((2, feat_width, ff_width // 4), BF16), (wide_block, BF16)],
            "shrink",
        )
        from_other = place.swap_core(other_part)
        reduce_grad(pieces, layer, False)
        if by_permutes and layer == last:
            Order.mark(running[0].from_one)
        if by_permutes and layer == 0:
            running[0].neighbour()
            running[2].two()
            running[1].three()
        ins = (
            late(own_part, from_other, d_second, unit_one)
            + [(VMEM, inverse_one), param(gain_one, layer)]
            + tables
        )
        work = [(block, F32), (block, BF16), (block, BF16), (block, BF16)]
        smalls[layer] = [b_grad, sums_two]
        if layer > 0:
            below_unit, below_inverse = saved[layer - 1][6:8]
            sums_one, d_second, branch_grad, sums_two = call(
                relay_kernel,
                ins + late(below_unit) + [(VMEM, below_inverse), param(gain_two, layer - 1)],
                [sums_shape, (EARLY, block, F32), (EARLY, block, BF16), sums_shape],
                work,
                "relay",
            )
            smalls[layer].append(sums_one)
    vectors = smalls[0] + [smalls[1][2]] + smalls[1]
    small_type = BF16 if by_permutes else F32
    sent, kept_rows, packed = call(
        last_kernel,
        ins + late(out_rows) + [(VMEM, vector) for vector in vectors],
        [(EARLY, block, BF16), (EARLY, block, BF16), (VMEM, (64, half_block), small_type)],
        work + [((8, feat_width), F32)],
        "last",
    )

    def finish():
        return call(
            finish_kernel,
            plain(kept_rows, back),
            [(HBM, (1, 2 * slab_len, feat_width), F32)],
            [((2,) + block, BF16), ((2,) + block, F32)],
            "finish",
        )

    if by_permutes:

        def share(mine):
            return [place.plane_one(mine), place.plane_two(mine)]

        out_last, in_last, out_first, in_first = running
        in_first.small = [(packed, pl.ds(0, packed.shape[0]))]
        out_first.three()
        in_first.two()
        out_last.four()
        in_last.neighbour()
        in_first.three()
        back = place.swap_layer(tie(sent, Order.token))
        in_last.four()
        out_first.neighbour()
        in_first.neighbour()
        (result,) = finish()
        mine = join("join_rest", [in_last, out_last])
        rest = share(mine)
        out_first.four()
        in_first.four()
        rest.append(place.plane_two(tie(rest[0], Order.token)))
        Order.wait(rest[1])
        last_mine = join("join_last", [in_first, out_first])
        last_rest = share(last_mine)
        groups = [[(last, False), (last, True)], [(0, False), (0, True)]]
        unit = (shard_rows, ff_width // BLOCKS)

        def collect(group, quarters, started):
            turns, arrays = zip(*quarters)
            held = ((len(turns) * len(group),) + unit,)
            n = len(turns)
            return call(
                partial(collect_kernel, group, turns, len(started)),
                plain(*arrays, *started),
                [(HBM, w_in.shape, F32), (HBM, w_out.shape, F32)],
                [held + (BF16,), held + (F32,)],
                "collect",
                aliases={n: 0, n + 1: 1} if started else None,
            )

        Order.wait(rest[2])
        started = collect(groups[0], zip((3, 0, 2, 1), [mine] + rest), ())
        mark = Order.mark(*last_rest)
        far = place.plane_two(tie(last_rest[0], mark))
        started = collect(groups[1], zip((3, 0, 2), [last_mine] + last_rest), tuple(started))
        at, size = 2 * shard_rows, (last_mine.shape[0] - 2 * shard_rows) // 2
        packed = sum(
            array[at + i * size : at + (i + 1) * size].astype(F32)
            for i, arrays in enumerate(((last_mine, last_rest[0]), (last_mine, last_rest[1])))
            for array in arrays
        )
        packed = packed.reshape(-1, 2, half_block).transpose(1, 0, 2).reshape(-1, half_block)
        packed = tie(packed, Order.token)
        Order.wait(packed)
        grad_in, grad_out = collect(groups[1], [(1, far)], tuple(started))
    else:
        back = place.swap_layer(sent)
        grad_in, grad_out = (
            jnp.stack([grads[layer, by_rows] for layer in range(layers)])
            for by_rows in (False, True)
        )
        packed = lax.psum(packed, AXES)
        (result,) = finish()
    b_part, part = ff_width // place.n_dp, feat_width // place.n_dp
    flat = packed.reshape(layers, -1)
    small_out = [lax.dynamic_slice_in_dim(flat, place.dp * b_part, b_part, 1)]
    sums = flat[:, ff_width : ff_width + 5 * feat_width].reshape(layers, 5, feat_width)
    sums = lax.dynamic_slice_in_dim(sums, place.dp * part, part, 2)
    small_out += [sums[:, i] for i in range(5)]
    return (result, grad_in, small_out[0], grad_out, *small_out[1:])


def solution(mesh):
    return jax.shard_map(
        body,
        mesh=mesh,
        in_specs=(
            P("section", "dp", None),
            P(None, "dp", None),
            P(None, "dp", None),
            P(),
            P(None, "dp", None),
            P(),
            P(),
            P(),
            P(),
            P(),
        ),
        out_specs=(
            P("section", "dp", None),
            P(None, "dp", None),
            P(None, "dp"),
            P(None, "dp", None),
            P(None, "dp"),
            P(None, "dp"),
            P(None, "dp"),
            P(None, "dp"),
            P(None, "dp"),
        ),
        check_vma=False,
    )
```

```python
from functools import partial
import math

import jax
import jax.numpy as jnp
import numpy as np
from jax import lax
from jax.experimental import pallas as pl
from jax.experimental.pallas import tpu as pltpu
from jax.sharding import PartitionSpec as P

AXES = ("section", "dp")
F32 = jnp.float32
BF16 = jnp.bfloat16
BLOCKS = 4
EVENT_COST, SHORT_COST = 10**10, 10**9
FAR_MARK_COST, NEAR_MARK_COST, MIDDLE_COST = 2000000000, 4000000000, 100000000
ROW_STEP = 256

VMEM = pl.BlockSpec(memory_space=pltpu.VMEM)
SMEM = pl.BlockSpec(memory_space=pltpu.SMEM)
HBM = pl.BlockSpec(memory_space=pltpu.HBM)
LATE, EARLY = "late", "early"


class Place:
    def __init__(self):
        self.n_section = lax.axis_size("section")
        self.n_dp = lax.axis_size("dp")
        self.chips = self.n_dp // 2
        self.section = lax.axis_index("section")
        self.dp = lax.axis_index("dp")
        self.core = self.dp % 2

    def permute(self, value, target):
        pairs = []
        for section in range(self.n_section):
            for chip in range(self.chips):
                for core in range(2):
                    to_section, to_chip, to_core = target(section, chip, core)
                    source = section * self.n_dp + chip * 2 + core
                    pairs.append((source, to_section * self.n_dp + to_chip * 2 + to_core))
        return lax.ppermute(value, AXES, pairs)

    def swap_core(self, value):
        return self.permute(value, lambda s, z, c: (s, z, 1 - c))

    def swap_layer(self, value):
        return self.permute(value, lambda s, z, c: (s ^ 1, z, c))

    def plane_one(self, value):
        return self.permute(value, lambda s, z, c: (s ^ (1 + c), z, c))

    def plane_two(self, value):
        return self.permute(value, lambda s, z, c: (s ^ (2 - c), z, c))

    def along_z(self, value, flip):
        return self.permute(value, lambda s, z, c: (s, z ^ flip, c))


class Spot:
    def __init__(self, by_permutes=True):
        dp = lax.axis_index("dp")
        self.core = dp % 2
        if by_permutes:
            self.section, self.chip = lax.axis_index("section"), dp // 2
            self.chips = lax.axis_size("dp") // 2
            self.held = (1 + self.core, 3, 2 - self.core, 0)
        else:
            self.section, self.held = 0, (0, 1, 2, 3)

    def block(self, turn):
        return self.section ^ self.held[turn]

    def turn_of(self, block):
        flip = block ^ self.section
        side = jnp.where(flip == self.held[0], 0, 2)
        return jnp.where(flip == 3, 1, jnp.where(flip == 0, 3, side))


def dft_tables(length):
    positions = np.arange(length)
    angles = (positions[:, None] * positions[None, :] % length) * (2.0 * math.pi) / length
    scaling = 1.0 / math.sqrt(length)
    return (np.cos(angles) * scaling, np.sin(angles) * scaling)


def sequence_tiles(base_len):
    cos_tiles, sin_tiles = [], []
    for parts in (1, 2, 4):
        cos_table, sin_table = dft_tables(parts * base_len)
        for i in range(parts):
            for j in range(parts):
                window = (
                    slice(i * base_len, (i + 1) * base_len),
                    slice(j * base_len, (j + 1) * base_len),
                )
                cos_tiles.append(cos_table[window])
                sin_tiles.append(sin_table[window])
    cos_tiles.append(np.zeros((base_len, base_len)))
    sin_tiles.append(np.zeros((base_len, base_len)))
    return np.stack(cos_tiles).astype(BF16), np.stack(sin_tiles).astype(BF16)


def tile_numbers(bucket_row, slots):
    parts = jnp.where(bucket_row < 3, 1 << jnp.minimum(bucket_row, 2), 0)
    ends = jnp.cumsum(parts)
    where = jnp.arange(slots, dtype=jnp.int32)
    segment = jnp.sum((where[:, None] >= ends[None, :]).astype(jnp.int32), axis=1)
    one_hot = (segment[:, None] == jnp.arange(slots)[None, :]).astype(jnp.int32)
    start = jnp.sum(one_hot * (ends - parts)[None, :], axis=1)
    size = jnp.sum(one_hot * parts[None, :], axis=1)
    first = jnp.where(size == 1, 0, jnp.where(size == 2, 1, 5))
    place = where - start
    numbers = first[:, None] + place[:, None] * size[:, None] + place[None, :]
    return jnp.where(segment[:, None] == segment[None, :], numbers, 21)


def rows_at(start, size):
    return pl.ds(pl.multiple_of(start, size), size)


def dot(left, right, dims=((1,), (0,))):
    return lax.dot_general(left, right, (dims, ((), ())), preferred_element_type=F32)


def row_steps(count, step=ROW_STEP):
    step = step if count % step == 0 else count

    def run(function):
        for i in range(count // step):
            function(pl.ds(i * step, step))

    return run


def column_sum(values):
    return jnp.sum(values, axis=0, keepdims=True)


class Copies:
    def __init__(self, sems):
        self.sems, self.count = sems, 0

    def start(self, source, target):
        copy = pltpu.make_async_copy(source, target, self.sems.at[self.count])
        copy.start()
        self.count += 1
        return copy


class Late:
    def __init__(self, ref):
        self.buffer = ref

    def __call__(self, parts=None):
        return self.buffer


class Early:
    def __init__(self, ref):
        self.buffer, self.leaving = ref, []

    def push(self, part=None):
        pass


def tie(value, *others):
    return lax.optimization_barrier((value,) + others)[0]


class Order:
    token = None

    @classmethod
    def begin(cls):
        cls.token = jnp.zeros((8, 128), F32)

    @classmethod
    def wait(cls, *arrays):
        cls.token = tie(cls.token, *arrays)

    @classmethod
    def mark(cls, *arrays, cost=EVENT_COST):
        cls.wait(*arrays)
        call(lambda *refs: None, [], [], [], "mark", cost=cost)
        return cls.token


def call(kernel, ins, outs, scratch, name, aliases=None, spare=4 * 2**20, cost=EVENT_COST):
    buffers = []
    n_ins, n_outs, n_scratch = len(ins), len(outs), len(scratch)
    counts = []

    def run(*refs):
        given, made = list(refs[:n_ins]), list(refs[n_ins + 1 :][:n_outs])
        token_out, refs = refs[n_ins + 1 + n_outs], refs[n_ins + 2 + n_outs :]
        own, held, copies = refs[:n_scratch], list(refs[n_scratch:-1]), Copies(refs[-1])
        late = []
        for i, entry in enumerate(ins):
            if entry[0] is LATE:
                given[i] = Late(given[i])
                late.append(given[i])
        early = []
        for i, out in enumerate(outs):
            if out[0] is EARLY:
                made[i] = Early(made[i])
                early.append(made[i])
        leaving = kernel(*given, *made, *own, copies) or []
        token_out[...] = jnp.zeros_like(token_out)
        for value in late:
            value()
        for copy in leaving + [copy for out in early for copy in out.leaving]:
            copy.wait()
        counts.append(copies.count)

    def spec_of(spec):
        return VMEM if spec in (LATE, EARLY) else spec

    held = list(scratch) + [(a[1].shape, a[1].dtype) for a in ins if a[0] in (LATE, VMEM)]
    held += [out[1:] for out in outs if out[0] in (EARLY, VMEM)]
    needed = sum(math.prod(shape) * jnp.dtype(dtype).itemsize for shape, dtype in held)

    def build(sems):
        return pl.pallas_call(
            run,
            in_specs=[spec_of(entry[0]) for entry in ins] + [HBM],
            out_specs=tuple(spec_of(out[0]) for out in outs) + (VMEM,),
            out_shape=tuple(jax.ShapeDtypeStruct(*out[1:]) for out in outs)
            + (jax.ShapeDtypeStruct((8, 128), F32),),
            scratch_shapes=[pltpu.VMEM(*s) for s in scratch]
            + buffers
            + [pltpu.SemaphoreType.DMA((sems,))],
            compiler_params=pltpu.CompilerParams(vmem_limit_bytes=needed + spare),
            cost_estimate=pl.CostEstimate(flops=cost, bytes_accessed=1000, transcendentals=0),
            input_output_aliases=aliases or {},
            name=name,
        )

    arrays = [entry[1] for entry in ins] + [Order.token]
    jax.eval_shape(build(96), *arrays)
    *made, Order.token = build(max(counts[-1], 1))(*arrays)
    return made


def plain(*arrays):
    return [(HBM, array) for array in arrays]


def move(name, terms, unit, outs, targets, extra=None):
    jobs = [
        ([(array, indices[i]) for array, indices in terms], unit, target)
        for i, target in enumerate(targets)
    ]
    if extra is not None:
        jobs.append(extra)
    given = []
    for job_terms, _, _ in jobs:
        for array, _ in job_terms:
            if not any(array is other for other in given):
                given.append(array)

    def run(*refs):
        ins, made = refs[: len(given)], refs[len(given) : len(given) + len(outs)]

        def at(index):
            index = index(Spot()) if callable(index) else index
            return index if index else Ellipsis

        for job_terms, _, (number, target) in jobs:
            parts = [
                next(ref for ref, other in zip(ins, given) if other is array)[at(index)]
                for array, index in job_terms
            ]
            if len(parts) > 1:
                parts = [sum((part.astype(F32) for part in parts[1:]), parts[0].astype(F32))]
            made[number][at(target)] = parts[0].astype(BF16)

    return call(
        run,
        [(VMEM, array) for array in given],
        [(VMEM, shape, BF16) for shape in outs],
        [],
        name,
    )


def pack(name, entries):
    entries = [entry if isinstance(entry, tuple) else (entry, None, None) for entry in entries]
    unit = entries[0][0].shape[-2:]
    sizes = [
        count or (1 if len(array.shape) == 2 else array.shape[0]) for array, _, count in entries
    ]
    starts = [sum(sizes[:i]) for i in range(len(sizes))]

    def run(*refs):
        out = refs[len(entries)]
        for i, (ref, (_, start, count)) in enumerate(zip(refs, entries)):
            source = ref[...] if start is None else ref[pl.ds(start, count)]
            out[pl.ds(starts[i], sizes[i])] = source.reshape((sizes[i],) + unit)

    whole = ((sum(sizes),) + unit, entries[0][0].dtype)
    (packed,) = call(
        run, [(VMEM, entry[0]) for entry in entries], [(VMEM,) + whole], [], name
    )
    return packed


def choose(copies, first, second, buffer):
    is_first = lax.axis_index("section") % 2 == 0
    sem = copies.sems.at[copies.count]
    copies.count += 1
    pair = [pltpu.make_async_copy(source, buffer, sem) for source in (first, second)]
    pl.when(is_first)(pair[0].start)
    pl.when(jnp.logical_not(is_first))(pair[1].start)
    return pair[0]


def prepare_kernel(layers, by_permutes, boundary, w_in, w_out, given, *refs):
    outs, (slab, rows, pieces, copies) = refs[: -4], refs[-4:]
    count = slab.shape[0]
    first, second = (boundary.at[0, pl.ds(i * count, count)] for i in range(2))
    slab_copy = choose(copies, second, first, slab)
    leaving = []
    if by_permutes:
        other_rows, *out_pieces = outs
        spot = Spot()
        width = w_in.shape[2] // (2 * BLOCKS)
        arriving = []
        for block in range(BLOCKS):
            source = w_in.at[:, :, rows_at((2 * block + 1 - spot.core) * width, width)]
            arriving.append(copies.start(source, rows.at[:, :, pl.ds(block * width, width)]))
        high = w_out.shape[1] // BLOCKS
        for layer in range(layers):
            source = w_out.at[layer, rows_at(spot.section * high, high)]
            arriving.append(copies.start(source, pieces.at[layer]))
        for copy in arriving[:BLOCKS]:
            copy.wait()
        leaving.append(copies.start(rows, other_rows))
        for layer in range(layers):
            arriving[BLOCKS + layer].wait()
            leaving.append(copies.start(pieces.at[layer], out_pieces[layer]))
    slab_copy.wait()
    leaving.append(copies.start(slab, given))
    return leaving


class Gather:
    def __init__(self, place, name, w, other_rows, layer, by_rows):
        self.place, self.name, self.by_rows = place, name, by_rows
        self.w, self.other_rows, self.layer = w, other_rows, layer

    def join(self, halves, out_pieces=()):
        layer, rows, width = self.layer, self.w.shape[1], self.w.shape[2] // (2 * BLOCKS)
        beside = len(out_pieces) > 0
        shape = (1 + len(out_pieces), rows, 2 * width) if beside else (2 * rows, width)

        def run(w, other, *refs):
            out_refs, (out, copies) = refs[:-2], refs[-2:]
            spot = Spot()
            own = w.at[layer, :, rows_at((2 * spot.section + spot.core) * width, width)]
            other = other.at[layer, :, rows_at(spot.section * width, width)]
            arriving = []
            for source, core in ((own, spot.core), (other, 1 - spot.core)):
                target = out.at[rows_at(core * rows, rows)]
                if beside:
                    target = out.at[0, :, rows_at(core * width, width)]
                arriving.append(copies.start(source, target))
            for i, ref in enumerate(out_refs):
                arriving.append(copies.start(ref, out.at[1 + i]))
            for copy in arriving:
                copy.wait()

        (piece,) = call(
            run,
            plain(self.w, halves, *out_pieces),
            [(VMEM, shape, BF16)],
            [],
            "piece_" + self.name,
        )
        return piece

    def shift(self, piece):
        self.moved = [self.place.along_z(piece, flip) for flip in (1, 2, 3)]

    def one(self):
        self.along = pack("along_" + self.name, self.moved)
        self.from_one = self.place.plane_one(self.along)
        self.from_two = self.place.plane_two(self.along)

    def two(self, *others):
        self.far = self.place.plane_two(tie(self.from_one, *others))

    def sources(self):
        moved = [self.along, self.from_one, self.from_two, self.far]
        return [self.w] + moved if self.by_rows else [self.w, self.other_rows] + moved


def pairs(own, moved):
    n, rows, width = own.shape

    def run(own, moved, pair_in, *refs):
        for i, ref in enumerate((own, moved)):
            for core in range(2):
                half = pl.ds(core * (width // 2), width // 2)
                pair_in[i, pl.ds(core * rows, rows)] = ref[0, :, half]
            for j in range(n - 1):
                refs[j][i] = ref[1 + j]

    shapes = [(VMEM, (2, 2 * rows, width // 2), BF16)] + [(VMEM, (2, rows, width), BF16)] * (n - 1)
    return call(run, [(VMEM, own), (VMEM, moved)], shapes, [], "pairs")


def load_in(layer, sources, scratch, copies):
    if len(sources) == 1:
        width = scratch.shape[2]
        return [[copies.start(sources[0].at[:, pl.ds(i * width, width)], scratch.at[i])] for i in range(2)]
    own, other, along, one, two, far = sources
    spot = Spot()
    rows, width = own.shape[1], along.shape[2]
    pairs = []
    for pair in range(2):
        started = []
        for side in range(2):
            turn = 2 * pair + side
            columns = pl.ds(side * width, width)
            block = spot.block(turn)
            source = (one, far, two, along)[turn]
            for apart in range(1, spot.chips):
                chip = spot.chip ^ apart
                target = scratch.at[pair, rows_at(chip * 2 * rows, 2 * rows), columns]
                started.append(copies.start(source.at[apart - 1], target))
            for core, ref, index in (
                (spot.core, own, rows_at((2 * block + spot.core) * width, width)),
                (1 - spot.core, other, rows_at(block * width, width)),
            ):
                target = scratch.at[pair, rows_at((2 * spot.chip + core) * rows, rows), columns]
                started.append(copies.start(ref.at[layer, :, index], target))
        pairs.append(started)
    return pairs


def load_out(layer, sources, scratch, copies):
    if len(sources) == 1:
        return [copies.start(sources[0], scratch)]
    own, along, one, two, far = sources
    spot = Spot()
    shard, rows = own.shape[1], along.shape[1]
    started = []
    for apart in range(spot.chips):
        chip = spot.chip ^ apart
        start = spot.turn_of(chip) * shard
        if apart == 0:
            started.append(copies.start(own.at[layer], scratch.at[rows_at(start, shard), :]))
            continue
        for turn, source in enumerate((one, far, two, along)):
            part = pl.ds(pl.multiple_of(start + spot.block(turn) * rows, rows), rows)
            started.append(copies.start(source.at[apart - 1], scratch.at[part, :]))
    return started


class Scatter:
    def __init__(self, place, name, first, rest, by_rows):
        self.place, self.name, self.rest, self.by_rows = place, name, rest, by_rows
        self.chips, self.unit = rest.shape[1], rest.shape[2:]
        self.from_one = place.plane_one(first)
        self.small = None

    def move(self, stage, terms, sent):
        rows, width = self.unit
        extra, height = None, sent * rows
        if self.small is not None:
            self.small_rows = self.small[0][1].size
            terms_small = [(array, (at,)) for array, at in self.small]
            target = (0, (pl.ds(height, self.small_rows),))
            extra = (terms_small, (self.small_rows, width), target)
            height += self.small_rows
        targets = [(0, (pl.ds(i * rows, rows),)) for i in range(sent)]
        name = stage + "_" + self.name
        (made,) = move(name, terms, self.unit, [(height, width)], targets, extra)
        return made

    def heard(self, sent, received, count):
        if self.small is not None:
            at = pl.ds(count * self.unit[0], self.small_rows)
            self.small = [(sent, at), (received, at)]

    def part(self, i):
        return (pl.ds(i * self.unit[0], self.unit[0]),)

    def two(self):
        terms = [
            (self.rest, [(0, i) for i in range(self.chips)]),
            (self.from_one, [(1, i) for i in range(self.chips)]),
        ]
        second = self.move("two", terms, self.chips)
        self.from_two = self.place.plane_two(second)
        self.heard(second, self.from_two, self.chips)
        return second

    def own_terms(self, aparts):
        return [
            (self.rest, [(1, i) for i in aparts]),
            (self.from_one, [(0, i) for i in aparts]),
            (self.from_two, [self.part(i) for i in aparts]),
        ]

    def three(self):
        pair = self.move("three", self.own_terms([2, 3]), 2)
        self.from_pair = self.place.along_z(pair, 2)
        self.heard(pair, self.from_pair, 2)
        return pair

    def neighbour(self):
        terms = self.own_terms([1]) + [(self.from_pair, [self.part(1)])]
        piece = self.move("next", terms, 1)
        self.from_next = self.place.along_z(piece, 1)
        self.heard(piece, self.from_next, 1)
        return piece

    def four(self):
        if self.by_rows:
            terms = self.own_terms([0]) + [
                (self.from_pair, [self.part(0)]),
                (self.from_next, [self.part(0)]),
            ]
            (self.sum,) = move(
                "four_" + self.name, terms, self.unit, [self.unit], [(0, ())]
            )
            return self.sum
        rows, width = self.unit[0] // 2, self.unit[1]
        parts = [
            lambda spot: (rows_at(spot.core * rows, rows),),
            lambda spot: (rows_at((1 - spot.core) * rows, rows),),
        ]

        def of(head):
            return [lambda spot, part=part: head + part(spot) for part in parts]

        terms = [
            (self.rest, of((1, 0))),
            (self.from_one, of((0, 0))),
            (self.from_two, of(())),
            (self.from_pair, of(())),
            (self.from_next, of(())),
        ]
        targets, extra, height = [(0, ()), (1, (pl.ds(0, rows),))], None, rows
        if self.small is not None:
            height += self.small_rows
            terms_small = [(array, (at,)) for array, at in self.small]
            extra = (terms_small, (self.small_rows, width), (1, (pl.ds(rows, self.small_rows),)))
        self.kept, self.given = move(
            "four_" + self.name, terms, (rows, width), [(rows, width), (height, width)], targets, extra
        )
        self.from_core = self.place.swap_core(self.given)
        return self.kept


def join(name, scatters):
    given = []
    for scatter in scatters:
        given += [scatter.sum] if scatter.by_rows else [scatter.kept, scatter.from_core]
    rows, width = scatters[0].kept.shape
    half, width = width, 2 * width
    with_small = [scatter for scatter in scatters if scatter.small is not None]
    given += [scatter.given for scatter in with_small]
    small_rows = with_small[0].small_rows // 2 if with_small else 0
    count = len(scatters)

    def run(*refs):
        ins, out = list(refs[: len(given)]), refs[len(given)]
        spot = Spot()

        def small(ref, at):
            for i in range(2):
                part = ref[pl.ds(rows + i * small_rows, small_rows)]
                out[pl.ds(at, small_rows), pl.ds(i * half, half)] = part

        for i, scatter in enumerate(scatters):
            part = pl.ds(i * rows, rows)
            if scatter.by_rows:
                out[part] = ins.pop(0)[...]
                continue
            for turn, core in enumerate((spot.core, 1 - spot.core)):
                ref = ins.pop(0)
                out[part, rows_at(core * half, half)] = ref[pl.ds(0, rows)]
                if turn == 1 and scatter.small is not None:
                    small(ref, count * rows + small_rows)
        for ref in ins:
            small(ref, count * rows)

    whole = ((count * rows + 2 * small_rows, width), BF16)
    (joined,) = call(run, [(VMEM, array) for array in given], [(VMEM,) + whole], [], name)
    return joined


def collect_kernel(group, turns, n_started, *refs):
    arrays, refs = refs[: len(turns)], refs[len(turns) + n_started :]
    (*outs, held, high, copies) = refs
    spot = Spot()
    rows, width = held.shape[1:]
    parts = []
    for i, (layer, by_rows) in enumerate(group):
        part = pl.ds(i * rows, rows)
        for source, turn in zip(arrays, turns):
            quarter = spot.block(turn)
            if by_rows:
                target = outs[1].at[layer, rows_at(quarter * rows, rows), :]
            else:
                target = outs[0].at[layer, :, rows_at(quarter * width, width)]
            parts.append((copies.start(source.at[part], held.at[len(parts)]), target))
    leaving = []
    for i, (copy, target) in enumerate(parts):
        copy.wait()
        high[i] = held[i].astype(F32)
        leaving.append(copies.start(high.at[i], target))
    return leaving


def norm(values):
    center = jnp.mean(values, axis=-1, keepdims=True)
    offsets = values - center
    inverse = lax.rsqrt(jnp.mean(offsets * offsets, axis=-1, keepdims=True) + 1e-05)
    return offsets * inverse, inverse


def norm_back(upstream, unit, inverse, gain):
    scaled = upstream * gain
    center = jnp.mean(scaled, axis=-1, keepdims=True)
    along = jnp.mean(scaled * unit, axis=-1, keepdims=True)
    return inverse * (scaled - center - unit * along)


def gelu_both(v):
    scale = math.sqrt(2.0 / math.pi)
    square = v * v
    half = 0.5 + 0.5 * jnp.tanh(v * (scale + (scale * 0.044715) * square))
    spread = (2.0 * half) * (1.0 - half)
    return v * half, half + (v * spread) * (scale + (3.0 * scale * 0.044715) * square)


def mix_forward(rows, hid, seq, gain, shift, real, imag, outs):
    unit, inverse, normed_low = outs
    hid_cos, hid_sin = hid[0](), hid[1]()

    @row_steps(rows.shape[0])
    def _(at):
        real[at, :] = dot(rows[at, :], hid_cos[...]).astype(BF16)
        imag[at, :] = dot(rows[at, :], hid_sin[...]).astype(BF16)

    seq_cos, seq_sin = seq[0](), seq[1]()

    @row_steps(rows.shape[0])
    def _(at):
        mixed = dot(seq_cos[at, :], real[...]) - dot(seq_sin[at, :], imag[...])
        unit_rows, inverse_rows = norm(rows[at, :].astype(F32) + mixed)
        unit.buffer[at, :] = unit_rows
        inverse[at, :] = inverse_rows
        normed_low.buffer[at, :] = (unit_rows * gain[...] + shift[...]).astype(BF16)
        normed_low.push(at)
        unit.push(at)


def first_mix_kernel(numbers, boundary, received, hid_cos, hid_sin, cos_tiles, sin_tiles, gain, shift, *refs):
    seq_cos, seq_sin = refs[0:2]
    outs, (rows, real, imag, copies) = refs[2:5], refs[5:]
    chosen = choose(copies, boundary.at[0, pl.ds(0, rows.shape[0])], received, rows)
    cos_tiles, sin_tiles = cos_tiles(), sin_tiles()
    base = cos_tiles.shape[1]
    slots = seq_cos.buffer.shape[0] // base
    for i in range(slots):
        for j in range(slots):
            window = (pl.ds(i * base, base), pl.ds(j * base, base))
            number = numbers[i * slots + j]
            seq_cos.buffer[window] = cos_tiles[number]
            seq_sin.buffer[window] = sin_tiles[number]
    seq_cos.push()
    seq_sin.push()
    seq = (lambda: seq_cos.buffer, lambda: seq_sin.buffer)
    chosen.wait()
    mix_forward(rows, (hid_cos, hid_sin), seq, gain, shift, real, imag, outs)


def expand_kernel(layer, by_permutes, n_sources, normed, other_normed, b_in, *refs):
    sources, (hidden, slope, whole, copies) = refs[:n_sources], refs[n_sources:]
    scratch = whole.buffer
    loaded = load_in(layer, sources, scratch, copies)
    spot = Spot(by_permutes)
    width = scratch.shape[2]
    count = normed.buffer.shape[0]
    for pair in range(2):
        biases = [b_in[:, rows_at(spot.block(2 * pair + i) * (width // 2), width // 2)] for i in range(2)]
        bias = jnp.concatenate(biases, axis=1)
        for copy in loaded[pair]:
            copy.wait()
        whole.push(pair)
        for place, rows in enumerate((normed, other_normed)):
            rows = rows()

            @row_steps(count)
            def _(at):
                value, rate = gelu_both(dot(rows[at, :], scratch[pair]) + bias)
                to = pl.ds(place * count + at.start, at.size)
                hidden.buffer[pair, to, :] = value.astype(BF16)
                slope.buffer[pair, to, :] = rate.astype(BF16)

        hidden.push(pair)
        slope.push(pair)


def contract_kernel(layer, n_sources, hidden, *refs):
    sources, (own, other, whole, copies) = refs[:n_sources], refs[n_sources:]
    scratch = whole.buffer
    loaded = load_out(layer, sources, scratch, copies)
    count, width = own.buffer.shape[0], hidden.buffer.shape[2]
    for copy in loaded:
        copy.wait()
    whole.push()
    for place, out in ((1, other), (0, own)):

        @row_steps(count)
        def _(at):
            rows = pl.ds(place * count + at.start, at.size)
            hidden(1)
            held = hidden.buffer
            total = dot(held[0, rows, :], scratch[0:width, :]) + dot(held[1, rows, :], scratch[width:, :])
            out.buffer[at, :] = total.astype(out.buffer.dtype)
            out.push(at)


def second_norm(at, own, received, unit_one, gain_one, shift_one, b_out):
    normed = unit_one[at, :] * gain_one[...] + shift_one[...]
    return norm(normed + (own[at, :] + received[at, :].astype(F32) + b_out[...]))


def middle_kernel(own, received, unit_one, gain_one, shift_one, b_out, gain_two, shift_two, *refs):
    hid, seq, (next_gain, next_shift) = refs[:2], refs[2:4], refs[4:6]
    unit_two, inverse_two = refs[6:8]
    outs, (mid, real, imag, _) = refs[8:11], refs[11:]
    own, received, unit_one = own(), received(), unit_one()

    @row_steps(mid.shape[0])
    def _(at):
        unit, inverse = second_norm(at, own, received, unit_one, gain_one, shift_one, b_out)
        unit_two.buffer[at, :] = unit
        inverse_two[at, :] = inverse
        mid[at, :] = (unit * gain_two[...] + shift_two[...]).astype(BF16)

    unit_two.push()
    mix_forward(mid, hid, seq, next_gain, next_shift, real, imag, outs)


def second_back(at, upstream, unit, inverse, gain, d_second, branch_grad, small):
    grad = norm_back(upstream, unit, inverse, gain[...])
    low = grad.astype(BF16)
    branch_grad.buffer[at, :] = low
    branch_grad.push(at)
    d_second.buffer[at, :] = grad
    d_second.push(at)
    small[0:1, :] += column_sum(low.astype(F32))
    small[1:2, :] += column_sum(upstream * unit)
    small[2:3, :] += column_sum(upstream)


def turn_kernel(own, received, unit_one, gain_one, shift_one, b_out, gain_two, shift_two, *refs):
    boundary, given, out_rows, d_second, branch_grad, small, cotangent, copies = refs
    count = cotangent.shape[0]
    chosen = choose(copies, given, boundary.at[0, pl.ds(count, count)], cotangent)
    own, received, unit_one = own(), received(), unit_one()
    small[...] = jnp.zeros_like(small)
    chosen.wait()

    @row_steps(own.shape[0])
    def _(at):
        unit, inverse = second_norm(at, own, received, unit_one, gain_one, shift_one, b_out)
        out_rows.buffer[at, :] = (unit * gain_two[...] + shift_two[...]).astype(BF16)
        upstream = cotangent[at, :].astype(F32)
        second_back(at, upstream, unit, inverse, gain_two, d_second, branch_grad, small)
        out_rows.push(at)


def grad_out_kernel(by_permutes, hidden, branch_grad, other_grad, *refs):
    outs, (tiles, copies) = refs[:-2], refs[-2:]
    spot = Spot(by_permutes)
    count = branch_grad.shape[0]
    shard = tiles.shape[1]
    for turn in range(BLOCKS):
        columns = pl.ds((turn % 2) * shard, shard)
        grad = 0.0
        for i, ref in enumerate((branch_grad, other_grad)):
            rows = hidden[turn // 2, pl.ds(i * count, count), columns]
            grad = grad + dot(rows, ref[...], ((0,), (0,)))
        if not by_permutes:
            outs[0][pl.ds(turn * shard, shard), :] = grad.astype(BF16)
            continue
        tiles[turn] = grad.astype(BF16)
        rows = outs[0].shape[2]
        apart = spot.block(turn) ^ spot.chip
        for slot in range(BLOCKS):
            part = tiles[turn, rows_at(spot.block(slot) * rows, rows), :]
            outs[slot // 2][slot % 2, apart] = part


def shrink_kernel(by_permutes, n_outs, branch_grad, other_grad, slope, normed, other_normed, whole_out, whole_in, *refs):
    outs, (b_grad, own, other, tiles, act_grad, copies) = refs[:n_outs], refs[n_outs:]
    spot = Spot(by_permutes)
    count = branch_grad.shape[0]
    width = tiles.shape[2]
    half = width // 2
    b_grad[...] = jnp.zeros_like(b_grad)
    for pair in range(2):
        sums = []
        for place, ref in enumerate((branch_grad, other_grad)):

            @row_steps(count)
            def _(at):
                rows = pl.ds(place * count + at.start, at.size)
                grad = dot(ref[at, :], whole_out[pl.ds(pair * width, width), :], ((1,), (1,)))
                low = (grad * slope[pair, rows, :].astype(F32)).astype(BF16)
                act_grad[pair, rows, :] = low
                sums.append(column_sum(low.astype(F32)))

        total = sum(sums[1:], sums[0])
        for side in range(2):
            block = spot.block(2 * pair + side)
            b_grad[:, rows_at((2 * block + spot.core) * half, half)] = total[:, side * half : (side + 1) * half]

        @row_steps(tiles.shape[1])
        def _(at):
            grad = 0.0
            for place, ref in enumerate((normed, other_normed)):
                grads = act_grad[pair, pl.ds(place * count, count), :]
                grad = grad + dot(ref[:, at], grads, ((0,), (0,)))
            if by_permutes:
                tiles[pair, at, :] = grad.astype(BF16)
            else:
                outs[0][at, pl.ds(pair * width, width)] = grad.astype(BF16)

        if by_permutes:
            rows = outs[0].shape[2]
            for side in range(2):
                for chip in range(spot.chips):
                    part = tiles[pair, pl.ds(chip * rows, rows), pl.ds(side * half, half)]
                    outs[pair][side, chip ^ spot.chip] = part
    for place, out in ((1, other), (0, own)):

        @row_steps(count)
        def _(at):
            rows = pl.ds(place * count + at.start, at.size)
            total = dot(act_grad[0, rows, :], whole_in[0], ((1,), (1,)))
            total = total + dot(act_grad[1, rows, :], whole_in[1], ((1,), (1,)))
            out[at, :] = total.astype(out.dtype)


def unmix(refs, total, mix_grad, real, imag, small, input_grad):
    own, received, d_second, unit_one, inverse_one, gain_one, hid_cos, hid_sin, seq_cos, seq_sin = refs
    own, received, d_second, unit_one = own(), received(), d_second(), unit_one()
    small[...] = jnp.zeros_like(small)

    @row_steps(total.shape[0])
    def _(at):
        upstream = d_second[at, :] + own[at, :] + received[at, :].astype(F32)
        unit = unit_one[at, :]
        grad = norm_back(upstream, unit, inverse_one[at, :], gain_one[...])
        total[at, :] = grad
        mix_grad[at, :] = grad.astype(BF16)
        small[0:1, :] += column_sum(upstream * unit)
        small[1:2, :] += column_sum(upstream)

    seq_cos, seq_sin = seq_cos(), seq_sin()

    @row_steps(total.shape[0])
    def _(at):
        real[at, :] = dot(seq_cos[at, :], mix_grad[...]).astype(BF16)
        imag[at, :] = (-dot(seq_sin[at, :], mix_grad[...])).astype(BF16)

    hid_cos, hid_sin = hid_cos(), hid_sin()

    @row_steps(total.shape[0])
    def _(at):
        grad = dot(real[at, :], hid_cos[...]) + dot(imag[at, :], hid_sin[...])
        input_grad(at, total[at, :] + grad)


def last_kernel(*refs):
    ins, (out_rows, *smalls) = refs[:10], refs[10:17]
    sent, kept, packed, total, mix_grad, real, imag, small, _ = refs[17:]
    is_first = lax.axis_index("section") % 2 == 0
    rows = out_rows()

    def input_grad(at, values):
        low = values.astype(BF16)
        sent.buffer[at, :] = jnp.where(is_first, rows[at, :], low)
        kept.buffer[at, :] = jnp.where(is_first, low, rows[at, :])
        sent.push(at)
        kept.push(at)

    unmix(ins, total, mix_grad, real, imag, small, input_grad)
    width = packed.shape[1]
    packed[...] = jnp.zeros_like(packed)
    for layer in range(2):
        b_grad, sums_two = smalls[3 * layer : 3 * layer + 2]
        sums_one = smalls[3 * layer + 2] if layer else small
        at = layer * (packed.shape[0] // 2)
        sums = (sums_two[0:1], sums_one[0:1], sums_one[1:2], sums_two[1:2], sums_two[2:3])
        for vector in (b_grad[...],) + sums:
            for i in range(vector.shape[1] // width):
                packed[at : at + 1, :] = vector[:, i * width : (i + 1) * width].astype(packed.dtype)
                at += 1


def finish_kernel(kept, back, result, held, high, copies):
    layer = lax.axis_index("section") % 2
    count = held.shape[1]
    arriving = [copies.start(ref, held.at[i]) for i, ref in enumerate((kept, back))]
    leaving = []
    for i, block in enumerate((layer, 1 - layer)):
        arriving[i].wait()
        high[i] = held[i].astype(F32)
        leaving.append(copies.start(high.at[i], result.at[0, rows_at(block * count, count)]))
    return leaving


def relay_kernel(*refs):
    ins, (unit_two, inverse_two, gain_two) = refs[:10], refs[10:13]
    small, d_second, branch_grad, small_two, total, mix_grad, real, imag, _ = refs[13:]
    small_two[...] = jnp.zeros_like(small_two)

    def input_grad(at, values):
        upstream = values.astype(BF16).astype(F32)
        unit = unit_two()[at, :]
        second_back(at, upstream, unit, inverse_two[at, :], gain_two, d_second, branch_grad, small_two)

    unmix(ins, total, mix_grad, real, imag, small, input_grad)


def body(boundary, bucket_ids, w_in, b_in, w_out, b_out, gain_one, shift_one, gain_two, shift_two):
    place = Place()
    Order.begin()
    layers = w_in.shape[0]
    micro_count = bucket_ids.shape[1]
    feat_width = boundary.shape[2]
    ff_width = w_in.shape[2]
    slab_len = boundary.shape[1] // micro_count
    slots = bucket_ids.shape[2]
    base_len = slab_len // slots
    half_block = ff_width // (2 * BLOCKS)
    by_permutes = place.n_section == 4 and place.chips == 4
    last = layers - 1

    bucket_row = bucket_ids[place.section // 2, place.section % 2]
    half_bias = lax.dynamic_index_in_dim(
        b_in.reshape(layers, BLOCKS, 2, half_block), place.core, 2, keepdims=False
    ).reshape(layers, -1)

    block = (slab_len, feat_width)
    both = (2 * slab_len, feat_width)
    wide_block = (2, 2 * slab_len, ff_width // 4)
    whole_in_shape = (2, feat_width, ff_width // 4)
    whole_out_shape = (ff_width // 2, feat_width)
    column = (VMEM, (slab_len, 1), F32)
    sums_shape = (VMEM, (8, feat_width), F32)
    mix_outs = [(EARLY, block, F32), column, (EARLY, block, BF16)]
    hid = [(LATE, jnp.asarray(table.astype(BF16))) for table in dft_tables(feat_width)]

    def late(*arrays):
        return [(LATE, array) for array in arrays]

    def param(array, layer):
        return (VMEM, array[layer][None])

    shard_rows, piece_rows = w_in.shape[1], w_out.shape[1] // BLOCKS
    prepared = [(HBM, block, BF16)]
    if by_permutes:
        prepared += [(HBM, (layers, shard_rows, ff_width // 2), BF16)]
        prepared += [(HBM, (piece_rows, feat_width), BF16)] * layers
    given, *prepared = call(
        partial(prepare_kernel, layers, by_permutes),
        plain(boundary, w_in, w_out),
        prepared,
        [
            (block, BF16),
            ((layers, shard_rows, ff_width // 2), BF16),
            ((layers, piece_rows, feat_width), BF16),
        ],
        "prepare",
        spare=54 * 2**20,
    )
    sources_in, sources_out = [None] * layers, [None] * layers
    if by_permutes:
        for_other, out_zero_piece, out_one_piece = prepared
        in_zero, out_zero, in_one, out_one = (
            Gather(place, name + str(layer), w, None, layer, by_rows)
            for layer in range(layers)
            for name, w, by_rows in (("in", w_in, False), ("out", w_out, True))
        )
        other_rows = place.swap_core(for_other)
        received = place.swap_layer(given)
        in_zero.other_rows = in_one.other_rows = other_rows
        in_zero.shift(in_zero.join(other_rows))
        own_pieces = in_one.join(other_rows, (out_zero_piece, out_one_piece))
        moved_pieces = place.along_z(own_pieces, 1)
        Order.wait(received)
        in_zero.one()
        pair_in, pair_zero, pair_one = pairs(own_pieces, moved_pieces)
        out_zero.moved = [(pair_zero, 1, 1), place.along_z(pair_zero, 2)]
    else:
        received = place.swap_layer(given)
        for layer in range(layers):
            whole_in, whole_out = (
                lax.all_gather(w[layer], "dp", axis=0, tiled=True) for w in (w_in, w_out)
            )
            whole_in = whole_in.reshape(feat_width, BLOCKS, 2, half_block)
            whole_out = whole_out.reshape(BLOCKS, 2, half_block, feat_width)
            whole_in = lax.dynamic_index_in_dim(whole_in, place.core, 2, keepdims=False)
            whole_out = lax.dynamic_index_in_dim(whole_out, place.core, 1, keepdims=False)
            sources_in[layer] = [whole_in.reshape(feat_width, -1)]
            sources_out[layer] = [whole_out.reshape(-1, feat_width)]

    numbers = tile_numbers(bucket_row, slots).reshape(-1)
    tiles = [(LATE, jnp.asarray(table)) for table in sequence_tiles(base_len)]
    seq_cos, seq_sin, *mixed = call(
        first_mix_kernel,
        [(SMEM, numbers)]
        + plain(boundary, received)
        + hid
        + tiles
        + [param(gain_one, 0), param(shift_one, 0)],
        [(EARLY, (slab_len, slab_len), BF16)] * 2 + mix_outs,
        [(block, BF16)] * 3,
        "first_mix",
    )
    tables = hid + late(seq_cos, seq_sin)

    both_pairs, all_rows = pl.ds(0, 2), pl.ds(0, 2 * slab_len)
    steps = slab_len // ROW_STEP
    row_parts = [
        (both_pairs, pl.ds(slab_len * place_ + i * ROW_STEP, ROW_STEP))
        for place_ in (1, 0)
        for i in range(steps)
    ]
    block_parts = [
        (pair, all_rows, pl.ds(side * half_block, half_block)) for pair in range(2) for side in range(2)
    ]
    pair_parts = [(pl.ds(pair, 1),) for pair in range(2)]
    half_parts = [(pl.ds(pair * 2 * half_block, 2 * half_block),) for pair in range(2)]

    saved, wholes_in, wholes_out = [], [], []
    for layer in range(layers):
        unit_one, inverse_one, normed = mixed
        if by_permutes and layer == 0:
            mark = Order.mark(in_zero.from_one, in_zero.from_two)
            in_zero.two(mark)
            other_normed = place.swap_core(tie(normed, mark))
            out_zero.one()
            in_one.moved = [(pair_in, 1, 1), place.along_z(tie(pair_in, out_zero.along), 2)]
            sources_in[0] = in_zero.sources()
        else:
            other_normed = place.swap_core(normed)
        if by_permutes and layer == 1:
            Order.mark(in_one.far, cost=FAR_MARK_COST)
            mark = Order.mark(out_one.from_one, out_one.from_two, cost=NEAR_MARK_COST)
            out_one.two(mark)
            sources_in[1] = in_one.sources()
        hidden, slope, whole_in = call(
            partial(expand_kernel, layer, by_permutes, len(sources_in[layer])),
            late(normed, other_normed)
            + [(VMEM, half_bias[layer][None])]
            + plain(*sources_in[layer]),
            [(EARLY, wide_block, BF16), (EARLY, wide_block, BF16), (EARLY, whole_in_shape, BF16)],
            [],
            "expand",
        )
        if by_permutes and layer == 0:
            mark = Order.mark(out_zero.from_one, out_zero.from_two)
            out_zero.two(mark)
            in_one.one()
            out_one.moved = [(pair_one, 1, 1), place.along_z(tie(pair_one, mark), 2)]
            sources_out[0] = out_zero.sources()
        if by_permutes and layer == 1:
            sources_out[1] = out_one.sources()
        own_part, other_part, whole_out = call(
            partial(contract_kernel, layer, len(sources_out[layer])),
            [(LATE, hidden, row_parts)] + plain(*sources_out[layer]),
            [(EARLY, block, F32), (EARLY, block, BF16), (EARLY, whole_out_shape, BF16)],
            [],
            "contract",
        )
        from_other = place.swap_core(other_part)
        if by_permutes and layer == 0:
            mark = Order.mark(in_one.from_one, in_one.from_two)
            in_one.two(mark)
            out_one.one()
        wholes_in.append(whole_in)
        wholes_out.append(whole_out)
        common = late(own_part, from_other, unit_one) + [
            param(p, layer) for p in (gain_one, shift_one, b_out, gain_two, shift_two)
        ]
        kept = [unit_one, inverse_one, normed, other_normed, hidden, slope]
        if layer < last:
            unit_two, inverse_two, *mixed = call(
                middle_kernel,
                common + tables + [param(gain_one, layer + 1), param(shift_one, layer + 1)],
                [(EARLY, block, F32), column] + mix_outs,
                [(block, BF16), (block, BF16), (block, BF16)],
                "middle",
                cost=MIDDLE_COST,
            )
            kept += [unit_two, inverse_two]
        saved.append(kept)

    out_rows, d_second, branch_grad, sums_two = call(
        turn_kernel,
        common + plain(boundary, received),
        [(EARLY, block, BF16), (EARLY, block, F32), (EARLY, block, BF16), sums_shape],
        [(block, BF16)],
        "turn",
    )

    if by_permutes:
        piece_out = (2, place.chips, w_out.shape[1] // BLOCKS, feat_width)
        piece_in = (2, place.chips, 2 * w_in.shape[1], half_block)
        grad_outs = {True: [(VMEM, piece_out, BF16)] * 2, False: [(VMEM, piece_in, BF16)] * 2}
    else:
        grad_outs = {
            True: [(VMEM, (ff_width // 2, feat_width), BF16)],
            False: [(VMEM, (feat_width, ff_width // 2), BF16)],
        }
    n_outs = len(grad_outs[True])
    grads, smalls, running = {}, {}, []

    def reduce_grad(pieces, layer, by_rows):
        name = ("out" if by_rows else "in") + str(layer)
        if by_permutes:
            grads[layer, by_rows] = Scatter(place, name, *pieces, by_rows)
            running.append(grads[layer, by_rows])
            return
        (half,) = pieces
        if by_rows:
            whole = jnp.zeros((BLOCKS, 2, half_block, feat_width), BF16)
            half = half.reshape(BLOCKS, 1, half_block, feat_width)
            whole = lax.dynamic_update_slice_in_dim(whole, half, place.core, 1)
            whole = whole.reshape(ff_width, feat_width)
        else:
            whole = jnp.zeros((feat_width, BLOCKS, 2, half_block), BF16)
            half = half.reshape(feat_width, BLOCKS, 1, half_block)
            whole = lax.dynamic_update_slice_in_dim(whole, half, place.core, 2)
            whole = whole.reshape(feat_width, ff_width)
        part = lax.psum_scatter(whole, "dp", scatter_dimension=0, tiled=True)
        grads[layer, by_rows] = lax.psum(part, "section").astype(F32)

    for layer in reversed(range(layers)):
        unit_one, inverse_one, normed, other_normed, hidden, slope = saved[layer][:6]
        other_grad = place.swap_core(branch_grad)
        if by_permutes and layer == 0:
            running[0].two()
            running[1].two()
        pieces = call(
            partial(grad_out_kernel, by_permutes),
            [(VMEM, hidden), (VMEM, branch_grad), (VMEM, other_grad)],
            grad_outs[True],
            [((BLOCKS, half_block, feat_width), BF16)],
            "grad_out",
        )
        reduce_grad(pieces, layer, True)
        if by_permutes and layer == 0:
            running[0].three()
            Order.mark(running[1].from_two)
        *pieces, b_grad, own_part, other_part = call(
            partial(shrink_kernel, by_permutes, n_outs),
            [
                (VMEM, array)
                for array in (branch_grad, other_grad, slope, normed, other_normed)
                + (wholes_out[layer], wholes_in[layer])
            ],
            grad_outs[False]
            + [(VMEM, (1, ff_width), F32), (VMEM, block, F32), (VMEM, block, BF16)],
            [((2, feat_width, ff_width // 4), BF16), (wide_block, BF16)],
            "shrink",
        )
        from_other = place.swap_core(other_part)
        reduce_grad(pieces, layer, False)
        if by_permutes and layer == last:
            Order.mark(running[0].from_one)
        if by_permutes and layer == 0:
            running[0].neighbour()
            running[2].two()
            running[1].three()
        ins = (
            late(own_part, from_other, d_second, unit_one)
            + [(VMEM, inverse_one), param(gain_one, layer)]
            + tables
        )
        work = [(block, F32), (block, BF16), (block, BF16), (block, BF16)]
        smalls[layer] = [b_grad, sums_two]
        if layer > 0:
            below_unit, below_inverse = saved[layer - 1][6:8]
            sums_one, d_second, branch_grad, sums_two = call(
                relay_kernel,
                ins + late(below_unit) + [(VMEM, below_inverse), param(gain_two, layer - 1)],
                [sums_shape, (EARLY, block, F32), (EARLY, block, BF16), sums_shape],
                work,
                "relay",
            )
            smalls[layer].append(sums_one)
    vectors = smalls[0] + [smalls[1][2]] + smalls[1]
    small_type = BF16 if by_permutes else F32
    sent, kept_rows, packed = call(
        last_kernel,
        ins + late(out_rows) + [(VMEM, vector) for vector in vectors],
        [(EARLY, block, BF16), (EARLY, block, BF16), (VMEM, (64, half_block), small_type)],
        work + [((8, feat_width), F32)],
        "last",
    )

    def finish():
        return call(
            finish_kernel,
            plain(kept_rows, back),
            [(HBM, (1, 2 * slab_len, feat_width), F32)],
            [((2,) + block, BF16), ((2,) + block, F32)],
            "finish",
        )

    if by_permutes:

        def share(mine):
            return [place.plane_one(mine), place.plane_two(mine)]

        out_last, in_last, out_first, in_first = running
        in_first.small = [(packed, pl.ds(0, packed.shape[0]))]
        out_first.three()
        in_first.two()
        out_last.four()
        in_last.neighbour()
        in_first.three()
        back = place.swap_layer(tie(sent, Order.token))
        in_last.four()
        out_first.neighbour()
        in_first.neighbour()
        (result,) = finish()
        mine = join("join_rest", [in_last, out_last])
        rest = share(mine)
        out_first.four()
        in_first.four()
        rest.append(place.plane_two(tie(rest[0], Order.token)))
        Order.wait(rest[1])
        last_mine = join("join_last", [in_first, out_first])
        last_rest = share(last_mine)
        groups = [[(last, False), (last, True)], [(0, False), (0, True)]]
        unit = (shard_rows, ff_width // BLOCKS)

        def collect(group, quarters, started):
            turns, arrays = zip(*quarters)
            held = ((len(turns) * len(group),) + unit,)
            n = len(turns)
            return call(
                partial(collect_kernel, group, turns, len(started)),
                plain(*arrays, *started),
                [(HBM, w_in.shape, F32), (HBM, w_out.shape, F32)],
                [held + (BF16,), held + (F32,)],
                "collect",
                aliases={n: 0, n + 1: 1} if started else None,
            )

        Order.wait(rest[2])
        started = collect(groups[0], zip((3, 0, 2, 1), [mine] + rest), ())
        mark = Order.mark(*last_rest)
        far = place.plane_two(tie(last_rest[0], mark))
        started = collect(groups[1], zip((3, 0, 2), [last_mine] + last_rest), tuple(started))
        at, size = 2 * shard_rows, (last_mine.shape[0] - 2 * shard_rows) // 2
        packed = sum(
            array[at + i * size : at + (i + 1) * size].astype(F32)
            for i, arrays in enumerate(((last_mine, last_rest[0]), (last_mine, last_rest[1])))
            for array in arrays
        )
        packed = packed.reshape(-1, 2, half_block).transpose(1, 0, 2).reshape(-1, half_block)
        packed = tie(packed, Order.token)
        Order.wait(packed)
        grad_in, grad_out = collect(groups[1], [(1, far)], tuple(started))
    else:
        back = place.swap_layer(sent)
        grad_in, grad_out = (
            jnp.stack([grads[layer, by_rows] for layer in range(layers)])
            for by_rows in (False, True)
        )
        packed = lax.psum(packed, AXES)
        (result,) = finish()
    b_part, part = ff_width // place.n_dp, feat_width // place.n_dp
    flat = packed.reshape(layers, -1)
    small_out = [lax.dynamic_slice_in_dim(flat, place.dp * b_part, b_part, 1)]
    sums = flat[:, ff_width : ff_width + 5 * feat_width].reshape(layers, 5, feat_width)
    sums = lax.dynamic_slice_in_dim(sums, place.dp * part, part, 2)
    small_out += [sums[:, i] for i in range(5)]
    return (result, grad_in, small_out[0], grad_out, *small_out[1:])


def solution(mesh):
    return jax.shard_map(
        body,
        mesh=mesh,
        in_specs=(
            P("section", "dp", None),
            P(None, "dp", None),
            P(None, "dp", None),
            P(),
            P(None, "dp", None),
            P(),
            P(),
            P(),
            P(),
            P(),
        ),
        out_specs=(
            P("section", "dp", None),
            P(None, "dp", None),
            P(None, "dp"),
            P(None, "dp", None),
            P(None, "dp"),
            P(None, "dp"),
            P(None, "dp"),
            P(None, "dp"),
            P(None, "dp"),
        ),
        check_vma=False,
    )
```

```python
from functools import partial
import math

import jax
import jax.numpy as jnp
import numpy as np
from jax import lax
from jax.experimental import pallas as pl
from jax.experimental.pallas import tpu as pltpu
from jax.sharding import PartitionSpec as P

AXES = ("section", "dp")
F32 = jnp.float32
BF16 = jnp.bfloat16
BLOCKS = 4
EVENT_COST, SHORT_COST = 10**10, 10**9
FAR_MARK_COST, NEAR_MARK_COST, MIDDLE_COST = 2000000000, 4000000000, 100000000
ROW_STEP = 256

VMEM = pl.BlockSpec(memory_space=pltpu.VMEM)
SMEM = pl.BlockSpec(memory_space=pltpu.SMEM)
HBM = pl.BlockSpec(memory_space=pltpu.HBM)
LATE, EARLY = "late", "early"


class Place:
    def __init__(self):
        self.n_section = lax.axis_size("section")
        self.n_dp = lax.axis_size("dp")
        self.chips = self.n_dp // 2
        self.section = lax.axis_index("section")
        self.dp = lax.axis_index("dp")
        self.core = self.dp % 2

    def permute(self, value, target):
        pairs = []
        for section in range(self.n_section):
            for chip in range(self.chips):
                for core in range(2):
                    to_section, to_chip, to_core = target(section, chip, core)
                    source = section * self.n_dp + chip * 2 + core
                    pairs.append((source, to_section * self.n_dp + to_chip * 2 + to_core))
        return lax.ppermute(value, AXES, pairs)

    def swap_core(self, value):
        return self.permute(value, lambda s, z, c: (s, z, 1 - c))

    def swap_layer(self, value):
        return self.permute(value, lambda s, z, c: (s ^ 1, z, c))

    def plane_one(self, value):
        return self.permute(value, lambda s, z, c: (s ^ (1 + c), z, c))

    def plane_two(self, value):
        return self.permute(value, lambda s, z, c: (s ^ (2 - c), z, c))

    def along_z(self, value, flip):
        return self.permute(value, lambda s, z, c: (s, z ^ flip, c))


class Spot:
    def __init__(self, by_permutes=True):
        dp = lax.axis_index("dp")
        self.core = dp % 2
        if by_permutes:
            self.section, self.chip = lax.axis_index("section"), dp // 2
            self.chips = lax.axis_size("dp") // 2
            self.held = (1 + self.core, 3, 2 - self.core, 0)
        else:
            self.section, self.held = 0, (0, 1, 2, 3)

    def block(self, turn):
        return self.section ^ self.held[turn]

    def turn_of(self, block):
        flip = block ^ self.section
        side = jnp.where(flip == self.held[0], 0, 2)
        return jnp.where(flip == 3, 1, jnp.where(flip == 0, 3, side))


def dft_tables(length):
    positions = np.arange(length)
    angles = (positions[:, None] * positions[None, :] % length) * (2.0 * math.pi) / length
    scaling = 1.0 / math.sqrt(length)
    return (np.cos(angles) * scaling, np.sin(angles) * scaling)


def sequence_tiles(base_len):
    cos_tiles, sin_tiles = [], []
    for parts in (1, 2, 4):
        cos_table, sin_table = dft_tables(parts * base_len)
        for i in range(parts):
            for j in range(parts):
                window = (
                    slice(i * base_len, (i + 1) * base_len),
                    slice(j * base_len, (j + 1) * base_len),
                )
                cos_tiles.append(cos_table[window])
                sin_tiles.append(sin_table[window])
    cos_tiles.append(np.zeros((base_len, base_len)))
    sin_tiles.append(np.zeros((base_len, base_len)))
    return np.stack(cos_tiles).astype(BF16), np.stack(sin_tiles).astype(BF16)


def tile_numbers(bucket_row, slots):
    parts = jnp.where(bucket_row < 3, 1 << jnp.minimum(bucket_row, 2), 0)
    ends = jnp.cumsum(parts)
    where = jnp.arange(slots, dtype=jnp.int32)
    segment = jnp.sum((where[:, None] >= ends[None, :]).astype(jnp.int32), axis=1)
    one_hot = (segment[:, None] == jnp.arange(slots)[None, :]).astype(jnp.int32)
    start = jnp.sum(one_hot * (ends - parts)[None, :], axis=1)
    size = jnp.sum(one_hot * parts[None, :], axis=1)
    first = jnp.where(size == 1, 0, jnp.where(size == 2, 1, 5))
    place = where - start
    numbers = first[:, None] + place[:, None] * size[:, None] + place[None, :]
    return jnp.where(segment[:, None] == segment[None, :], numbers, 21)


def rows_at(start, size):
    return pl.ds(pl.multiple_of(start, size), size)


def dot(left, right, dims=((1,), (0,))):
    return lax.dot_general(left, right, (dims, ((), ())), preferred_element_type=F32)


def row_steps(count, step=ROW_STEP):
    step = step if count % step == 0 else count

    def run(function):
        for i in range(count // step):
            function(pl.ds(i * step, step))

    return run


def column_sum(values):
    return jnp.sum(values, axis=0, keepdims=True)


class Copies:
    def __init__(self, sems):
        self.sems, self.count = sems, 0

    def start(self, source, target):
        copy = pltpu.make_async_copy(source, target, self.sems.at[self.count])
        copy.start()
        self.count += 1
        return copy


class Late:
    def __init__(self, ref):
        self.buffer = ref

    def __call__(self, parts=None):
        return self.buffer


class Early:
    def __init__(self, ref):
        self.buffer, self.leaving = ref, []

    def push(self, part=None):
        pass


def tie(value, *others):
    return lax.optimization_barrier((value,) + others)[0]


class Order:
    token = None

    @classmethod
    def begin(cls):
        cls.token = jnp.zeros((8, 128), F32)

    @classmethod
    def wait(cls, *arrays):
        cls.token = tie(cls.token, *arrays)

    @classmethod
    def mark(cls, *arrays, cost=EVENT_COST):
        cls.wait(*arrays)
        call(lambda *refs: None, [], [], [], "mark", cost=cost)
        return cls.token


def call(kernel, ins, outs, scratch, name, aliases=None, spare=4 * 2**20, cost=EVENT_COST):
    buffers = []
    n_ins, n_outs, n_scratch = len(ins), len(outs), len(scratch)
    counts = []

    def run(*refs):
        given, made = list(refs[:n_ins]), list(refs[n_ins + 1 :][:n_outs])
        token_out, refs = refs[n_ins + 1 + n_outs], refs[n_ins + 2 + n_outs :]
        own, held, copies = refs[:n_scratch], list(refs[n_scratch:-1]), Copies(refs[-1])
        late = []
        for i, entry in enumerate(ins):
            if entry[0] is LATE:
                given[i] = Late(given[i])
                late.append(given[i])
        early = []
        for i, out in enumerate(outs):
            if out[0] is EARLY:
                made[i] = Early(made[i])
                early.append(made[i])
        leaving = kernel(*given, *made, *own, copies) or []
        token_out[...] = jnp.zeros_like(token_out)
        for value in late:
            value()
        for copy in leaving + [copy for out in early for copy in out.leaving]:
            copy.wait()
        counts.append(copies.count)

    def spec_of(spec):
        return VMEM if spec in (LATE, EARLY) else spec

    held = list(scratch) + [(a[1].shape, a[1].dtype) for a in ins if a[0] in (LATE, VMEM)]
    held += [out[1:] for out in outs if out[0] in (EARLY, VMEM)]
    needed = sum(math.prod(shape) * jnp.dtype(dtype).itemsize for shape, dtype in held)

    def build(sems):
        return pl.pallas_call(
            run,
            in_specs=[spec_of(entry[0]) for entry in ins] + [HBM],
            out_specs=tuple(spec_of(out[0]) for out in outs) + (VMEM,),
            out_shape=tuple(jax.ShapeDtypeStruct(*out[1:]) for out in outs)
            + (jax.ShapeDtypeStruct((8, 128), F32),),
            scratch_shapes=[pltpu.VMEM(*s) for s in scratch]
            + buffers
            + [pltpu.SemaphoreType.DMA((sems,))],
            compiler_params=pltpu.CompilerParams(vmem_limit_bytes=needed + spare),
            cost_estimate=pl.CostEstimate(flops=cost, bytes_accessed=1000, transcendentals=0),
            input_output_aliases=aliases or {},
            name=name,
        )

    arrays = [entry[1] for entry in ins] + [Order.token]
    jax.eval_shape(build(96), *arrays)
    *made, Order.token = build(max(counts[-1], 1))(*arrays)
    return made


def plain(*arrays):
    return [(HBM, array) for array in arrays]


def move(name, terms, unit, outs, targets, extra=None):
    jobs = [
        ([(array, indices[i]) for array, indices in terms], unit, target)
        for i, target in enumerate(targets)
    ]
    if extra is not None:
        jobs.append(extra)
    given = []
    for job_terms, _, _ in jobs:
        for array, _ in job_terms:
            if not any(array is other for other in given):
                given.append(array)

    def run(*refs):
        ins, made = refs[: len(given)], refs[len(given) : len(given) + len(outs)]

        def at(index):
            index = index(Spot()) if callable(index) else index
            return index if index else Ellipsis

        for job_terms, _, (number, target) in jobs:
            parts = [
                next(ref for ref, other in zip(ins, given) if other is array)[at(index)]
                for array, index in job_terms
            ]
            if len(parts) > 1:
                parts = [sum((part.astype(F32) for part in parts[1:]), parts[0].astype(F32))]
            made[number][at(target)] = parts[0].astype(BF16)

    return call(
        run,
        [(VMEM, array) for array in given],
        [(VMEM, shape, BF16) for shape in outs],
        [],
        name,
    )


def pack(name, entries):
    entries = [entry if isinstance(entry, tuple) else (entry, None, None) for entry in entries]
    unit = entries[0][0].shape[-2:]
    sizes = [
        count or (1 if len(array.shape) == 2 else array.shape[0]) for array, _, count in entries
    ]
    starts = [sum(sizes[:i]) for i in range(len(sizes))]

    def run(*refs):
        out = refs[len(entries)]
        for i, (ref, (_, start, count)) in enumerate(zip(refs, entries)):
            source = ref[...] if start is None else ref[pl.ds(start, count)]
            out[pl.ds(starts[i], sizes[i])] = source.reshape((sizes[i],) + unit)

    whole = ((sum(sizes),) + unit, entries[0][0].dtype)
    (packed,) = call(
        run, [(VMEM, entry[0]) for entry in entries], [(VMEM,) + whole], [], name
    )
    return packed


def choose(copies, first, second, buffer):
    is_first = lax.axis_index("section") % 2 == 0
    sem = copies.sems.at[copies.count]
    copies.count += 1
    pair = [pltpu.make_async_copy(source, buffer, sem) for source in (first, second)]
    pl.when(is_first)(pair[0].start)
    pl.when(jnp.logical_not(is_first))(pair[1].start)
    return pair[0]


def prepare_kernel(layers, by_permutes, boundary, w_in, w_out, given, *refs):
    outs, (slab, rows, pieces, copies) = refs[: -4], refs[-4:]
    count = slab.shape[0]
    first, second = (boundary.at[0, pl.ds(i * count, count)] for i in range(2))
    slab_copy = choose(copies, second, first, slab)
    leaving = []
    if by_permutes:
        other_rows, *out_pieces = outs
        spot = Spot()
        width = w_in.shape[2] // (2 * BLOCKS)
        arriving = []
        for block in range(BLOCKS):
            source = w_in.at[:, :, rows_at((2 * block + 1 - spot.core) * width, width)]
            arriving.append(copies.start(source, rows.at[:, :, pl.ds(block * width, width)]))
        high = w_out.shape[1] // BLOCKS
        for layer in range(layers):
            source = w_out.at[layer, rows_at(spot.section * high, high)]
            arriving.append(copies.start(source, pieces.at[layer]))
        for copy in arriving[:BLOCKS]:
            copy.wait()
        leaving.append(copies.start(rows, other_rows))
        for layer in range(layers):
            arriving[BLOCKS + layer].wait()
            leaving.append(copies.start(pieces.at[layer], out_pieces[layer]))
    slab_copy.wait()
    leaving.append(copies.start(slab, given))
    return leaving


class Gather:
    def __init__(self, place, name, w, other_rows, layer, by_rows):
        self.place, self.name, self.by_rows = place, name, by_rows
        self.w, self.other_rows, self.layer = w, other_rows, layer

    def join(self, halves, out_pieces=()):
        layer, rows, width = self.layer, self.w.shape[1], self.w.shape[2] // (2 * BLOCKS)
        beside = len(out_pieces) > 0
        shape = (1 + len(out_pieces), rows, 2 * width) if beside else (2 * rows, width)

        def run(w, other, *refs):
            out_refs, (out, copies) = refs[:-2], refs[-2:]
            spot = Spot()
            own = w.at[layer, :, rows_at((2 * spot.section + spot.core) * width, width)]
            other = other.at[layer, :, rows_at(spot.section * width, width)]
            arriving = []
            for source, core in ((own, spot.core), (other, 1 - spot.core)):
                target = out.at[rows_at(core * rows, rows)]
                if beside:
                    target = out.at[0, :, rows_at(core * width, width)]
                arriving.append(copies.start(source, target))
            for i, ref in enumerate(out_refs):
                arriving.append(copies.start(ref, out.at[1 + i]))
            for copy in arriving:
                copy.wait()

        (piece,) = call(
            run,
            plain(self.w, halves, *out_pieces),
            [(VMEM, shape, BF16)],
            [],
            "piece_" + self.name,
        )
        return piece

    def shift(self, piece):
        self.moved = [self.place.along_z(piece, flip) for flip in (1, 2, 3)]

    def one(self):
        self.along = pack("along_" + self.name, self.moved)
        self.from_one = self.place.plane_one(self.along)
        self.from_two = self.place.plane_two(self.along)

    def two(self, *others):
        self.far = self.place.plane_two(tie(self.from_one, *others))

    def sources(self):
        moved = [self.along, self.from_one, self.from_two, self.far]
        return [self.w] + moved if self.by_rows else [self.w, self.other_rows] + moved


def pairs(own, moved):
    n, rows, width = own.shape

    def run(own, moved, pair_in, *refs):
        for i, ref in enumerate((own, moved)):
            for core in range(2):
                half = pl.ds(core * (width // 2), width // 2)
                pair_in[i, pl.ds(core * rows, rows)] = ref[0, :, half]
            for j in range(n - 1):
                refs[j][i] = ref[1 + j]

    shapes = [(VMEM, (2, 2 * rows, width // 2), BF16)] + [(VMEM, (2, rows, width), BF16)] * (n - 1)
    return call(run, [(VMEM, own), (VMEM, moved)], shapes, [], "pairs")


def load_in(layer, sources, scratch, copies):
    if len(sources) == 1:
        width = scratch.shape[2]
        return [[copies.start(sources[0].at[:, pl.ds(i * width, width)], scratch.at[i])] for i in range(2)]
    own, other, along, one, two, far = sources
    spot = Spot()
    rows, width = own.shape[1], along.shape[2]
    pairs = []
    for pair in range(2):
        started = []
        for side in range(2):
            turn = 2 * pair + side
            columns = pl.ds(side * width, width)
            block = spot.block(turn)
            source = (one, far, two, along)[turn]
            for apart in range(1, spot.chips):
                chip = spot.chip ^ apart
                target = scratch.at[pair, rows_at(chip * 2 * rows, 2 * rows), columns]
                started.append(copies.start(source.at[apart - 1], target))
            for core, ref, index in (
                (spot.core, own, rows_at((2 * block + spot.core) * width, width)),
                (1 - spot.core, other, rows_at(block * width, width)),
            ):
                target = scratch.at[pair, rows_at((2 * spot.chip + core) * rows, rows), columns]
                started.append(copies.start(ref.at[layer, :, index], target))
        pairs.append(started)
    return pairs


def load_out(layer, sources, scratch, copies):
    if len(sources) == 1:
        return [copies.start(sources[0], scratch)]
    own, along, one, two, far = sources
    spot = Spot()
    shard, rows = own.shape[1], along.shape[1]
    started = []
    for apart in range(spot.chips):
        chip = spot.chip ^ apart
        start = spot.turn_of(chip) * shard
        if apart == 0:
            started.append(copies.start(own.at[layer], scratch.at[rows_at(start, shard), :]))
            continue
        for turn, source in enumerate((one, far, two, along)):
            part = pl.ds(pl.multiple_of(start + spot.block(turn) * rows, rows), rows)
            started.append(copies.start(source.at[apart - 1], scratch.at[part, :]))
    return started


class Scatter:
    def __init__(self, place, name, first, rest, by_rows):
        self.place, self.name, self.rest, self.by_rows = place, name, rest, by_rows
        self.chips, self.unit = rest.shape[1], rest.shape[2:]
        self.from_one = place.plane_one(first)
        self.small = None

    def move(self, stage, terms, sent):
        rows, width = self.unit
        extra, height = None, sent * rows
        if self.small is not None:
            self.small_rows = self.small[0][1].size
            terms_small = [(array, (at,)) for array, at in self.small]
            target = (0, (pl.ds(height, self.small_rows),))
            extra = (terms_small, (self.small_rows, width), target)
            height += self.small_rows
        targets = [(0, (pl.ds(i * rows, rows),)) for i in range(sent)]
        name = stage + "_" + self.name
        (made,) = move(name, terms, self.unit, [(height, width)], targets, extra)
        return made

    def heard(self, sent, received, count):
        if self.small is not None:
            at = pl.ds(count * self.unit[0], self.small_rows)
            self.small = [(sent, at), (received, at)]

    def part(self, i):
        return (pl.ds(i * self.unit[0], self.unit[0]),)

    def two(self):
        terms = [
            (self.rest, [(0, i) for i in range(self.chips)]),
            (self.from_one, [(1, i) for i in range(self.chips)]),
        ]
        second = self.move("two", terms, self.chips)
        self.from_two = self.place.plane_two(second)
        self.heard(second, self.from_two, self.chips)
        return second

    def own_terms(self, aparts):
        return [
            (self.rest, [(1, i) for i in aparts]),
            (self.from_one, [(0, i) for i in aparts]),
            (self.from_two, [self.part(i) for i in aparts]),
        ]

    def three(self):
        pair = self.move("three", self.own_terms([2, 3]), 2)
        self.from_pair = self.place.along_z(pair, 2)
        self.heard(pair, self.from_pair, 2)
        return pair

    def neighbour(self):
        terms = self.own_terms([1]) + [(self.from_pair, [self.part(1)])]
        piece = self.move("next", terms, 1)
        self.from_next = self.place.along_z(piece, 1)
        self.heard(piece, self.from_next, 1)
        return piece

    def four(self):
        if self.by_rows:
            terms = self.own_terms([0]) + [
                (self.from_pair, [self.part(0)]),
                (self.from_next, [self.part(0)]),
            ]
            (self.sum,) = move(
                "four_" + self.name, terms, self.unit, [self.unit], [(0, ())]
            )
            return self.sum
        rows, width = self.unit[0] // 2, self.unit[1]
        parts = [
            lambda spot: (rows_at(spot.core * rows, rows),),
            lambda spot: (rows_at((1 - spot.core) * rows, rows),),
        ]

        def of(head):
            return [lambda spot, part=part: head + part(spot) for part in parts]

        terms = [
            (self.rest, of((1, 0))),
            (self.from_one, of((0, 0))),
            (self.from_two, of(())),
            (self.from_pair, of(())),
            (self.from_next, of(())),
        ]
        targets, extra, height = [(0, ()), (1, (pl.ds(0, rows),))], None, rows
        if self.small is not None:
            height += self.small_rows
            terms_small = [(array, (at,)) for array, at in self.small]
            extra = (terms_small, (self.small_rows, width), (1, (pl.ds(rows, self.small_rows),)))
        self.kept, self.given = move(
            "four_" + self.name, terms, (rows, width), [(rows, width), (height, width)], targets, extra
        )
        self.from_core = self.place.swap_core(self.given)
        return self.kept


def join(name, scatters):
    given = []
    for scatter in scatters:
        given += [scatter.sum] if scatter.by_rows else [scatter.kept, scatter.from_core]
    rows, width = scatters[0].kept.shape
    half, width = width, 2 * width
    with_small = [scatter for scatter in scatters if scatter.small is not None]
    given += [scatter.given for scatter in with_small]
    small_rows = with_small[0].small_rows // 2 if with_small else 0
    count = len(scatters)

    def run(*refs):
        ins, out = list(refs[: len(given)]), refs[len(given)]
        spot = Spot()

        def small(ref, at):
            for i in range(2):
                part = ref[pl.ds(rows + i * small_rows, small_rows)]
                out[pl.ds(at, small_rows), pl.ds(i * half, half)] = part

        for i, scatter in enumerate(scatters):
            part = pl.ds(i * rows, rows)
            if scatter.by_rows:
                out[part] = ins.pop(0)[...]
                continue
            for turn, core in enumerate((spot.core, 1 - spot.core)):
                ref = ins.pop(0)
                out[part, rows_at(core * half, half)] = ref[pl.ds(0, rows)]
                if turn == 1 and scatter.small is not None:
                    small(ref, count * rows + small_rows)
        for ref in ins:
            small(ref, count * rows)

    whole = ((count * rows + 2 * small_rows, width), BF16)
    (joined,) = call(run, [(VMEM, array) for array in given], [(VMEM,) + whole], [], name)
    return joined


def collect_kernel(group, turns, n_started, *refs):
    arrays, refs = refs[: len(turns)], refs[len(turns) + n_started :]
    (*outs, held, high, copies) = refs
    spot = Spot()
    rows, width = held.shape[1:]
    parts = []
    for i, (layer, by_rows) in enumerate(group):
        part = pl.ds(i * rows, rows)
        for source, turn in zip(arrays, turns):
            quarter = spot.block(turn)
            if by_rows:
                target = outs[1].at[layer, rows_at(quarter * rows, rows), :]
            else:
                target = outs[0].at[layer, :, rows_at(quarter * width, width)]
            parts.append((copies.start(source.at[part], held.at[len(parts)]), target))
    leaving = []
    for i, (copy, target) in enumerate(parts):
        copy.wait()
        high[i] = held[i].astype(F32)
        leaving.append(copies.start(high.at[i], target))
    return leaving


def norm(values):
    center = jnp.mean(values, axis=-1, keepdims=True)
    offsets = values - center
    inverse = lax.rsqrt(jnp.mean(offsets * offsets, axis=-1, keepdims=True) + 1e-05)
    return offsets * inverse, inverse


def norm_back(upstream, unit, inverse, gain):
    scaled = upstream * gain
    center = jnp.mean(scaled, axis=-1, keepdims=True)
    along = jnp.mean(scaled * unit, axis=-1, keepdims=True)
    return inverse * (scaled - center - unit * along)


def gelu_both(v):
    scale = math.sqrt(2.0 / math.pi)
    square = v * v
    half = 0.5 + 0.5 * jnp.tanh(v * (scale + (scale * 0.044715) * square))
    spread = (2.0 * half) * (1.0 - half)
    return v * half, half + (v * spread) * (scale + (3.0 * scale * 0.044715) * square)


def mix_forward(rows, hid, seq, gain, shift, real, imag, outs):
    unit, inverse, normed_low = outs
    hid_cos, hid_sin = hid[0](), hid[1]()

    @row_steps(rows.shape[0])
    def _(at):
        real[at, :] = dot(rows[at, :], hid_cos[...]).astype(BF16)
        imag[at, :] = dot(rows[at, :], hid_sin[...]).astype(BF16)

    seq_cos, seq_sin = seq[0](), seq[1]()

    @row_steps(rows.shape[0])
    def _(at):
        mixed = dot(seq_cos[at, :], real[...]) - dot(seq_sin[at, :], imag[...])
        unit_rows, inverse_rows = norm(rows[at, :].astype(F32) + mixed)
        unit.buffer[at, :] = unit_rows
        inverse[at, :] = inverse_rows
        normed_low.buffer[at, :] = (unit_rows * gain[...] + shift[...]).astype(BF16)
        normed_low.push(at)
        unit.push(at)


def first_mix_kernel(numbers, boundary, received, hid_cos, hid_sin, cos_tiles, sin_tiles, gain, shift, *refs):
    seq_cos, seq_sin = refs[0:2]
    outs, (rows, real, imag, copies) = refs[2:5], refs[5:]
    chosen = choose(copies, boundary.at[0, pl.ds(0, rows.shape[0])], received, rows)
    cos_tiles, sin_tiles = cos_tiles(), sin_tiles()
    base = cos_tiles.shape[1]
    slots = seq_cos.buffer.shape[0] // base
    for i in range(slots):
        for j in range(slots):
            window = (pl.ds(i * base, base), pl.ds(j * base, base))
            number = numbers[i * slots + j]
            seq_cos.buffer[window] = cos_tiles[number]
            seq_sin.buffer[window] = sin_tiles[number]
    seq_cos.push()
    seq_sin.push()
    seq = (lambda: seq_cos.buffer, lambda: seq_sin.buffer)
    chosen.wait()
    mix_forward(rows, (hid_cos, hid_sin), seq, gain, shift, real, imag, outs)


def expand_kernel(layer, by_permutes, n_sources, normed, other_normed, b_in, *refs):
    sources, (hidden, slope, whole, copies) = refs[:n_sources], refs[n_sources:]
    scratch = whole.buffer
    loaded = load_in(layer, sources, scratch, copies)
    spot = Spot(by_permutes)
    width = scratch.shape[2]
    count = normed.buffer.shape[0]
    for pair in range(2):
        biases = [b_in[:, rows_at(spot.block(2 * pair + i) * (width // 2), width // 2)] for i in range(2)]
        bias = jnp.concatenate(biases, axis=1)
        for copy in loaded[pair]:
            copy.wait()
        whole.push(pair)
        for place, rows in enumerate((normed, other_normed)):
            rows = rows()

            @row_steps(count)
            def _(at):
                value, rate = gelu_both(dot(rows[at, :], scratch[pair]) + bias)
                to = pl.ds(place * count + at.start, at.size)
                hidden.buffer[pair, to, :] = value.astype(BF16)
                slope.buffer[pair, to, :] = rate.astype(BF16)

        hidden.push(pair)
        slope.push(pair)


def contract_kernel(layer, n_sources, hidden, *refs):
    sources, (own, other, whole, copies) = refs[:n_sources], refs[n_sources:]
    scratch = whole.buffer
    loaded = load_out(layer, sources, scratch, copies)
    count, width = own.buffer.shape[0], hidden.buffer.shape[2]
    for copy in loaded:
        copy.wait()
    whole.push()
    for place, out in ((1, other), (0, own)):

        @row_steps(count)
        def _(at):
            rows = pl.ds(place * count + at.start, at.size)
            hidden(1)
            held = hidden.buffer
            total = dot(held[0, rows, :], scratch[0:width, :]) + dot(held[1, rows, :], scratch[width:, :])
            out.buffer[at, :] = total.astype(out.buffer.dtype)
            out.push(at)


def second_norm(at, own, received, unit_one, gain_one, shift_one, b_out):
    normed = unit_one[at, :] * gain_one[...] + shift_one[...]
    return norm(normed + (own[at, :] + received[at, :].astype(F32) + b_out[...]))


def middle_kernel(own, received, unit_one, gain_one, shift_one, b_out, gain_two, shift_two, *refs):
    hid, seq, (next_gain, next_shift) = refs[:2], refs[2:4], refs[4:6]
    unit_two, inverse_two = refs[6:8]
    outs, (mid, real, imag, _) = refs[8:11], refs[11:]
    own, received, unit_one = own(), received(), unit_one()

    @row_steps(mid.shape[0])
    def _(at):
        unit, inverse = second_norm(at, own, received, unit_one, gain_one, shift_one, b_out)
        unit_two.buffer[at, :] = unit
        inverse_two[at, :] = inverse
        mid[at, :] = (unit * gain_two[...] + shift_two[...]).astype(BF16)

    unit_two.push()
    mix_forward(mid, hid, seq, next_gain, next_shift, real, imag, outs)


def second_back(at, upstream, unit, inverse, gain, d_second, branch_grad, small):
    grad = norm_back(upstream, unit, inverse, gain[...])
    low = grad.astype(BF16)
    branch_grad.buffer[at, :] = low
    branch_grad.push(at)
    d_second.buffer[at, :] = grad
    d_second.push(at)
    small[0:1, :] += column_sum(low.astype(F32))
    small[1:2, :] += column_sum(upstream * unit)
    small[2:3, :] += column_sum(upstream)


def turn_kernel(own, received, unit_one, gain_one, shift_one, b_out, gain_two, shift_two, *refs):
    boundary, given, out_rows, d_second, branch_grad, small, cotangent, copies = refs
    count = cotangent.shape[0]
    chosen = choose(copies, given, boundary.at[0, pl.ds(count, count)], cotangent)
    own, received, unit_one = own(), received(), unit_one()
    small[...] = jnp.zeros_like(small)
    chosen.wait()

    @row_steps(own.shape[0])
    def _(at):
        unit, inverse = second_norm(at, own, received, unit_one, gain_one, shift_one, b_out)
        out_rows.buffer[at, :] = (unit * gain_two[...] + shift_two[...]).astype(BF16)
        upstream = cotangent[at, :].astype(F32)
        second_back(at, upstream, unit, inverse, gain_two, d_second, branch_grad, small)
        out_rows.push(at)


def grad_out_kernel(by_permutes, hidden, branch_grad, other_grad, *refs):
    outs, (tiles, copies) = refs[:-2], refs[-2:]
    spot = Spot(by_permutes)
    count = branch_grad.shape[0]
    shard = tiles.shape[1]
    for turn in range(BLOCKS):
        columns = pl.ds((turn % 2) * shard, shard)
        grad = 0.0
        for i, ref in enumerate((branch_grad, other_grad)):
            rows = hidden[turn // 2, pl.ds(i * count, count), columns]
            grad = grad + dot(rows, ref[...], ((0,), (0,)))
        if not by_permutes:
            outs[0][pl.ds(turn * shard, shard), :] = grad.astype(BF16)
            continue
        tiles[turn] = grad.astype(BF16)
        rows = outs[0].shape[2]
        apart = spot.block(turn) ^ spot.chip
        for slot in range(BLOCKS):
            part = tiles[turn, rows_at(spot.block(slot) * rows, rows), :]
            outs[slot // 2][slot % 2, apart] = part


def shrink_kernel(by_permutes, n_outs, branch_grad, other_grad, slope, normed, other_normed, whole_out, whole_in, *refs):
    outs, (b_grad, own, other, tiles, act_grad, copies) = refs[:n_outs], refs[n_outs:]
    spot = Spot(by_permutes)
    count = branch_grad.shape[0]
    width = tiles.shape[2]
    half = width // 2
    b_grad[...] = jnp.zeros_like(b_grad)
    for pair in range(2):
        sums = []
        for place, ref in enumerate((branch_grad, other_grad)):

            @row_steps(count)
            def _(at):
                rows = pl.ds(place * count + at.start, at.size)
                grad = dot(ref[at, :], whole_out[pl.ds(pair * width, width), :], ((1,), (1,)))
                low = (grad * slope[pair, rows, :].astype(F32)).astype(BF16)
                act_grad[pair, rows, :] = low
                sums.append(column_sum(low.astype(F32)))

        total = sum(sums[1:], sums[0])
        for side in range(2):
            block = spot.block(2 * pair + side)
            b_grad[:, rows_at((2 * block + spot.core) * half, half)] = total[:, side * half : (side + 1) * half]

        @row_steps(tiles.shape[1])
        def _(at):
            grad = 0.0
            for place, ref in enumerate((normed, other_normed)):
                grads = act_grad[pair, pl.ds(place * count, count), :]
                grad = grad + dot(ref[:, at], grads, ((0,), (0,)))
            if by_permutes:
                tiles[pair, at, :] = grad.astype(BF16)
            else:
                outs[0][at, pl.ds(pair * width, width)] = grad.astype(BF16)

        if by_permutes:
            rows = outs[0].shape[2]
            for side in range(2):
                for chip in range(spot.chips):
                    part = tiles[pair, pl.ds(chip * rows, rows), pl.ds(side * half, half)]
                    outs[pair][side, chip ^ spot.chip] = part
    for place, out in ((1, other), (0, own)):

        @row_steps(count)
        def _(at):
            rows = pl.ds(place * count + at.start, at.size)
            total = dot(act_grad[0, rows, :], whole_in[0], ((1,), (1,)))
            total = total + dot(act_grad[1, rows, :], whole_in[1], ((1,), (1,)))
            out[at, :] = total.astype(out.dtype)


def unmix(refs, total, mix_grad, real, imag, small, input_grad):
    own, received, d_second, unit_one, inverse_one, gain_one, hid_cos, hid_sin, seq_cos, seq_sin = refs
    own, received, d_second, unit_one = own(), received(), d_second(), unit_one()
    small[...] = jnp.zeros_like(small)

    @row_steps(total.shape[0])
    def _(at):
        upstream = d_second[at, :] + own[at, :] + received[at, :].astype(F32)
        unit = unit_one[at, :]
        grad = norm_back(upstream, unit, inverse_one[at, :], gain_one[...])
        total[at, :] = grad
        mix_grad[at, :] = grad.astype(BF16)
        small[0:1, :] += column_sum(upstream * unit)
        small[1:2, :] += column_sum(upstream)

    seq_cos, seq_sin = seq_cos(), seq_sin()

    @row_steps(total.shape[0])
    def _(at):
        real[at, :] = dot(seq_cos[at, :], mix_grad[...]).astype(BF16)
        imag[at, :] = (-dot(seq_sin[at, :], mix_grad[...])).astype(BF16)

    hid_cos, hid_sin = hid_cos(), hid_sin()

    @row_steps(total.shape[0])
    def _(at):
        grad = dot(real[at, :], hid_cos[...]) + dot(imag[at, :], hid_sin[...])
        input_grad(at, total[at, :] + grad)


def last_kernel(*refs):
    ins, (out_rows, *smalls) = refs[:10], refs[10:17]
    sent, kept, packed, total, mix_grad, real, imag, small, _ = refs[17:]
    is_first = lax.axis_index("section") % 2 == 0
    rows = out_rows()

    def input_grad(at, values):
        low = values.astype(BF16)
        sent.buffer[at, :] = jnp.where(is_first, rows[at, :], low)
        kept.buffer[at, :] = jnp.where(is_first, low, rows[at, :])
        sent.push(at)
        kept.push(at)

    unmix(ins, total, mix_grad, real, imag, small, input_grad)
    width = packed.shape[1]
    packed[...] = jnp.zeros_like(packed)
    for layer in range(2):
        b_grad, sums_two = smalls[3 * layer : 3 * layer + 2]
        sums_one = smalls[3 * layer + 2] if layer else small
        at = layer * (packed.shape[0] // 2)
        sums = (sums_two[0:1], sums_one[0:1], sums_one[1:2], sums_two[1:2], sums_two[2:3])
        for vector in (b_grad[...],) + sums:
            for i in range(vector.shape[1] // width):
                packed[at : at + 1, :] = vector[:, i * width : (i + 1) * width].astype(packed.dtype)
                at += 1


def finish_kernel(kept, back, result, held, high, copies):
    layer = lax.axis_index("section") % 2
    count = held.shape[1]
    arriving = [copies.start(ref, held.at[i]) for i, ref in enumerate((kept, back))]
    leaving = []
    for i, block in enumerate((layer, 1 - layer)):
        arriving[i].wait()
        high[i] = held[i].astype(F32)
        leaving.append(copies.start(high.at[i], result.at[0, rows_at(block * count, count)]))
    return leaving


def relay_kernel(*refs):
    ins, (unit_two, inverse_two, gain_two) = refs[:10], refs[10:13]
    small, d_second, branch_grad, small_two, total, mix_grad, real, imag, _ = refs[13:]
    small_two[...] = jnp.zeros_like(small_two)

    def input_grad(at, values):
        upstream = values.astype(BF16).astype(F32)
        unit = unit_two()[at, :]
        second_back(at, upstream, unit, inverse_two[at, :], gain_two, d_second, branch_grad, small_two)

    unmix(ins, total, mix_grad, real, imag, small, input_grad)


def body(boundary, bucket_ids, w_in, b_in, w_out, b_out, gain_one, shift_one, gain_two, shift_two):
    place = Place()
    Order.begin()
    layers = w_in.shape[0]
    micro_count = bucket_ids.shape[1]
    feat_width = boundary.shape[2]
    ff_width = w_in.shape[2]
    slab_len = boundary.shape[1] // micro_count
    slots = bucket_ids.shape[2]
    base_len = slab_len // slots
    half_block = ff_width // (2 * BLOCKS)
    by_permutes = place.n_section == 4 and place.chips == 4
    last = layers - 1

    bucket_row = bucket_ids[place.section // 2, place.section % 2]
    half_bias = lax.dynamic_index_in_dim(
        b_in.reshape(layers, BLOCKS, 2, half_block), place.core, 2, keepdims=False
    ).reshape(layers, -1)

    block = (slab_len, feat_width)
    both = (2 * slab_len, feat_width)
    wide_block = (2, 2 * slab_len, ff_width // 4)
    whole_in_shape = (2, feat_width, ff_width // 4)
    whole_out_shape = (ff_width // 2, feat_width)
    column = (VMEM, (slab_len, 1), F32)
    sums_shape = (VMEM, (8, feat_width), F32)
    mix_outs = [(EARLY, block, F32), column, (EARLY, block, BF16)]
    hid = [(LATE, jnp.asarray(table.astype(BF16))) for table in dft_tables(feat_width)]

    def late(*arrays):
        return [(LATE, array) for array in arrays]

    def param(array, layer):
        return (VMEM, array[layer][None])

    shard_rows, piece_rows = w_in.shape[1], w_out.shape[1] // BLOCKS
    prepared = [(HBM, block, BF16)]
    if by_permutes:
        prepared += [(HBM, (layers, shard_rows, ff_width // 2), BF16)]
        prepared += [(HBM, (piece_rows, feat_width), BF16)] * layers
    given, *prepared = call(
        partial(prepare_kernel, layers, by_permutes),
        plain(boundary, w_in, w_out),
        prepared,
        [
            (block, BF16),
            ((layers, shard_rows, ff_width // 2), BF16),
            ((layers, piece_rows, feat_width), BF16),
        ],
        "prepare",
        spare=54 * 2**20,
    )
    sources_in, sources_out = [None] * layers, [None] * layers
    if by_permutes:
        for_other, out_zero_piece, out_one_piece = prepared
        in_zero, out_zero, in_one, out_one = (
            Gather(place, name + str(layer), w, None, layer, by_rows)
            for layer in range(layers)
            for name, w, by_rows in (("in", w_in, False), ("out", w_out, True))
        )
        other_rows = place.swap_core(for_other)
        received = place.swap_layer(given)
        in_zero.other_rows = in_one.other_rows = other_rows
        in_zero.shift(in_zero.join(other_rows))
        own_pieces = in_one.join(other_rows, (out_zero_piece, out_one_piece))
        moved_pieces = place.along_z(own_pieces, 1)
        Order.wait(received)
        in_zero.one()
        pair_in, pair_zero, pair_one = pairs(own_pieces, moved_pieces)
        out_zero.moved = [(pair_zero, 1, 1), place.along_z(pair_zero, 2)]
    else:
        received = place.swap_layer(given)
        for layer in range(layers):
            whole_in, whole_out = (
                lax.all_gather(w[layer], "dp", axis=0, tiled=True) for w in (w_in, w_out)
            )
            whole_in = whole_in.reshape(feat_width, BLOCKS, 2, half_block)
            whole_out = whole_out.reshape(BLOCKS, 2, half_block, feat_width)
            whole_in = lax.dynamic_index_in_dim(whole_in, place.core, 2, keepdims=False)
            whole_out = lax.dynamic_index_in_dim(whole_out, place.core, 1, keepdims=False)
            sources_in[layer] = [whole_in.reshape(feat_width, -1)]
            sources_out[layer] = [whole_out.reshape(-1, feat_width)]

    numbers = tile_numbers(bucket_row, slots).reshape(-1)
    tiles = [(LATE, jnp.asarray(table)) for table in sequence_tiles(base_len)]
    seq_cos, seq_sin, *mixed = call(
        first_mix_kernel,
        [(SMEM, numbers)]
        + plain(boundary, received)
        + hid
        + tiles
        + [param(gain_one, 0), param(shift_one, 0)],
        [(EARLY, (slab_len, slab_len), BF16)] * 2 + mix_outs,
        [(block, BF16)] * 3,
        "first_mix",
    )
    tables = hid + late(seq_cos, seq_sin)

    both_pairs, all_rows = pl.ds(0, 2), pl.ds(0, 2 * slab_len)
    steps = slab_len // ROW_STEP
    row_parts = [
        (both_pairs, pl.ds(slab_len * place_ + i * ROW_STEP, ROW_STEP))
        for place_ in (1, 0)
        for i in range(steps)
    ]
    block_parts = [
        (pair, all_rows, pl.ds(side * half_block, half_block)) for pair in range(2) for side in range(2)
    ]
    pair_parts = [(pl.ds(pair, 1),) for pair in range(2)]
    half_parts = [(pl.ds(pair * 2 * half_block, 2 * half_block),) for pair in range(2)]

    saved, wholes_in, wholes_out = [], [], []
    for layer in range(layers):
        unit_one, inverse_one, normed = mixed
        if by_permutes and layer == 0:
            mark = Order.mark(in_zero.from_one, in_zero.from_two)
            in_zero.two(mark)
            other_normed = place.swap_core(tie(normed, mark))
            out_zero.one()
            in_one.moved = [(pair_in, 1, 1), place.along_z(tie(pair_in, out_zero.along), 2)]
            sources_in[0] = in_zero.sources()
        else:
            other_normed = place.swap_core(normed)
        if by_permutes and layer == 1:
            Order.mark(in_one.far, cost=FAR_MARK_COST)
            mark = Order.mark(out_one.from_one, out_one.from_two, cost=NEAR_MARK_COST)
            out_one.two(mark)
            sources_in[1] = in_one.sources()
        hidden, slope, whole_in = call(
            partial(expand_kernel, layer, by_permutes, len(sources_in[layer])),
            late(normed, other_normed)
            + [(VMEM, half_bias[layer][None])]
            + plain(*sources_in[layer]),
            [(EARLY, wide_block, BF16), (EARLY, wide_block, BF16), (EARLY, whole_in_shape, BF16)],
            [],
            "expand",
        )
        if by_permutes and layer == 0:
            mark = Order.mark(out_zero.from_one, out_zero.from_two)
            out_zero.two(mark)
            in_one.one()
            out_one.moved = [(pair_one, 1, 1), place.along_z(tie(pair_one, mark), 2)]
            sources_out[0] = out_zero.sources()
        if by_permutes and layer == 1:
            sources_out[1] = out_one.sources()
        own_part, other_part, whole_out = call(
            partial(contract_kernel, layer, len(sources_out[layer])),
            [(LATE, hidden, row_parts)] + plain(*sources_out[layer]),
            [(EARLY, block, F32), (EARLY, block, BF16), (EARLY, whole_out_shape, BF16)],
            [],
            "contract",
        )
        from_other = place.swap_core(other_part)
        if by_permutes and layer == 0:
            mark = Order.mark(in_one.from_one, in_one.from_two)
            in_one.two(mark)
            out_one.one()
        wholes_in.append(whole_in)
        wholes_out.append(whole_out)
        common = late(own_part, from_other, unit_one) + [
            param(p, layer) for p in (gain_one, shift_one, b_out, gain_two, shift_two)
        ]
        kept = [unit_one, inverse_one, normed, other_normed, hidden, slope]
        if layer < last:
            unit_two, inverse_two, *mixed = call(
                middle_kernel,
                common + tables + [param(gain_one, layer + 1), param(shift_one, layer + 1)],
                [(EARLY, block, F32), column] + mix_outs,
                [(block, BF16), (block, BF16), (block, BF16)],
                "middle",
                cost=MIDDLE_COST,
            )
            kept += [unit_two, inverse_two]
        saved.append(kept)

    out_rows, d_second, branch_grad, sums_two = call(
        turn_kernel,
        common + plain(boundary, received),
        [(EARLY, block, BF16), (EARLY, block, F32), (EARLY, block, BF16), sums_shape],
        [(block, BF16)],
        "turn",
    )

    if by_permutes:
        piece_out = (2, place.chips, w_out.shape[1] // BLOCKS, feat_width)
        piece_in = (2, place.chips, 2 * w_in.shape[1], half_block)
        grad_outs = {True: [(VMEM, piece_out, BF16)] * 2, False: [(VMEM, piece_in, BF16)] * 2}
    else:
        grad_outs = {
            True: [(VMEM, (ff_width // 2, feat_width), BF16)],
            False: [(VMEM, (feat_width, ff_width // 2), BF16)],
        }
    n_outs = len(grad_outs[True])
    grads, smalls, running = {}, {}, []

    def reduce_grad(pieces, layer, by_rows):
        name = ("out" if by_rows else "in") + str(layer)
        if by_permutes:
            grads[layer, by_rows] = Scatter(place, name, *pieces, by_rows)
            running.append(grads[layer, by_rows])
            return
        (half,) = pieces
        if by_rows:
            whole = jnp.zeros((BLOCKS, 2, half_block, feat_width), BF16)
            half = half.reshape(BLOCKS, 1, half_block, feat_width)
            whole = lax.dynamic_update_slice_in_dim(whole, half, place.core, 1)
            whole = whole.reshape(ff_width, feat_width)
        else:
            whole = jnp.zeros((feat_width, BLOCKS, 2, half_block), BF16)
            half = half.reshape(feat_width, BLOCKS, 1, half_block)
            whole = lax.dynamic_update_slice_in_dim(whole, half, place.core, 2)
            whole = whole.reshape(feat_width, ff_width)
        part = lax.psum_scatter(whole, "dp", scatter_dimension=0, tiled=True)
        grads[layer, by_rows] = lax.psum(part, "section").astype(F32)

    for layer in reversed(range(layers)):
        unit_one, inverse_one, normed, other_normed, hidden, slope = saved[layer][:6]
        other_grad = place.swap_core(branch_grad)
        if by_permutes and layer == 0:
            running[0].two()
            running[1].two()
        pieces = call(
            partial(grad_out_kernel, by_permutes),
            [(VMEM, hidden), (VMEM, branch_grad), (VMEM, other_grad)],
            grad_outs[True],
            [((BLOCKS, half_block, feat_width), BF16)],
            "grad_out",
        )
        reduce_grad(pieces, layer, True)
        if by_permutes and layer == 0:
            running[0].three()
            Order.mark(running[1].from_two)
        *pieces, b_grad, own_part, other_part = call(
            partial(shrink_kernel, by_permutes, n_outs),
            [
                (VMEM, array)
                for array in (branch_grad, other_grad, slope, normed, other_normed)
                + (wholes_out[layer], wholes_in[layer])
            ],
            grad_outs[False]
            + [(VMEM, (1, ff_width), F32), (VMEM, block, F32), (VMEM, block, BF16)],
            [((2, feat_width, ff_width // 4), BF16), (wide_block, BF16)],
            "shrink",
        )
        from_other = place.swap_core(other_part)
        reduce_grad(pieces, layer, False)
        if by_permutes and layer == last:
            Order.mark(running[0].from_one)
        if by_permutes and layer == 0:
            running[0].neighbour()
            running[2].two()
            running[1].three()
        ins = (
            late(own_part, from_other, d_second, unit_one)
            + [(VMEM, inverse_one), param(gain_one, layer)]
            + tables
        )
        work = [(block, F32), (block, BF16), (block, BF16), (block, BF16)]
        smalls[layer] = [b_grad, sums_two]
        if layer > 0:
            below_unit, below_inverse = saved[layer - 1][6:8]
            sums_one, d_second, branch_grad, sums_two = call(
                relay_kernel,
                ins + late(below_unit) + [(VMEM, below_inverse), param(gain_two, layer - 1)],
                [sums_shape, (EARLY, block, F32), (EARLY, block, BF16), sums_shape],
                work,
                "relay",
            )
            smalls[layer].append(sums_one)
    vectors = smalls[0] + [smalls[1][2]] + smalls[1]
    small_type = BF16 if by_permutes else F32
    sent, kept_rows, packed = call(
        last_kernel,
        ins + late(out_rows) + [(VMEM, vector) for vector in vectors],
        [(EARLY, block, BF16), (EARLY, block, BF16), (VMEM, (64, half_block), small_type)],
        work + [((8, feat_width), F32)],
        "last",
    )

    def finish():
        return call(
            finish_kernel,
            plain(kept_rows, back),
            [(HBM, (1, 2 * slab_len, feat_width), F32)],
            [((2,) + block, BF16), ((2,) + block, F32)],
            "finish",
        )

    if by_permutes:

        def share(mine):
            return [place.plane_one(mine), place.plane_two(mine)]

        out_last, in_last, out_first, in_first = running
        in_first.small = [(packed, pl.ds(0, packed.shape[0]))]
        out_first.three()
        in_first.two()
        out_last.four()
        in_last.neighbour()
        in_first.three()
        back = place.swap_layer(tie(sent, Order.token))
        in_last.four()
        out_first.neighbour()
        in_first.neighbour()
        (result,) = finish()
        mine = join("join_rest", [in_last, out_last])
        rest = share(mine)
        out_first.four()
        in_first.four()
        rest.append(place.plane_two(tie(rest[0], Order.token)))
        Order.wait(rest[1])
        last_mine = join("join_last", [in_first, out_first])
        last_rest = share(last_mine)
        groups = [[(last, False), (last, True)], [(0, False), (0, True)]]
        unit = (shard_rows, ff_width // BLOCKS)

        def collect(group, quarters, started):
            turns, arrays = zip(*quarters)
            held = ((len(turns) * len(group),) + unit,)
            n = len(turns)
            return call(
                partial(collect_kernel, group, turns, len(started)),
                plain(*arrays, *started),
                [(HBM, w_in.shape, F32), (HBM, w_out.shape, F32)],
                [held + (BF16,), held + (F32,)],
                "collect",
                aliases={n: 0, n + 1: 1} if started else None,
            )

        Order.mark(rest[2])
        mark = Order.mark(*last_rest)
        far = place.plane_two(tie(last_rest[0], mark))
        started = collect(groups[0], zip((3, 0, 2, 1), [mine] + rest), ())
        started = collect(groups[1], zip((3, 0, 2), [last_mine] + last_rest), tuple(started))
        at, size = 2 * shard_rows, (last_mine.shape[0] - 2 * shard_rows) // 2
        packed = sum(
            array[at + i * size : at + (i + 1) * size].astype(F32)
            for i, arrays in enumerate(((last_mine, last_rest[0]), (last_mine, last_rest[1])))
            for array in arrays
        )
        packed = packed.reshape(-1, 2, half_block).transpose(1, 0, 2).reshape(-1, half_block)
        packed = tie(packed, Order.token)
        Order.wait(packed)
        grad_in, grad_out = collect(groups[1], [(1, far)], tuple(started))
    else:
        back = place.swap_layer(sent)
        grad_in, grad_out = (
            jnp.stack([grads[layer, by_rows] for layer in range(layers)])
            for by_rows in (False, True)
        )
        packed = lax.psum(packed, AXES)
        (result,) = finish()
    b_part, part = ff_width // place.n_dp, feat_width // place.n_dp
    flat = packed.reshape(layers, -1)
    small_out = [lax.dynamic_slice_in_dim(flat, place.dp * b_part, b_part, 1)]
    sums = flat[:, ff_width : ff_width + 5 * feat_width].reshape(layers, 5, feat_width)
    sums = lax.dynamic_slice_in_dim(sums, place.dp * part, part, 2)
    small_out += [sums[:, i] for i in range(5)]
    return (result, grad_in, small_out[0], grad_out, *small_out[1:])


def solution(mesh):
    return jax.shard_map(
        body,
        mesh=mesh,
        in_specs=(
            P("section", "dp", None),
            P(None, "dp", None),
            P(None, "dp", None),
            P(),
            P(None, "dp", None),
            P(),
            P(),
            P(),
            P(),
            P(),
        ),
        out_specs=(
            P("section", "dp", None),
            P(None, "dp", None),
            P(None, "dp"),
            P(None, "dp", None),
            P(None, "dp"),
            P(None, "dp"),
            P(None, "dp"),
            P(None, "dp"),
            P(None, "dp"),
        ),
        check_vma=False,
    )
```
